128 devices in a mesh: dp: 2 (over core), ctx: 16 (over y, z), tp: 4 (over x).
Axes of the slice: x: 4, y: 4, z: 4, core: 2. Of those that a mesh axis runs over, the one named last changes fastest.
Arguments:
- queries: bfloat16 [2, 32768, 1024], P('dp', 'ctx', 'tp'), may hold values from -16 to 16
- key_vectors: bfloat16 [2, 32768, 1024], P('dp', 'ctx', 'tp'), may hold values from -16 to 16
- value_vectors: bfloat16 [2, 32768, 1024], P('dp', 'ctx', 'tp'), may hold values from -6 to 6
- grad_output: bfloat16 [2, 32768, 1024], P('dp', 'ctx', 'tp'), may hold values from -6 to 6
- out_weight: bfloat16 [1024, 1024], P('tp'), may hold values from -0.1875 to 0.1875
- random_ids: int32 [2, 512, 3], P('dp'), may hold values from 0 to 511, as said below
- random_valid: int32 [2, 512, 3], P('dp'), may hold values 0 or 1
- global_ids: int32 [2, 2], P('dp'), may hold values from 0 to 511, as said below
Outputs:
- projected: bfloat16 [2, 32768, 1024], P('dp', 'ctx', 'tp')
- grad_queries: bfloat16 [2, 32768, 1024], P('dp', 'ctx', 'tp')
- grad_keys: bfloat16 [2, 32768, 1024], P('dp', 'ctx', 'tp')
- grad_values: bfloat16 [2, 32768, 1024], P('dp', 'ctx', 'tp')
- grad_weight: float32 [1024, 1024], P('tp')
The draws below stay inside these ranges and needn't reach their ends.
Inputs may be any that keep to these rules, and one draw needn't show every extreme that they name: `random_ids`: entries name blocks of the same document. For each document and each ctx index i (query blocks 32 * i to 32 * i + 31), the random entries of those rows name blocks of exactly 12 ctx indices, 8 entries for each of them, padding entries included. `global_ids`: the 2 numbers of a document differ; one of them is the document's last block, 511.
All inputs are finite; a program needn't handle non-finite values. No bound on the sum of `random_valid` on one device may be relied on, other than what follows from the above.
Results may differ from the reference program's by a relative error of at most 0.02.
Values may be sent and summed in bfloat16 or wider, within the bound.
No kernel may reach another device: no remote copies, remote signals or barrier semaphores. Data moves between devices by JAX's collectives and lax.ppermute only.
A program may use at most 192 MiB of HBM per device.

```python
import math
import jax
import jax.numpy as jnp
from jax import lax

H = 16
HD = 64
BLK = 64
R = 3
G = 2
D = 1024
NB = 32
NBLK = 512
TOKENS = 32768
DOCS = 2
USED = 12


def drawn_vectors(key, salt):
    shape = (DOCS, TOKENS, D)
    base_draw = jnp.clip(jax.random.normal(jax.random.fold_in(key, salt), shape, jnp.float32), -6.0, 6.0)
    return base_draw.astype(jnp.bfloat16)


def draw_queries(key, part):
    return drawn_vectors(key, 11)


def draw_key_vectors(key, part):
    return drawn_vectors(key, 12)


def draw_random_ids(key, part):
    ctx_total = NBLK // NB
    device_keys = jax.random.split(jax.random.fold_in(key, 31), DOCS * ctx_total)

    def one_device(dev_key):
        owners = jax.random.permutation(jax.random.fold_in(dev_key, 1), ctx_total)[:USED].astype(jnp.int32)
        entries = jnp.arange(NB * R, dtype=jnp.int32)
        owner_of = owners[entries % USED]
        shuffled = jax.random.permutation(jax.random.fold_in(dev_key, 2), owner_of).astype(jnp.int32)
        local_blocks = jax.random.randint(jax.random.fold_in(dev_key, 3), (NB * R,), 0, NB, dtype=jnp.int32)
        return (shuffled * NB + local_blocks).reshape(NB, R)
    drawn = jax.vmap(one_device)(device_keys)
    return drawn.reshape(DOCS, NBLK, R).astype(jnp.int32)


def draw_global_ids(key, part):
    doc_keys = jax.random.split(jax.random.fold_in(key, 41), DOCS)

    def one_doc(doc_key):
        others = jax.random.permutation(jax.random.fold_in(doc_key, 1), NBLK - 1)[:G - 1].astype(jnp.int32)
        listed = jnp.concatenate([jnp.full((1,), NBLK - 1, jnp.int32), others])
        order = jax.random.permutation(jax.random.fold_in(doc_key, 2), G).astype(jnp.int32)
        return listed[order].astype(jnp.int32)
    return jax.vmap(one_doc)(doc_keys).astype(jnp.int32)


def set_ends(values, key, smallest, largest):
    shape = values.shape
    index_at = [jax.random.randint(jax.random.fold_in(key, axis), (), 0, shape[axis]) for axis in range(len(shape))]
    values = values.at[tuple(index_at)].set(smallest)
    longest = shape.index(max(shape))
    index_at[longest] = (index_at[longest] + 1) % shape[longest]
    return values.at[tuple(index_at)].set(largest)


def block_scale(stream_key, shape, shards, least, high):
    gain, own = 1.0, jax.random.fold_in(stream_key, 6)
    for dim, blocks in shards:
        steps = jnp.exp(jax.random.uniform(jax.random.fold_in(own, dim), (blocks,), jnp.float32, least / len(shards), high / len(shards)))
        gain = gain * jnp.repeat(steps, shape[dim] // blocks).reshape([-1 if axis == dim else 1 for axis in range(len(shape))])
    return gain


def normal_values(stream_key, dims, spread, reach, shards=(), kind=jnp.bfloat16):
    values = jax.random.normal(stream_key, dims, jnp.float32) * spread
    if len(shards) > 0:
        values = block_scale(stream_key, dims, shards, -0.22, 0.18) * values
    return jnp.clip(values, min=-reach, max=reach).astype(kind)


def setup_inputs(seed: int = 0) -> dict:
    arg_keys = jax.random.split(jax.random.key(seed), 9)
    queries = draw_queries(jax.random.fold_in(arg_keys[8], 71), 0)
    key_vectors = draw_key_vectors(jax.random.fold_in(arg_keys[8], 71), 0)
    value_vectors = normal_values(arg_keys[2], (DOCS, TOKENS, D), 1.0, 6.0, ((0, 2), (1, 16), (2, 4)))
    grad_output = normal_values(arg_keys[3], (DOCS, TOKENS, D), 1.0, 6.0, ((0, 2), (1, 16), (2, 4)))
    out_weight = normal_values(arg_keys[4], (D, D), D ** -0.5, 0.1875, ((0, 4),))
    random_ids = draw_random_ids(jax.random.fold_in(arg_keys[8], 71), 0)
    random_valid = set_ends((jax.random.randint(arg_keys[6], (DOCS, NBLK, R), 0, 4) < 3).astype(jnp.int32), jax.random.fold_in(arg_keys[6], 1), 0, 1)
    global_ids = draw_global_ids(jax.random.fold_in(arg_keys[8], 71), 0)
    return dict(queries=queries, key_vectors=key_vectors, value_vectors=value_vectors, grad_output=grad_output, out_weight=out_weight, random_ids=random_ids, random_valid=random_valid, global_ids=global_ids)


NEG_FILL = -1e+30

def attend_block(query_now, key_set, value_set, present, grad_now):
    scaling = 1.0 / math.sqrt(HD)
    query_f32 = query_now.astype(jnp.float32)
    key_f32 = key_set.astype(jnp.float32)
    value_f32 = value_set.astype(jnp.float32)
    grad_f32 = grad_now.astype(jnp.float32)
    scores = jnp.einsum('gqhd,gkhd->ghqk', query_f32, key_f32) * scaling
    keep_mask = present[:, None, None, :]
    scores = jnp.where(keep_mask, scores, NEG_FILL)
    row_peak = lax.optimization_barrier(jnp.max(scores, axis=-1, keepdims=True))
    exp_terms = jnp.where(keep_mask, jnp.exp(scores - row_peak), 0.0)
    prob_full = exp_terms / lax.optimization_barrier(jnp.sum(exp_terms, axis=-1, keepdims=True))
    prob_low = prob_full.astype(jnp.bfloat16)
    prob_back = prob_low.astype(jnp.float32)
    context = jnp.einsum('ghqk,gkhd->gqhd', prob_back, value_f32).astype(jnp.bfloat16)
    grad_prob = jnp.einsum('gqhd,gkhd->ghqk', grad_f32, value_f32)
    row_delta = lax.optimization_barrier(jnp.sum(prob_full * grad_prob, axis=-1, keepdims=True))
    grad_score = (prob_full * (grad_prob - row_delta) * scaling).astype(jnp.bfloat16)
    score_f32 = grad_score.astype(jnp.float32)
    grad_query = jnp.einsum('ghqk,gkhd->gqhd', score_f32, key_f32).astype(jnp.bfloat16)
    grad_key = jnp.einsum('ghqk,gqhd->gkhd', score_f32, query_f32)
    grad_value = jnp.einsum('ghqk,gqhd->gkhd', prob_back, grad_f32)
    return (context, grad_query, grad_key, grad_value)

def doc_pass(queries, key_vectors, value_vectors, grad_output, out_weight, random_ids, random_valid, global_ids):
    grad_context = jnp.dot(grad_output, out_weight.T, preferred_element_type=jnp.float32).astype(jnp.bfloat16)
    blocks = jnp.arange(NBLK, dtype=jnp.int32)
    window_ids = jnp.stack([blocks - 1, blocks, blocks + 1], axis=1)
    window_ok = jnp.stack([blocks > 0, blocks >= 0, blocks < NBLK - 1], axis=1)
    global_cols = jnp.broadcast_to(global_ids.astype(jnp.int32)[None, :], (NBLK, G))
    entry_ids = jnp.concatenate([window_ids, random_ids.astype(jnp.int32), global_cols], axis=1)
    entry_ok = jnp.concatenate([window_ok, random_valid == 1, jnp.ones((NBLK, G), dtype=bool)], axis=1)
    safe_ids = jnp.clip(entry_ids, 0, NBLK - 1).astype(jnp.int32)
    key_blocks = key_vectors.reshape(NBLK, BLK, D)
    value_blocks = value_vectors.reshape(NBLK, BLK, D)
    query_blocks = queries.reshape(NBLK, BLK, H, HD)
    grad_blocks = grad_context.reshape(NBLK, BLK, H, HD)
    entry_count = 3 + R + G
    group_size = math.gcd(NBLK, 16)

    def advance(carry, group_index):
        acc_key, acc_value = carry
        row_start = (group_index * group_size).astype(jnp.int32)
        ids_now = lax.dynamic_slice_in_dim(safe_ids, row_start, group_size, 0)
        ok_now = lax.dynamic_slice_in_dim(entry_ok, row_start, group_size, 0)
        query_now = lax.dynamic_slice_in_dim(query_blocks, row_start, group_size, 0)
        grad_now = lax.dynamic_slice_in_dim(grad_blocks, row_start, group_size, 0)
        key_set = key_blocks[ids_now].reshape(group_size, entry_count * BLK, H, HD)
        value_set = value_blocks[ids_now].reshape(group_size, entry_count * BLK, H, HD)
        present = jnp.repeat(ok_now, BLK, axis=1)
        context, grad_query, grad_key, grad_value = attend_block(query_now, key_set, value_set, present, grad_now)
        both = jnp.stack([grad_key, grad_value]).reshape(2, group_size, entry_count, BLK, D)
        rounded = lax.optimization_barrier(both[:, :, 3:3 + R].astype(jnp.bfloat16)).astype(jnp.float32)
        both = jnp.concatenate([both[:, :, :3], rounded, both[:, :, 3 + R:]], axis=2)
        flat_ids = ids_now.reshape(-1)
        acc_key = acc_key.at[flat_ids].add(both[0].reshape(group_size * entry_count, BLK, D))
        acc_value = acc_value.at[flat_ids].add(both[1].reshape(group_size * entry_count, BLK, D))
        return ((acc_key, acc_value), (context, grad_query))
    zero_acc = jnp.zeros((NBLK, BLK, D), jnp.float32)
    group_list = jnp.arange(NBLK // group_size, dtype=jnp.int32)
    (acc_key, acc_value), (contexts, grad_queries) = lax.scan(advance, (zero_acc, zero_acc), group_list)
    context = contexts.reshape(TOKENS, D)
    projected = jnp.dot(context, out_weight, preferred_element_type=jnp.float32).astype(jnp.bfloat16)
    weight_term = jnp.dot(context.T, grad_output, preferred_element_type=jnp.float32)
    return (projected, grad_queries.reshape(TOKENS, D), acc_key.reshape(TOKENS, D).astype(jnp.bfloat16), acc_value.reshape(TOKENS, D).astype(jnp.bfloat16), weight_term)

def reference(queries, key_vectors, value_vectors, grad_output, out_weight, random_ids, random_valid, global_ids):
    outputs = []
    for doc_index in range(DOCS):
        outputs.append(doc_pass(queries[doc_index], key_vectors[doc_index], value_vectors[doc_index], grad_output[doc_index], out_weight, random_ids[doc_index], random_valid[doc_index], global_ids[doc_index]))
    projected = jnp.stack([item[0] for item in outputs])
    grad_queries = jnp.stack([item[1] for item in outputs])
    grad_keys = jnp.stack([item[2] for item in outputs])
    grad_values = jnp.stack([item[3] for item in outputs])
    grad_weight = outputs[0][4]
    for item in outputs[1:]:
        grad_weight = grad_weight + item[4]
    return (projected, grad_queries, grad_keys, grad_values, grad_weight)
```

```python
import functools

import jax
import jax.numpy as jnp
from jax import lax
from jax.experimental import pallas as pl
from jax.experimental.pallas import tpu as pltpu
from jax.sharding import PartitionSpec as P

HD = 64
BLK = 64
R = 3
G = 2
LANES = 128
NEG_FILL = -1e30
VMEM_LIMIT = 56 * 1024 * 1024

NT = (((1,), (1,)), ((), ()))
NN = (((1,), (0,)), ((), ()))
TN = (((0,), (0,)), ((), ()))


def dot(a, b, dims):
    return lax.dot_general(a, b, dims, preferred_element_type=jnp.float32)


def smem():
    return pl.BlockSpec(memory_space=pltpu.SMEM)


def whole(shape, column=None):
    if column is None:
        return pl.BlockSpec(shape, lambda i: (0,) * len(shape))
    return pl.BlockSpec(shape, lambda i: (0,) * (len(shape) - 1) + (column,))


def params(**more):
    return pltpu.CompilerParams(vmem_limit_bytes=VMEM_LIMIT, **more)


def pick_kernel(slots, idx_ref, k_ref, v_ref, out_ref):
    def body(s, _):
        src = pl.multiple_of(idx_ref[s] * BLK, BLK)
        dst = pl.multiple_of(s * 2 * BLK, 2 * BLK)
        out_ref[pl.ds(dst, BLK), :] = k_ref[pl.ds(src, BLK), :]
        out_ref[pl.ds(dst + BLK, BLK), :] = v_ref[pl.ds(src, BLK), :]
        return 0

    lax.fori_loop(0, slots, body, 0, unroll=4)


def pick_blocks(idx, keys, values, column, slots):
    rows = keys.shape[0]
    return pl.pallas_call(
        functools.partial(pick_kernel, slots),
        grid=(1,),
        in_specs=[smem(), whole((rows, LANES), column), whole((rows, LANES), column)],
        out_specs=whole((slots * 2 * BLK, LANES)),
        out_shape=jax.ShapeDtypeStruct((slots * 2 * BLK, LANES), jnp.bfloat16),
        compiler_params=params(),
        cost_estimate=pl.CostEstimate(flops=0, bytes_accessed=10 << 20, transcendentals=0),
    )(idx, keys, values)


def grad_context_kernel(g0, g1, g2, g3, w_ref, out_ref):
    width = g0.shape[1]
    total = None
    for i, g in enumerate((g0, g1, g2, g3)):
        term = dot(g[...], w_ref[:, i * width : (i + 1) * width], NT)
        total = term if total is None else total + term
    out_ref[...] = total.astype(jnp.bfloat16)


def grad_context_of(pieces, weight):
    rows, width = pieces[0].shape
    heads = weight.shape[0]
    tile = 512
    return pl.pallas_call(
        grad_context_kernel,
        grid=(rows // tile,),
        in_specs=[pl.BlockSpec((tile, width), lambda i: (i, 0))] * 4
        + [pl.BlockSpec(weight.shape, lambda i: (0, 0))],
        out_specs=pl.BlockSpec((tile, heads), lambda i: (i, 0)),
        out_shape=jax.ShapeDtypeStruct((rows, heads), jnp.bfloat16),
        compiler_params=params(),
        cost_estimate=pl.CostEstimate(flops=2 * rows * 1024 * heads, bytes_accessed=6 << 20, transcendentals=0),
    )(*pieces, weight)


def attend_kernel(
    blocks, slot_ref, bias_ref, q_ref, k_ref, v_ref, g_ref, edge_ref, glob_ref, fetched_ref, dq_in_ref,
    ctx_ref, dq_ref, ret_ref, win_ref, gsum_ref, kpad, vpad,
):
    del dq_in_ref
    rows = blocks * BLK
    kpad[0:BLK, :] = edge_ref[0]
    vpad[0:BLK, :] = edge_ref[1]
    kpad[rows + BLK : rows + 2 * BLK, :] = edge_ref[2]
    vpad[rows + BLK : rows + 2 * BLK, :] = edge_ref[3]
    kpad[BLK : rows + BLK, :] = k_ref[...]
    vpad[BLK : rows + BLK, :] = v_ref[...]
    win_ref[...] = jnp.zeros_like(win_ref)
    gsum_ref[...] = jnp.zeros_like(gsum_ref)
    low = lax.broadcasted_iota(jnp.int32, (BLK, LANES), 1) < HD

    def body(i, _):
        row = pl.multiple_of(i * BLK, BLK)
        q = q_ref[pl.ds(row, BLK), :] * jnp.bfloat16(0.125)
        g = g_ref[pl.ds(row, BLK), :]
        zero = jnp.zeros_like(q)
        qbd = jnp.concatenate([jnp.where(low, q, zero), jnp.where(low, zero, q)], axis=0)
        gbd = jnp.concatenate([jnp.where(low, g, zero), jnp.where(low, zero, g)], axis=0)
        starts = [pl.multiple_of(slot_ref[i * R + r] * 2 * BLK, 2 * BLK) for r in range(R)]
        kcat = jnp.concatenate(
            [kpad[pl.ds(row, 3 * BLK), :]]
            + [fetched_ref[pl.ds(s, BLK), :] for s in starts]
            + [glob_ref[0, 0], glob_ref[1, 0]],
            axis=0,
        )
        vcat = jnp.concatenate(
            [vpad[pl.ds(row, 3 * BLK), :]]
            + [fetched_ref[pl.ds(s + BLK, BLK), :] for s in starts]
            + [glob_ref[0, 1], glob_ref[1, 1]],
            axis=0,
        )
        scores = dot(kcat, qbd, NT)
        scores = jnp.concatenate(
            [
                scores[e * BLK : (e + 1) * BLK] + (bias_ref[i * 8 + e] if e in (0, 2, 3, 4, 5) else 0.0)
                for e in range(8)
            ],
            axis=0,
        )
        peak = jnp.max(scores, axis=0, keepdims=True)
        terms = jnp.exp(scores - peak)
        probs = terms * (1.0 / jnp.sum(terms, axis=0, keepdims=True))
        probs_low = probs.astype(jnp.bfloat16)
        grad_probs = dot(vcat, gbd, NT)
        delta = jnp.sum(probs * grad_probs, axis=0, keepdims=True)
        grad_scores = (probs * (grad_probs - delta)).astype(jnp.bfloat16)
        context = dot(probs_low, vcat, TN)
        grad_q = dot(grad_scores, kcat, TN)
        grad_k = dot(grad_scores, qbd, NN)
        grad_v = dot(probs_low, gbd, NN)
        ctx_ref[pl.ds(row, BLK), :] = jnp.where(low, context[:BLK], context[BLK:]).astype(jnp.bfloat16)
        dq_ref[pl.ds(row, BLK), :] = (
            jnp.where(low, grad_q[:BLK], grad_q[BLK:]) * 0.125
        ).astype(jnp.bfloat16)
        win_ref[0, pl.ds(row, 3 * BLK), :] += grad_k[: 3 * BLK]
        win_ref[1, pl.ds(row, 3 * BLK), :] += grad_v[: 3 * BLK]
        for r, s in enumerate(starts):
            part = slice((3 + r) * BLK, (4 + r) * BLK)
            ret_ref[pl.ds(s, BLK), :] = grad_k[part].astype(jnp.bfloat16)
            ret_ref[pl.ds(s + BLK, BLK), :] = grad_v[part].astype(jnp.bfloat16)
        for e in range(G):
            part = slice((3 + R + e) * BLK, (4 + R + e) * BLK)
            gsum_ref[e, 0] += grad_k[part]
            gsum_ref[e, 1] += grad_v[part]
        return 0

    lax.fori_loop(0, blocks, body, 0, unroll=2)


def attend(slot, bias, q, k, v, g, edges, glob, fetched, dq_in, column):
    rows, width = q.shape
    blocks = rows // BLK
    half = whole((rows, LANES), column)
    out_shape = (
        jax.ShapeDtypeStruct((rows, LANES), jnp.bfloat16),
        jax.ShapeDtypeStruct((rows, width), jnp.bfloat16),
        jax.ShapeDtypeStruct(fetched.shape, jnp.bfloat16),
        jax.ShapeDtypeStruct((2, rows + 2 * BLK, LANES), jnp.float32),
        jax.ShapeDtypeStruct((G, 2, BLK, LANES), jnp.float32),
    )
    first = dq_in is None
    if first:
        dq_in = jnp.zeros((8, 128), jnp.bfloat16)
    return pl.pallas_call(
        functools.partial(attend_kernel, blocks),
        grid=(1,),
        in_specs=[
            smem(), smem(), half, half, half, half,
            whole((4, BLK, LANES), column),
            whole((G, 2, BLK, LANES), column),
            whole(fetched.shape),
            pl.BlockSpec(memory_space=pl.ANY),
        ],
        out_specs=(
            whole((rows, LANES)), half, whole(fetched.shape),
            whole(out_shape[3].shape), whole(out_shape[4].shape),
        ),
        out_shape=out_shape,
        scratch_shapes=[
            pltpu.VMEM((rows + 2 * BLK, LANES), jnp.bfloat16),
            pltpu.VMEM((rows + 2 * BLK, LANES), jnp.bfloat16),
        ],
        input_output_aliases={} if first else {9: 1},
        compiler_params=params(),
        cost_estimate=pl.CostEstimate(
            flops=12 * blocks * 512 * 128 * 128 * 2, bytes_accessed=16 << 20, transcendentals=blocks * 512 * 128
        ),
    )(slot, bias, q, k, v, g, edges, glob, fetched, dq_in)


def collect_kernel(
    requesters, capacity, blocks, idx_ref, used_ref, glob_ref, win_ref, back_ref, edge_ref, gsum_ref,
    dk_in_ref, dv_in_ref, dk_ref, dv_ref, acc,
):
    del dk_in_ref, dv_in_ref
    rows = blocks * BLK
    acc[...] = win_ref[:, BLK : rows + BLK, :]
    acc[:, rows - BLK : rows, :] += edge_ref[0].astype(jnp.float32)
    acc[:, 0:BLK, :] += edge_ref[1].astype(jnp.float32)
    for e in range(G):

        @pl.when(glob_ref[G + e] == 1)
        def _():
            at = pl.multiple_of(glob_ref[e] * BLK, BLK)
            acc[:, pl.ds(at, BLK), :] += gsum_ref[e].astype(jnp.float32)

    def body(a, _):
        @pl.when(used_ref[a] > 0)
        def _():
            for c in range(capacity):
                s = a * capacity + c
                at = pl.multiple_of(idx_ref[s] * BLK, BLK)
                src = pl.multiple_of(s * 2 * BLK, 2 * BLK)
                acc[0, pl.ds(at, BLK), :] += back_ref[pl.ds(src, BLK), :].astype(jnp.float32)
                acc[1, pl.ds(at, BLK), :] += back_ref[pl.ds(src + BLK, BLK), :].astype(jnp.float32)

        return 0

    lax.fori_loop(0, requesters, body, 0)
    dk_ref[...] = acc[0].astype(jnp.bfloat16)
    dv_ref[...] = acc[1].astype(jnp.bfloat16)


def collect(idx, used, glob, win, back, edges, gsum, before, width, column, requesters, capacity):
    rows = win.shape[1] - 2 * BLK
    first = before is None
    if first:
        before = (jnp.zeros((8, 128), jnp.bfloat16),) * 2
    half = whole((rows, LANES), column)
    out = jax.ShapeDtypeStruct((rows, width), jnp.bfloat16)
    return pl.pallas_call(
        functools.partial(collect_kernel, requesters, capacity, rows // BLK),
        grid=(1,),
        in_specs=[
            smem(), smem(), smem(), whole(win.shape), whole(back.shape), whole(edges.shape),
            whole(gsum.shape), pl.BlockSpec(memory_space=pl.ANY), pl.BlockSpec(memory_space=pl.ANY),
        ],
        out_specs=(half, half),
        out_shape=(out, out),
        scratch_shapes=[pltpu.VMEM((2, rows, LANES), jnp.float32)],
        input_output_aliases={} if first else {7: 0, 8: 1},
        compiler_params=params(),
        cost_estimate=pl.CostEstimate(flops=4 << 20, bytes_accessed=8 << 20, transcendentals=0),
    )(idx, used, glob, win, back, edges, gsum, *before)


def weight_kernel(c0, c1, g0, g1, g2, g3, out_ref, acc):
    @pl.when(pl.program_id(0) == 0)
    def _():
        acc[...] = jnp.zeros_like(acc)

    width = g0.shape[1]
    for r, c in enumerate((c0, c1)):
        for i, g in enumerate((g0, g1, g2, g3)):
            acc[r * LANES : (r + 1) * LANES, i * width : (i + 1) * width] += dot(c[...], g[...], TN)

    @pl.when(pl.program_id(0) == pl.num_programs(0) - 1)
    def _():
        out_ref[...] = acc[...].astype(jnp.bfloat16)


def weight_terms(contexts, pieces):
    rows, width = pieces[0].shape
    tile = 512
    shape = (2 * LANES, 4 * width)
    return pl.pallas_call(
        weight_kernel,
        grid=(rows // tile,),
        in_specs=[pl.BlockSpec((tile, LANES), lambda i: (i, 0))] * 2
        + [pl.BlockSpec((tile, width), lambda i: (i, 0))] * 4,
        out_specs=pl.BlockSpec(shape, lambda i: (0, 0)),
        out_shape=jax.ShapeDtypeStruct(shape, jnp.bfloat16),
        scratch_shapes=[pltpu.VMEM(shape, jnp.float32)],
        compiler_params=params(),
        cost_estimate=pl.CostEstimate(flops=2 * rows * 1024 * 256, bytes_accessed=6 << 20, transcendentals=0),
    )(*contexts, *pieces)


def project_kernel(*refs):
    contexts, w_ref, out_ref = refs[:8], refs[8], refs[9]
    total = None
    for i, c in enumerate(contexts):
        term = dot(c[...], w_ref[i * LANES : (i + 1) * LANES, :], NN)
        total = term if total is None else total + term
    out_ref[...] = total.astype(jnp.bfloat16)


def project(contexts, weight):
    rows = contexts[0].shape[0]
    width = weight.shape[1]
    tile = 512
    return pl.pallas_call(
        project_kernel,
        grid=(rows // tile,),
        in_specs=[pl.BlockSpec((tile, LANES), lambda i: (i, 0))] * 8
        + [pl.BlockSpec(weight.shape, lambda i: (0, 0))],
        out_specs=pl.BlockSpec((tile, width), lambda i: (i, 0)),
        out_shape=jax.ShapeDtypeStruct((rows, width), jnp.bfloat16),
        compiler_params=params(),
        cost_estimate=pl.CostEstimate(flops=2 * rows * 1024 * width, bytes_accessed=6 << 20, transcendentals=0),
    )(*contexts, weight)


def from_others(array, axis):
    size = lax.axis_size(axis)
    found = [array]
    for by in range(1, size):
        found.append(lax.ppermute(array, axis, [((i + by) % size, i) for i in range(size)]))
    return found


def passed_along(array, axis, by):
    size = lax.axis_size(axis)
    pairs = [(i, i + by) for i in range(size) if 0 <= i + by < size]
    return lax.ppermute(array, axis, pairs)


def per_device(
    queries, key_vectors, value_vectors, grad_output, out_weight, random_ids, random_valid, global_ids
):
    ctx_count = lax.axis_size("ctx")
    tp_count = lax.axis_size("tp")
    me = lax.axis_index("ctx")
    tp_me = lax.axis_index("tp")
    q, k, v, g_out = queries[0], key_vectors[0], value_vectors[0], grad_output[0]
    rows, width = q.shape
    blocks = rows // BLK
    requests = blocks * R
    capacity = requests // (ctx_count * 3 // 4)
    slots = ctx_count * capacity

    ids = random_ids[0].reshape(ctx_count, requests)
    owner = ids // blocks
    local = ids % blocks
    order = jnp.arange(requests, dtype=jnp.int32)
    earlier = order[None, :] < order[:, None]
    mine = owner == me
    rank = jnp.sum((mine[:, None, :] & earlier[None]).astype(jnp.int32), axis=2)
    hit = mine[:, None, :] & (rank[:, None, :] == jnp.arange(capacity, dtype=jnp.int32)[None, :, None])
    send_idx = jnp.sum(jnp.where(hit, local[:, None, :], 0), axis=2).reshape(slots)
    used = jnp.sum(mine.astype(jnp.int32), axis=1)
    my_owner = lax.dynamic_index_in_dim(owner, me, 0, keepdims=False)
    my_rank = jnp.sum(((my_owner[:, None] == my_owner[None, :]) & earlier).astype(jnp.int32), axis=1)
    my_slot = my_owner * capacity + my_rank

    def exchange(array):
        parts = array.reshape(ctx_count, capacity * 2 * BLK, LANES)
        return lax.all_to_all(parts, "ctx", split_axis=0, concat_axis=0, tiled=True).reshape(array.shape)

    send_a = pick_blocks(send_idx, k, v, 0, slots)
    fetched_a = exchange(send_a)
    send_b = pick_blocks(send_idx, k, v, 1, slots)

    glob_owner = global_ids[0] // blocks
    glob_local = global_ids[0] % blocks
    owned = glob_owner == me
    picked = jnp.stack(
        [
            jnp.stack([lax.dynamic_slice_in_dim(x, glob_local[e] * BLK, BLK, 0) for x in (k, v)])
            * owned[e].astype(jnp.bfloat16)
            for e in range(G)
        ]
    ).reshape(ctx_count, -1, width)
    picked = lax.all_to_all(picked, "ctx", split_axis=0, concat_axis=0, tiled=True)
    picked = jnp.sum(picked.astype(jnp.float32), axis=0).astype(jnp.bfloat16)
    glob = lax.all_gather(picked, "ctx", axis=0, tiled=True).reshape(G, 2, BLK, width)

    last = jnp.stack([k[rows - BLK :], v[rows - BLK :]])
    initial = jnp.stack([k[:BLK], v[:BLK]])
    edges = jnp.concatenate([passed_along(last, "ctx", 1), passed_along(initial, "ctx", -1)])

    pieces = from_others(g_out, "tp")
    turned = jnp.roll(out_weight, -tp_me * width, axis=1)
    grad_context = grad_context_of(pieces, turned)
    wparts = out_weight.reshape(width, tp_count, width).transpose(1, 0, 2)
    wcols = lax.all_to_all(wparts, "tp", split_axis=0, concat_axis=0, tiled=True).reshape(tp_count * width, width)
    wcols = jnp.roll(wcols, -tp_me * width, axis=0)

    block_no = me * blocks + jnp.arange(blocks, dtype=jnp.int32)
    valid = lax.dynamic_slice_in_dim(random_valid[0], me * blocks, blocks, 0)
    present = jnp.concatenate(
        [
            (block_no > 0)[:, None],
            jnp.ones((blocks, 1), bool),
            (block_no < blocks * ctx_count - 1)[:, None],
            valid == 1,
            jnp.ones((blocks, G), bool),
        ],
        axis=1,
    )
    bias = jnp.where(present, 0.0, NEG_FILL).astype(jnp.float32).reshape(-1)

    send_b, fetched_a = lax.optimization_barrier((send_b, fetched_a))
    fetched_b = exchange(send_b)
    ctx_a, dq_a, ret_a, win_a, gsum_a = attend(
        my_slot, bias, q, k, v, grad_context, edges, glob, fetched_a, None, 0
    )
    ret_a, fetched_b = lax.optimization_barrier((ret_a, fetched_b))
    back_a = exchange(ret_a)
    ctx_pieces_a = from_others(ctx_a, "tp")
    ctx_b, grad_q, ret_b, win_b, gsum_b = attend(
        my_slot, bias, q, k, v, grad_context, edges, glob, fetched_b, dq_a, 1
    )
    ret_b, back_a = lax.optimization_barrier((ret_b, back_a))
    back_b = exchange(ret_b)
    ctx_pieces_b = from_others(ctx_b, "tp")

    terms = weight_terms((ctx_a, ctx_b), pieces)
    gsum = jnp.concatenate([gsum_a, gsum_b], axis=-1).astype(jnp.bfloat16)
    share = jnp.concatenate(
        [terms.reshape(ctx_count, -1, 4 * width), gsum.reshape(ctx_count, -1, 4 * width)], axis=1
    )
    share = lax.all_to_all(share, "ctx", split_axis=0, concat_axis=0, tiled=True)
    share = jnp.sum(share.astype(jnp.float32), axis=0)
    wrows = 2 * LANES // ctx_count
    other = lax.ppermute(share[:wrows], "dp", [(0, 1), (1, 0)])
    share = jnp.concatenate([share[:wrows] + other, share[wrows:]]).astype(jnp.bfloat16)
    share = lax.all_gather(share, "ctx", axis=0)
    grad_weight = share[:, :wrows].reshape(2 * LANES, 4 * width).astype(jnp.float32)
    grad_weight = jnp.roll(grad_weight, tp_me * width, axis=1)
    gsum = share[:, wrows:].reshape(G, 2, BLK, width)

    def outer(win):
        first = passed_along(win[:, :BLK].astype(jnp.bfloat16), "ctx", -1)
        final = passed_along(win[:, rows + BLK :].astype(jnp.bfloat16), "ctx", 1)
        return jnp.stack([first, final])

    glob_at = jnp.concatenate([glob_local, owned.astype(jnp.int32)])
    half = functools.partial(collect, send_idx, used, glob_at)
    grads = half(win_a, back_a, outer(win_a), gsum[..., :LANES], None, width, 0, ctx_count, capacity)
    grads = half(win_b, back_b, outer(win_b), gsum[..., LANES:], grads, width, 1, ctx_count, capacity)
    ordered = [c for pair in zip(ctx_pieces_a, ctx_pieces_b) for c in pair]
    projected = project(ordered, wcols)
    return projected[None], grad_q[None], grads[0][None], grads[1][None], grad_weight


def solution(mesh):
    tokens = P("dp", "ctx", "tp")
    in_specs = (
        tokens, tokens, tokens, tokens, P("tp", None), P("dp", None, None), P("dp", None, None), P("dp", None),
    )
    out_specs = (tokens, tokens, tokens, tokens, P("tp", None))
    return jax.shard_map(per_device, mesh=mesh, in_specs=in_specs, out_specs=out_specs, check_vma=False)
```

```python
import functools

import jax
import jax.numpy as jnp
from jax import lax
from jax.experimental import pallas as pl
from jax.experimental.pallas import tpu as pltpu
from jax.sharding import PartitionSpec as P

HD = 64
BLK = 64
R = 3
G = 2
LANES = 128
NEG_FILL = -1e30
VMEM_LIMIT = 56 * 1024 * 1024

NT = (((1,), (1,)), ((), ()))
NN = (((1,), (0,)), ((), ()))
TN = (((0,), (0,)), ((), ()))


def dot(a, b, dims):
    return lax.dot_general(a, b, dims, preferred_element_type=jnp.float32)


def smem():
    return pl.BlockSpec(memory_space=pltpu.SMEM)


def whole(shape, column=None):
    if column is None:
        return pl.BlockSpec(shape, lambda i: (0,) * len(shape))
    return pl.BlockSpec(shape, lambda i: (0,) * (len(shape) - 1) + (column,))


def params(**more):
    return pltpu.CompilerParams(vmem_limit_bytes=VMEM_LIMIT, **more)


def pick_kernel(slots, idx_ref, k_ref, v_ref, out_ref):
    def body(s, _):
        src = pl.multiple_of(idx_ref[s] * BLK, BLK)
        dst = pl.multiple_of(s * 2 * BLK, 2 * BLK)
        out_ref[pl.ds(dst, BLK), :] = k_ref[pl.ds(src, BLK), :]
        out_ref[pl.ds(dst + BLK, BLK), :] = v_ref[pl.ds(src, BLK), :]
        return 0

    lax.fori_loop(0, slots, body, 0, unroll=4)


def pick_blocks(idx, keys, values, column, slots):
    rows = keys.shape[0]
    return pl.pallas_call(
        functools.partial(pick_kernel, slots),
        grid=(1,),
        in_specs=[smem(), whole((rows, LANES), column), whole((rows, LANES), column)],
        out_specs=whole((slots * 2 * BLK, LANES)),
        out_shape=jax.ShapeDtypeStruct((slots * 2 * BLK, LANES), jnp.bfloat16),
        compiler_params=params(),
        cost_estimate=pl.CostEstimate(flops=0, bytes_accessed=10 << 20, transcendentals=0),
    )(idx, keys, values)


def grad_context_kernel(at_ref, *refs):
    del at_ref
    total = None
    for g, w in zip(refs[:4], refs[4:8]):
        term = dot(g[...], w[...], NT)
        total = term if total is None else total + term
    refs[8][...] = total.astype(jnp.bfloat16)


def grad_context_of(at, pieces, weight):
    rows, width = pieces[0].shape
    heads = weight.shape[0]
    tile = 512
    turned = [
        pl.BlockSpec((heads, width), functools.partial(lambda j, i, at: (0, (at[0] + j) % 4), j))
        for j in range(4)
    ]
    return pl.pallas_call(
        grad_context_kernel,
        grid_spec=pltpu.PrefetchScalarGridSpec(
            num_scalar_prefetch=1,
            grid=(rows // tile,),
            in_specs=[pl.BlockSpec((tile, width), lambda i, at: (i, 0))] * 4 + turned,
            out_specs=pl.BlockSpec((tile, heads), lambda i, at: (i, 0)),
        ),
        out_shape=jax.ShapeDtypeStruct((rows, heads), jnp.bfloat16),
        compiler_params=params(),
        cost_estimate=pl.CostEstimate(flops=2 * rows * 1024 * heads, bytes_accessed=6 << 20, transcendentals=0),
    )(at, *pieces, weight, weight, weight, weight)


def attend_kernel(
    blocks, last_block, me_ref, slot_ref, valid_ref, q_ref, k_ref, v_ref, g_ref, before_ref, after_ref, glob_ref,
    fetched_ref, dq_in_ref, ctx_ref, dq_ref, ret_ref, win_out_ref, outer_ref, gsum_out_ref,
    kpad, vpad, win_ref, gsum_ref,
):
    del dq_in_ref
    rows = blocks * BLK
    kpad[0:BLK, :] = before_ref[0]
    vpad[0:BLK, :] = before_ref[1]
    kpad[rows + BLK : rows + 2 * BLK, :] = after_ref[0]
    vpad[rows + BLK : rows + 2 * BLK, :] = after_ref[1]
    kpad[BLK : rows + BLK, :] = k_ref[...]
    vpad[BLK : rows + BLK, :] = v_ref[...]
    win_ref[...] = jnp.zeros_like(win_ref)
    gsum_ref[...] = jnp.zeros_like(gsum_ref)
    low = lax.broadcasted_iota(jnp.int32, (BLK, LANES), 1) < HD

    def body(i, _):
        row = pl.multiple_of(i * BLK, BLK)
        q = q_ref[pl.ds(row, BLK), :] * jnp.bfloat16(0.125)
        g = g_ref[pl.ds(row, BLK), :]
        zero = jnp.zeros_like(q)
        qbd = jnp.concatenate([jnp.where(low, q, zero), jnp.where(low, zero, q)], axis=0)
        gbd = jnp.concatenate([jnp.where(low, g, zero), jnp.where(low, zero, g)], axis=0)
        starts = [pl.multiple_of(slot_ref[i * R + r] * 2 * BLK, 2 * BLK) for r in range(R)]
        kcat = jnp.concatenate(
            [kpad[pl.ds(row, 3 * BLK), :]]
            + [fetched_ref[pl.ds(s, BLK), :] for s in starts]
            + [glob_ref[0, 0], glob_ref[1, 0]],
            axis=0,
        )
        vcat = jnp.concatenate(
            [vpad[pl.ds(row, 3 * BLK), :]]
            + [fetched_ref[pl.ds(s + BLK, BLK), :] for s in starts]
            + [glob_ref[0, 1], glob_ref[1, 1]],
            axis=0,
        )
        scores = dot(kcat, qbd, NT)
        block = me_ref[0] * blocks + i
        present = [block > 0, None, block < last_block]
        present += [valid_ref[i * R + r] == 1 for r in range(R)] + [None] * G
        parts = []
        for e, there in enumerate(present):
            part = scores[e * BLK : (e + 1) * BLK]
            parts.append(part if there is None else part + jnp.where(there, 0.0, NEG_FILL))
        scores = jnp.concatenate(parts, axis=0)
        peak = jnp.max(scores, axis=0, keepdims=True)
        terms = jnp.exp(scores - peak)
        probs = terms * (1.0 / jnp.sum(terms, axis=0, keepdims=True))
        probs_low = probs.astype(jnp.bfloat16)
        grad_probs = dot(vcat, gbd, NT)
        delta = jnp.sum(probs * grad_probs, axis=0, keepdims=True)
        grad_scores = (probs * (grad_probs - delta)).astype(jnp.bfloat16)
        context = dot(probs_low, vcat, TN)
        grad_q = dot(grad_scores, kcat, TN)
        grad_k = dot(grad_scores, qbd, NN)
        grad_v = dot(probs_low, gbd, NN)
        ctx_ref[pl.ds(row, BLK), :] = jnp.where(low, context[:BLK], context[BLK:]).astype(jnp.bfloat16)
        dq_ref[pl.ds(row, BLK), :] = (
            jnp.where(low, grad_q[:BLK], grad_q[BLK:]) * 0.125
        ).astype(jnp.bfloat16)
        win_ref[0, pl.ds(row, 3 * BLK), :] += grad_k[: 3 * BLK]
        win_ref[1, pl.ds(row, 3 * BLK), :] += grad_v[: 3 * BLK]
        for r, s in enumerate(starts):
            part = slice((3 + r) * BLK, (4 + r) * BLK)
            ret_ref[pl.ds(s, BLK), :] = grad_k[part].astype(jnp.bfloat16)
            ret_ref[pl.ds(s + BLK, BLK), :] = grad_v[part].astype(jnp.bfloat16)
        for e in range(G):
            part = slice((3 + R + e) * BLK, (4 + R + e) * BLK)
            gsum_ref[e, 0] += grad_k[part]
            gsum_ref[e, 1] += grad_v[part]
        return 0

    lax.fori_loop(0, blocks, body, 0, unroll=2)
    win_out_ref[...] = win_ref[:, BLK : rows + BLK, :]
    outer_ref[0] = win_ref[:, 0:BLK, :].astype(jnp.bfloat16)
    outer_ref[1] = win_ref[:, rows + BLK : rows + 2 * BLK, :].astype(jnp.bfloat16)
    gsum_out_ref[...] = gsum_ref[...].reshape(G * 2 * BLK, LANES).astype(jnp.bfloat16)


def attend(last_block, me, slot, valid, q, k, v, g, before, after, glob, fetched, dq_in, column):
    rows, width = q.shape
    blocks = rows // BLK
    half = whole((rows, LANES), column)
    out_shape = (
        jax.ShapeDtypeStruct((rows, LANES), jnp.bfloat16),
        jax.ShapeDtypeStruct((rows, width), jnp.bfloat16),
        jax.ShapeDtypeStruct(fetched.shape, jnp.bfloat16),
        jax.ShapeDtypeStruct((2, rows, LANES), jnp.float32),
        jax.ShapeDtypeStruct((2, 2, BLK, LANES), jnp.bfloat16),
        jax.ShapeDtypeStruct((G * 2 * BLK, LANES), jnp.bfloat16),
    )
    first = dq_in is None
    if first:
        dq_in = jnp.zeros((8, 128), jnp.bfloat16)
    return pl.pallas_call(
        functools.partial(attend_kernel, blocks, last_block),
        grid=(1,),
        in_specs=[
            smem(), smem(), smem(), half, half, half, half,
            whole((2, BLK, LANES), column),
            whole((2, BLK, LANES), column),
            whole((G, 2, BLK, LANES), column),
            whole(fetched.shape),
            pl.BlockSpec(memory_space=pl.ANY),
        ],
        out_specs=(
            whole((rows, LANES)), half, whole(fetched.shape),
            whole(out_shape[3].shape), whole(out_shape[4].shape), whole(out_shape[5].shape),
        ),
        out_shape=out_shape,
        scratch_shapes=[
            pltpu.VMEM((rows + 2 * BLK, LANES), jnp.bfloat16),
            pltpu.VMEM((rows + 2 * BLK, LANES), jnp.bfloat16),
            pltpu.VMEM((2, rows + 2 * BLK, LANES), jnp.float32),
            pltpu.VMEM((G, 2, BLK, LANES), jnp.float32),
        ],
        input_output_aliases={} if first else {11: 1},
        compiler_params=params(),
        cost_estimate=pl.CostEstimate(
            flops=12 * blocks * 512 * 128 * 128 * 2, bytes_accessed=16 << 20, transcendentals=blocks * 512 * 128
        ),
    )(me, slot, valid, q, k, v, g, before, after, glob, fetched, dq_in)


def land(requesters, capacity, idx_ref, used_ref, win_ref, back_ref, up_ref, down_ref, acc):
    rows = acc.shape[1]
    acc[...] = win_ref[...]
    acc[:, rows - BLK : rows, :] += up_ref[...].astype(jnp.float32)
    acc[:, 0:BLK, :] += down_ref[...].astype(jnp.float32)

    def body(a, _):
        @pl.when(used_ref[a] > 0)
        def _():
            for c in range(capacity):
                s = a * capacity + c
                at = pl.multiple_of(idx_ref[s] * BLK, BLK)
                src = pl.multiple_of(s * 2 * BLK, 2 * BLK)
                acc[0, pl.ds(at, BLK), :] += back_ref[pl.ds(src, BLK), :].astype(jnp.float32)
                acc[1, pl.ds(at, BLK), :] += back_ref[pl.ds(src + BLK, BLK), :].astype(jnp.float32)

        return 0

    lax.fori_loop(0, requesters, body, 0)


def first_kernel(
    requesters, capacity, idx_ref, used_ref, glob_ref, win_ref, back_ref, up_ref, down_ref,
    dk_ref, dv_ref, kept_ref, acc,
):
    land(requesters, capacity, idx_ref, used_ref, win_ref, back_ref, up_ref, down_ref, acc)
    dk_ref[...] = acc[0].astype(jnp.bfloat16)
    dv_ref[...] = acc[1].astype(jnp.bfloat16)
    for e in range(G):
        at = pl.multiple_of(glob_ref[e] * BLK, BLK)
        kept_ref[e] = acc[:, pl.ds(at, BLK), :]


def second_kernel(
    requesters, capacity, idx_ref, used_ref, glob_ref, win_ref, back_ref, up_ref, down_ref, gsum_a_ref, gsum_b_ref,
    kept_ref, dk_in_ref, dv_in_ref, dk_ref, dv_ref, acc,
):
    land(requesters, capacity, idx_ref, used_ref, win_ref, back_ref, up_ref, down_ref, acc)
    for e in range(G):

        @pl.when(glob_ref[G + e] == 1)
        def _():
            at = pl.multiple_of(glob_ref[e] * BLK, BLK)
            acc[:, pl.ds(at, BLK), :] += gsum_b_ref[e].astype(jnp.float32)

    dk_ref[:, LANES:] = acc[0].astype(jnp.bfloat16)
    dv_ref[:, LANES:] = acc[1].astype(jnp.bfloat16)
    dk_ref[:, :LANES] = dk_in_ref[...]
    dv_ref[:, :LANES] = dv_in_ref[...]
    for e in range(G):

        @pl.when(glob_ref[G + e] == 1)
        def _():
            at = pl.multiple_of(glob_ref[e] * BLK, BLK)
            total = (kept_ref[e] + gsum_a_ref[e].astype(jnp.float32)).astype(jnp.bfloat16)
            dk_ref[pl.ds(at, BLK), :LANES] = total[0]
            dv_ref[pl.ds(at, BLK), :LANES] = total[1]


def collect_first(idx, used, glob, win, back, up, down, requesters, capacity):
    rows = win.shape[1]
    out = jax.ShapeDtypeStruct((rows, LANES), jnp.bfloat16)
    kept = jax.ShapeDtypeStruct((G, 2, BLK, LANES), jnp.float32)
    return pl.pallas_call(
        functools.partial(first_kernel, requesters, capacity),
        grid=(1,),
        in_specs=[smem()] * 3 + [whole(x.shape) for x in (win, back, up, down)],
        out_specs=(whole(out.shape), whole(out.shape), whole(kept.shape)),
        out_shape=(out, out, kept),
        scratch_shapes=[pltpu.VMEM((2, rows, LANES), jnp.float32)],
        compiler_params=params(),
        cost_estimate=pl.CostEstimate(flops=4 << 20, bytes_accessed=8 << 20, transcendentals=0),
    )(idx, used, glob, win, back, up, down)


def collect_second(idx, used, glob, win, back, up, down, gsum_a, gsum_b, before, requesters, capacity):
    rows = win.shape[1]
    out = jax.ShapeDtypeStruct((rows, 2 * LANES), jnp.bfloat16)
    dk, dv, kept = before
    arrays = (win, back, up, down, gsum_a, gsum_b, kept, dk, dv)
    return pl.pallas_call(
        functools.partial(second_kernel, requesters, capacity),
        grid=(1,),
        in_specs=[smem()] * 3 + [whole(x.shape) for x in arrays],
        out_specs=(whole(out.shape), whole(out.shape)),
        out_shape=(out, out),
        scratch_shapes=[pltpu.VMEM((2, rows, LANES), jnp.float32)],
        compiler_params=params(),
        cost_estimate=pl.CostEstimate(flops=4 << 20, bytes_accessed=8 << 20, transcendentals=0),
    )(idx, used, glob, *arrays)


def share_kernel(at_ref, c0, c1, g0, g1, g2, g3, s0, s1, out_ref, acc):
    @pl.when(pl.program_id(0) == 0)
    def _():
        acc[...] = jnp.zeros_like(acc)

    width = g0.shape[1]
    for r, c in enumerate((c0, c1)):
        for i, g in enumerate((g0, g1, g2, g3)):
            acc[r * LANES : (r + 1) * LANES, i * width : (i + 1) * width] += dot(c[...], g[...], TN)

    @pl.when(pl.program_id(0) == pl.num_programs(0) - 1)
    def _():
        for i in range(4):
            to = pl.multiple_of(((at_ref[0] + i) % 4) * width, width)
            out_ref[:, pl.ds(to, width)] = acc[:, i * width : (i + 1) * width].astype(jnp.bfloat16)
        out_ref[:, 4 * width : 4 * width + LANES] = s0[...]
        out_ref[:, 4 * width + LANES :] = s1[...]


def share_terms(at, contexts, pieces, sums):
    rows, width = pieces[0].shape
    tile = 512
    shape = (2 * LANES, 4 * width + 2 * LANES)
    return pl.pallas_call(
        share_kernel,
        grid=(rows // tile,),
        in_specs=[smem()]
        + [pl.BlockSpec((tile, LANES), lambda i: (i, 0))] * 2
        + [pl.BlockSpec((tile, width), lambda i: (i, 0))] * 4
        + [whole(x.shape) for x in sums],
        out_specs=pl.BlockSpec(shape, lambda i: (0, 0)),
        out_shape=jax.ShapeDtypeStruct(shape, jnp.bfloat16),
        scratch_shapes=[pltpu.VMEM((2 * LANES, 4 * width), jnp.float32)],
        compiler_params=params(),
        cost_estimate=pl.CostEstimate(flops=2 * rows * 1024 * 256, bytes_accessed=6 << 20, transcendentals=0),
    )(at, *contexts, *pieces, *sums)


def project_kernel(*refs):
    contexts, weights, out_ref = refs[:8], refs[8:12], refs[12]
    total = None
    for i, c in enumerate(contexts):
        w = weights[i // 2]
        term = dot(c[...], w[(i % 2) * LANES : (i % 2 + 1) * LANES, :], NN)
        total = term if total is None else total + term
    out_ref[...] = total.astype(jnp.bfloat16)


def project(contexts, weights):
    rows = contexts[0].shape[0]
    width = weights[0].shape[1]
    tile = 512
    return pl.pallas_call(
        project_kernel,
        grid=(rows // tile,),
        in_specs=[pl.BlockSpec((tile, LANES), lambda i: (i, 0))] * 8
        + [pl.BlockSpec(w.shape, lambda i: (0, 0)) for w in weights],
        out_specs=pl.BlockSpec((tile, width), lambda i: (i, 0)),
        out_shape=jax.ShapeDtypeStruct((rows, width), jnp.bfloat16),
        compiler_params=params(),
        cost_estimate=pl.CostEstimate(flops=2 * rows * 1024 * width, bytes_accessed=6 << 20, transcendentals=0),
    )(*contexts, *weights)


def from_others(array, axis):
    size = lax.axis_size(axis)
    found = [array]
    for by in range(1, size):
        found.append(lax.ppermute(array, axis, [((i + by) % size, i) for i in range(size)]))
    return found


def passed_along(array, axis, by):
    size = lax.axis_size(axis)
    pairs = [(i, i + by) for i in range(size) if 0 <= i + by < size]
    return lax.ppermute(array, axis, pairs)


def one_of_four(array, stride):
    span = 4 * stride
    total = array
    for by in (1, 3, 2):
        pairs = [(i, i // span * span + (i + by * stride) % span) for i in range(16)]
        total = total + lax.ppermute(array, "ctx", pairs)
    return total


def per_device(
    queries, key_vectors, value_vectors, grad_output, out_weight, random_ids, random_valid, global_ids
):
    ctx_count = lax.axis_size("ctx")
    tp_count = lax.axis_size("tp")
    me = lax.axis_index("ctx")
    tp_me = lax.axis_index("tp")
    q, k, v, g_out = queries[0], key_vectors[0], value_vectors[0], grad_output[0]
    rows, width = q.shape
    blocks = rows // BLK
    requests = blocks * R
    capacity = requests // (ctx_count * 3 // 4)
    slots = ctx_count * capacity
    barrier = lax.optimization_barrier

    pieces = from_others(g_out, "tp")

    glob_owner = global_ids[0] // blocks
    glob_local = global_ids[0] % blocks
    owned = glob_owner == me
    picked = jnp.concatenate(
        [
            lax.dynamic_slice_in_dim(x, glob_local[e] * BLK, BLK, 0) * owned[e].astype(jnp.bfloat16)
            for e in range(G)
            for x in (k, v)
        ]
    )
    glob = one_of_four(picked, 1)
    before = passed_along(jnp.stack([k[rows - BLK :], v[rows - BLK :]]), "ctx", 1)
    after = passed_along(jnp.stack([k[:BLK], v[:BLK]]), "ctx", -1)

    ids = random_ids[0].reshape(ctx_count, requests)
    owner = ids // blocks
    local = ids % blocks
    order = jnp.arange(requests, dtype=jnp.int32)
    earlier = order[None, :] < order[:, None]
    mine = owner == me
    rank = jnp.sum((mine[:, None, :] & earlier[None]).astype(jnp.int32), axis=2)
    hit = mine[:, None, :] & (rank[:, None, :] == jnp.arange(capacity, dtype=jnp.int32)[None, :, None])
    send_idx = jnp.sum(jnp.where(hit, local[:, None, :], 0), axis=2).reshape(slots)
    send_a = pick_blocks(send_idx, k, v, 0, slots)

    def exchange(array):
        parts = array.reshape(ctx_count, -1, array.shape[-1])
        return lax.all_to_all(parts, "ctx", split_axis=0, concat_axis=0, tiled=True).reshape(array.shape)

    send_a, glob, before, after = barrier((send_a, glob, before, after))
    fetched_a = exchange(send_a)
    glob = one_of_four(glob, 4).reshape(G, 2, BLK, width)
    send_b = pick_blocks(send_idx, k, v, 1, slots)
    used = jnp.sum(mine.astype(jnp.int32), axis=1)
    my_owner = lax.dynamic_index_in_dim(owner, me, 0, keepdims=False)
    my_rank = jnp.sum(((my_owner[:, None] == my_owner[None, :]) & earlier).astype(jnp.int32), axis=1)
    my_slot = my_owner * capacity + my_rank
    valid = lax.dynamic_slice_in_dim(random_valid[0], me * blocks, blocks, 0).reshape(-1)
    tp_at = tp_me.reshape(1)
    wcols = [None] * tp_count
    for by in range(tp_count):
        part = lax.dynamic_slice_in_dim(out_weight, (tp_me + by) % tp_count * width, width, 1)
        if by:
            part = lax.ppermute(part, "tp", [(i, (i + by) % tp_count) for i in range(tp_count)])
        wcols[-by % tp_count] = part
    grad_context = grad_context_of(tp_at, pieces, out_weight)

    ready = barrier((send_b, fetched_a, grad_context, glob, used, my_slot, valid, *wcols))
    send_b, fetched_a, grad_context, glob, used, my_slot, valid, *wcols = ready
    fetched_b = exchange(send_b)
    half = functools.partial(
        attend, blocks * ctx_count - 1, me.reshape(1), my_slot, valid, q, k, v, grad_context, before, after, glob
    )
    ctx_a, dq_a, ret_a, win_a, outer_a, gsum_a = half(fetched_a, None, 0)
    ret_a, fetched_b = barrier((ret_a, fetched_b))
    back_a = exchange(ret_a)
    up_a, down_a = passed_along(outer_a[0], "ctx", -1), passed_along(outer_a[1], "ctx", 1)
    ctx_pieces_a = from_others(ctx_a, "tp")
    ctx_b, grad_q, ret_b, win_b, outer_b, gsum_b = half(fetched_b, dq_a, 1)
    ctx_pieces_b = from_others(ctx_b, "tp")
    up_b, down_b = passed_along(outer_b[0], "ctx", -1), passed_along(outer_b[1], "ctx", 1)

    share = share_terms(tp_at, (ctx_a, ctx_b), pieces, (gsum_a, gsum_b))
    share, back_a = barrier((share, back_a))
    share = exchange(share)
    glob_at = jnp.concatenate([glob_local, owned.astype(jnp.int32)])
    first = collect_first(send_idx, used, glob_at, win_a, back_a, up_a, down_a, ctx_count, capacity)
    ordered = [c for pair in zip(ctx_pieces_a, ctx_pieces_b) for c in pair]
    projected = project(ordered, wcols)
    ready = barrier((ret_b, share, projected, up_b, down_b, *first))
    ret_b, share, projected, up_b, down_b, *first = ready
    back_b = exchange(ret_b)
    share = jnp.sum(share.reshape(ctx_count, -1, share.shape[-1]).astype(jnp.float32), axis=0)
    other = lax.ppermute(share[:, : 4 * width], "dp", [(0, 1), (1, 0)])
    share = jnp.concatenate([share[:, : 4 * width] + other, share[:, 4 * width :]], axis=1).astype(jnp.bfloat16)
    share = lax.all_gather(share, "ctx", axis=0, tiled=True)
    grad_weight = share[:, : 4 * width].astype(jnp.float32)
    gsums = [
        share[:, 4 * width + c * LANES : 4 * width + (c + 1) * LANES].reshape(G, 2, BLK, LANES) for c in range(2)
    ]
    grads = collect_second(
        send_idx, used, glob_at, win_b, back_b, up_b, down_b, *gsums, first, ctx_count, capacity
    )
    return projected[None], grad_q[None], grads[0][None], grads[1][None], grad_weight


def solution(mesh):
    tokens = P("dp", "ctx", "tp")
    in_specs = (
        tokens, tokens, tokens, tokens, P("tp", None), P("dp", None, None), P("dp", None, None), P("dp", None),
    )
    out_specs = (tokens, tokens, tokens, tokens, P("tp", None))
    return jax.shard_map(per_device, mesh=mesh, in_specs=in_specs, out_specs=out_specs, check_vma=False)
```

```python
import functools

import jax
import jax.numpy as jnp
from jax import lax
from jax.experimental import pallas as pl
from jax.experimental.pallas import tpu as pltpu
from jax.sharding import PartitionSpec as P

HD = 64
BLK = 64
R = 3
G = 2
LANES = 128
NEG_FILL = -1e30
VMEM_LIMIT = 56 * 1024 * 1024
CARRIED = 160

NT = (((1,), (1,)), ((), ()))
NN = (((1,), (0,)), ((), ()))
TN = (((0,), (0,)), ((), ()))


def dot(a, b, dims):
    return lax.dot_general(a, b, dims, preferred_element_type=jnp.float32)


def smem():
    return pl.BlockSpec(memory_space=pltpu.SMEM)


def whole(shape, column=None):
    if column is None:
        return pl.BlockSpec(shape, lambda i: (0,) * len(shape))
    return pl.BlockSpec(shape, lambda i: (0,) * (len(shape) - 1) + (column,))


def params(**more):
    return pltpu.CompilerParams(vmem_limit_bytes=VMEM_LIMIT, **more)


def pick_kernel(slots, idx_ref, k_ref, v_ref, out_ref):
    def body(s, _):
        src = pl.multiple_of(idx_ref[s] * BLK, BLK)
        dst = pl.multiple_of(s * 2 * BLK, 2 * BLK)
        out_ref[pl.ds(dst, BLK), :] = k_ref[pl.ds(src, BLK), :]
        out_ref[pl.ds(dst + BLK, BLK), :] = v_ref[pl.ds(src, BLK), :]
        return 0

    lax.fori_loop(0, slots, body, 0, unroll=4)


def pick_blocks(idx, keys, values, column, slots):
    rows = keys.shape[0]
    return pl.pallas_call(
        functools.partial(pick_kernel, slots),
        grid=(1,),
        in_specs=[smem(), whole((rows, LANES), column), whole((rows, LANES), column)],
        out_specs=whole((slots * 2 * BLK, LANES)),
        out_shape=jax.ShapeDtypeStruct((slots * 2 * BLK, LANES), jnp.bfloat16),
        compiler_params=params(),
        cost_estimate=pl.CostEstimate(flops=0, bytes_accessed=10 << 20, transcendentals=0),
    )(idx, keys, values)


def pick_global_kernel(blocks, glob_ref, me_ref, k_ref, v_ref, out_ref):
    owned = glob_ref[pl.program_id(0)] // blocks == me_ref[0]
    out_ref[:BLK, :] = jnp.where(owned, k_ref[...], jnp.zeros_like(k_ref))
    out_ref[BLK:, :] = jnp.where(owned, v_ref[...], jnp.zeros_like(v_ref))


def pick_global(glob, me, keys, values):
    rows, width = keys.shape
    blocks = rows // BLK
    block = pl.BlockSpec((BLK, width), lambda e, glob, me: (glob[e] % blocks, 0))
    return pl.pallas_call(
        functools.partial(pick_global_kernel, blocks),
        grid_spec=pltpu.PrefetchScalarGridSpec(
            num_scalar_prefetch=2,
            grid=(G,),
            in_specs=[block, block],
            out_specs=pl.BlockSpec((2 * BLK, width), lambda e, glob, me: (e, 0)),
        ),
        out_shape=jax.ShapeDtypeStruct((G * 2 * BLK, width), jnp.bfloat16),
        compiler_params=params(),
        cost_estimate=pl.CostEstimate(flops=0, bytes_accessed=1 << 19, transcendentals=0),
    )(glob, me, keys, values)


TILE = 512


def ring_specs(rows, width):
    last = rows // TILE // 2
    full = pl.BlockSpec((TILE, width), lambda i, *_: (i, 0))
    upper = pl.BlockSpec((TILE, width), lambda i, *_: (jnp.minimum(i, last - 1), 0))
    lower = pl.BlockSpec((TILE, width), lambda i, *_: (jnp.maximum(i - last, 0), 0))
    return [full, full, full, upper, lower]


def ring_values(refs):
    own, following, previous, upper, lower = refs
    top = pl.program_id(0) < pl.num_programs(0) // 2
    return own[...], following[...], jnp.where(top, upper[...], lower[...]), previous[...]


def grad_context_kernel(at_ref, *refs):
    del at_ref
    total = None
    for g, w in zip(ring_values(refs[:5]), refs[5:9]):
        term = dot(g, w[...], NT)
        total = term if total is None else total + term
    refs[9][...] = total.astype(jnp.bfloat16)


def grad_context_of(at, pieces, weight):
    rows, width = pieces[0].shape
    heads = weight.shape[0]
    turned = [
        pl.BlockSpec((heads, width), functools.partial(lambda j, i, at: (0, (at[0] + j) % 4), j))
        for j in range(4)
    ]
    return pl.pallas_call(
        grad_context_kernel,
        grid_spec=pltpu.PrefetchScalarGridSpec(
            num_scalar_prefetch=1,
            grid=(rows // TILE,),
            in_specs=ring_specs(rows, width) + turned,
            out_specs=pl.BlockSpec((TILE, heads), lambda i, at: (i, 0)),
        ),
        out_shape=jax.ShapeDtypeStruct((rows, heads), jnp.bfloat16),
        compiler_params=params(),
        cost_estimate=pl.CostEstimate(flops=2 * rows * 1024 * heads, bytes_accessed=16 << 20, transcendentals=0),
    )(at, *pieces, weight, weight, weight, weight)


def attend_kernel(
    blocks, last_block, me_ref, slot_ref, to_ref, valid_ref, q_ref, k_ref, v_ref, g_ref, before_ref, after_ref, glob_ref,
    fetched_ref, dq_in_ref, ctx_ref, dq_ref, win_out_ref, up_ref, down_ref, gsum_out_ref, *more,
):
    del dq_in_ref
    parts_out, (kpad, vpad, win_ref, gsum_ref) = more[:-4], more[-4:]
    if len(parts_out) == 1:
        ret_ref = parts_out[0]
    else:
        *parts_out, ret_ref = parts_out
    rows = blocks * BLK
    kpad[0:BLK, :] = before_ref[0]
    vpad[0:BLK, :] = before_ref[1]
    kpad[rows + BLK : rows + 2 * BLK, :] = after_ref[0]
    vpad[rows + BLK : rows + 2 * BLK, :] = after_ref[1]
    kpad[BLK : rows + BLK, :] = k_ref[...]
    vpad[BLK : rows + BLK, :] = v_ref[...]
    win_ref[...] = jnp.zeros_like(win_ref)
    gsum_ref[...] = jnp.zeros_like(gsum_ref)
    low = lax.broadcasted_iota(jnp.int32, (BLK, LANES), 1) < HD

    def body(i, _):
        row = pl.multiple_of(i * BLK, BLK)
        q = q_ref[pl.ds(row, BLK), :] * jnp.bfloat16(0.125)
        g = g_ref[pl.ds(row, BLK), :]
        zero = jnp.zeros_like(q)
        qbd = jnp.concatenate([jnp.where(low, q, zero), jnp.where(low, zero, q)], axis=0)
        gbd = jnp.concatenate([jnp.where(low, g, zero), jnp.where(low, zero, g)], axis=0)
        starts = [pl.multiple_of(slot_ref[i * R + r] * 2 * BLK, 2 * BLK) for r in range(R)]
        kcat = jnp.concatenate(
            [kpad[pl.ds(row, 3 * BLK), :]]
            + [fetched_ref[pl.ds(s, BLK), :] for s in starts]
            + [glob_ref[0, 0], glob_ref[1, 0]],
            axis=0,
        )
        vcat = jnp.concatenate(
            [vpad[pl.ds(row, 3 * BLK), :]]
            + [fetched_ref[pl.ds(s + BLK, BLK), :] for s in starts]
            + [glob_ref[0, 1], glob_ref[1, 1]],
            axis=0,
        )
        scores = dot(kcat, qbd, NT)
        block = me_ref[0] * blocks + i
        present = [block > 0, None, block < last_block]
        present += [valid_ref[i * R + r] == 1 for r in range(R)] + [None] * G
        parts = []
        for e, there in enumerate(present):
            part = scores[e * BLK : (e + 1) * BLK]
            parts.append(part if there is None else part + jnp.where(there, 0.0, NEG_FILL))
        scores = jnp.concatenate(parts, axis=0)
        peak = jnp.max(scores, axis=0, keepdims=True)
        terms = jnp.exp(scores - peak)
        probs = terms * (1.0 / jnp.sum(terms, axis=0, keepdims=True))
        probs_low = probs.astype(jnp.bfloat16)
        grad_probs = dot(vcat, gbd, NT)
        delta = jnp.sum(probs * grad_probs, axis=0, keepdims=True)
        grad_scores = (probs * (grad_probs - delta)).astype(jnp.bfloat16)
        context = dot(probs_low, vcat, TN)
        grad_q = dot(grad_scores, kcat, TN)
        grad_k = dot(grad_scores, qbd, NN)
        grad_v = dot(probs_low, gbd, NN)
        ctx_ref[pl.ds(row, BLK), :] = jnp.where(low, context[:BLK], context[BLK:]).astype(jnp.bfloat16)
        dq_ref[pl.ds(row, BLK), :] = (
            jnp.where(low, grad_q[:BLK], grad_q[BLK:]) * 0.125
        ).astype(jnp.bfloat16)
        win_ref[0, pl.ds(row, 3 * BLK), :] += grad_k[: 3 * BLK]
        win_ref[1, pl.ds(row, 3 * BLK), :] += grad_v[: 3 * BLK]
        for r in range(R):
            part = slice((3 + r) * BLK, (4 + r) * BLK)
            to = pl.multiple_of(to_ref[i * R + r] * 2 * BLK, 2 * BLK)
            ret_ref[pl.ds(to, BLK), :] = grad_k[part].astype(jnp.bfloat16)
            ret_ref[pl.ds(to + BLK, BLK), :] = grad_v[part].astype(jnp.bfloat16)
        for e in range(G):
            part = slice((3 + R + e) * BLK, (4 + R + e) * BLK)
            gsum_ref[e, 0] += grad_k[part]
            gsum_ref[e, 1] += grad_v[part]
        return 0

    lax.fori_loop(0, blocks, body, 0, unroll=2)
    win_out_ref[...] = win_ref[:, BLK : rows + BLK, :]
    up_ref[...] = win_ref[:, 0:BLK, :].astype(jnp.bfloat16)
    down_ref[...] = win_ref[:, rows + BLK : rows + 2 * BLK, :].astype(jnp.bfloat16)
    gsum_out_ref[...] = gsum_ref[...].reshape(G * 2 * BLK, LANES).astype(jnp.bfloat16)
    if len(parts_out) > 1:
        devices, _, lanes = parts_out[0].shape
        count = ret_ref.shape[0] // 2 // devices
        for p, part_ref in enumerate(parts_out):
            for d in range(devices):
                start = (p * devices + d) * count
                part_ref[d, 0:count, :] = ret_ref[start : start + count, :]


def attend(last_block, me, slot, to, valid, q, k, v, g, before, after, glob, fetched, dq_in, column):
    rows, width = q.shape
    blocks = rows // BLK
    half = whole((rows, LANES), column)
    first = dq_in is None
    shapes = [
        ((rows, LANES), jnp.bfloat16),
        ((rows, width), jnp.bfloat16),
        ((2, rows, LANES), jnp.float32),
        ((2, BLK, LANES), jnp.bfloat16),
        ((2, BLK, LANES), jnp.bfloat16),
        ((G * 2 * BLK, LANES), jnp.bfloat16),
    ]
    scratch = [
        pltpu.VMEM((rows + 2 * BLK, LANES), jnp.bfloat16),
        pltpu.VMEM((rows + 2 * BLK, LANES), jnp.bfloat16),
        pltpu.VMEM((2, rows + 2 * BLK, LANES), jnp.float32),
        pltpu.VMEM((G, 2, BLK, LANES), jnp.float32),
    ]
    if first:
        dq_in = jnp.zeros((16, 128), jnp.bfloat16)
        shapes.append((fetched.shape, jnp.bfloat16))
    else:
        shapes += [((16, fetched.shape[0] // 32 + CARRIED, LANES), jnp.bfloat16)] * 2
        scratch.insert(0, pltpu.VMEM(fetched.shape, jnp.bfloat16))
    specs = [whole(shape) for shape, _ in shapes]
    specs[1] = half
    return pl.pallas_call(
        functools.partial(attend_kernel, blocks, last_block),
        grid=(1,),
        in_specs=[
            smem(), smem(), smem(), smem(), half, half, half, half,
            whole((2, BLK, LANES), column),
            whole((2, BLK, LANES), column),
            whole((G, 2, BLK, LANES), column),
            whole(fetched.shape),
            pl.BlockSpec(memory_space=pl.ANY),
        ],
        out_specs=tuple(specs),
        out_shape=tuple(jax.ShapeDtypeStruct(*shape) for shape in shapes),
        scratch_shapes=scratch,
        input_output_aliases={} if first else {12: 1},
        compiler_params=params(),
        cost_estimate=pl.CostEstimate(
            flops=12 * blocks * 512 * 128 * 128 * 2, bytes_accessed=80 << 20, transcendentals=blocks * 512 * 128
        ),
    )(me, slot, to, valid, q, k, v, g, before, after, glob, fetched, dq_in)


def land(entries, idx_ref, used_ref, back_ref, acc):
    first, end, capacity = entries

    def body(a, _):
        @pl.when(used_ref[a] > 0)
        def _():
            for c in range(first, end):
                at = pl.multiple_of(idx_ref[a * capacity + c] * BLK, BLK)
                src = (c - first) * 2 * BLK
                acc[0, pl.ds(at, BLK), :] += back_ref[a, src : src + BLK, :].astype(jnp.float32)
                acc[1, pl.ds(at, BLK), :] += back_ref[a, src + BLK : src + 2 * BLK, :].astype(jnp.float32)

        return 0

    lax.fori_loop(0, back_ref.shape[0], body, 0)


def edges(up_ref, down_ref, acc):
    rows = acc.shape[1]
    acc[:, rows - BLK : rows, :] += up_ref[...].astype(jnp.float32)
    acc[:, 0:BLK, :] += down_ref[...].astype(jnp.float32)


def first_kernel(
    capacity, idx_ref, used_ref, glob_ref, win_ref, back_ref, up_ref, down_ref, dk_ref, dv_ref, kept_ref, acc
):
    acc[...] = win_ref[...]
    edges(up_ref, down_ref, acc)
    land((0, capacity, capacity), idx_ref, used_ref, back_ref, acc)
    dk_ref[...] = acc[0].astype(jnp.bfloat16)
    dv_ref[...] = acc[1].astype(jnp.bfloat16)
    blocks = acc.shape[1] // BLK
    for e in range(G):
        at = pl.multiple_of(glob_ref[e] % blocks * BLK, BLK)
        kept_ref[e] = acc[:, pl.ds(at, BLK), :]


def middle_kernel(capacity, idx_ref, used_ref, win_ref, back_ref, up_ref, down_ref, acc):
    acc[...] = win_ref[...]
    edges(up_ref, down_ref, acc)
    land((0, capacity // 2, capacity), idx_ref, used_ref, back_ref, acc)


def last_kernel(
    capacity, idx_ref, used_ref, glob_ref, me_ref, win_ref, back_ref, kept_ref, dk_in_ref, dv_in_ref,
    dk_ref, dv_ref, gw_ref, acc,
):
    acc[...] = win_ref[...]
    land((capacity // 2, capacity, capacity), idx_ref, used_ref, back_ref, acc)
    blocks = acc.shape[1] // BLK
    start = capacity * BLK
    sums = start + gw_ref.shape[1] // LANES * 16

    def total(half, e):
        found = [
            jnp.concatenate(
                [
                    back_ref[(e * 2 + t) * 4 + d, sums + half * 16 : sums + (half + 1) * 16, :].astype(jnp.float32)
                    for d in range(4)
                ]
            )
            for t in range(2)
        ]
        return jnp.stack(found)

    for e in range(G):

        @pl.when(glob_ref[e] // blocks == me_ref[0])
        def _():
            at = pl.multiple_of(glob_ref[e] % blocks * BLK, BLK)
            acc[:, pl.ds(at, BLK), :] += total(1, e)

    dk_ref[:, LANES:] = acc[0].astype(jnp.bfloat16)
    dv_ref[:, LANES:] = acc[1].astype(jnp.bfloat16)
    dk_ref[:, :LANES] = dk_in_ref[...]
    dv_ref[:, :LANES] = dv_in_ref[...]
    for e in range(G):

        @pl.when(glob_ref[e] // blocks == me_ref[0])
        def _():
            at = pl.multiple_of(glob_ref[e] % blocks * BLK, BLK)
            both = (kept_ref[e] + total(0, e)).astype(jnp.bfloat16)
            dk_ref[pl.ds(at, BLK), :LANES] = both[0]
            dv_ref[pl.ds(at, BLK), :LANES] = both[1]

    for d in range(back_ref.shape[0]):
        for j in range(gw_ref.shape[1] // LANES):
            rows = back_ref[d, start + 16 * j : start + 16 * (j + 1), :]
            gw_ref[16 * d : 16 * (d + 1), j * LANES : (j + 1) * LANES] = rows.astype(jnp.float32)


def collect_first(idx, used, glob, win, back, up, down, capacity):
    rows = win.shape[1]
    out = jax.ShapeDtypeStruct((rows, LANES), jnp.bfloat16)
    kept = jax.ShapeDtypeStruct((G, 2, BLK, LANES), jnp.float32)
    return pl.pallas_call(
        functools.partial(first_kernel, capacity),
        grid=(1,),
        in_specs=[smem()] * 3 + [whole(x.shape) for x in (win, back, up, down)],
        out_specs=(whole(out.shape), whole(out.shape), whole(kept.shape)),
        out_shape=(out, out, kept),
        scratch_shapes=[pltpu.VMEM((2, rows, LANES), jnp.float32)],
        compiler_params=params(),
        cost_estimate=pl.CostEstimate(flops=4 << 20, bytes_accessed=16 << 20, transcendentals=0),
    )(idx, used, glob, win, back, up, down)


def collect_middle(idx, used, win, back, up, down, capacity):
    return pl.pallas_call(
        functools.partial(middle_kernel, capacity),
        grid=(1,),
        in_specs=[smem()] * 2 + [whole(x.shape) for x in (win, back, up, down)],
        out_specs=whole(win.shape),
        out_shape=jax.ShapeDtypeStruct(win.shape, jnp.float32),
        compiler_params=params(),
        cost_estimate=pl.CostEstimate(flops=4 << 20, bytes_accessed=14 << 20, transcendentals=0),
    )(idx, used, win, back, up, down)


def collect_last(idx, used, glob, me, win, back, before, capacity):
    rows = win.shape[1]
    out = jax.ShapeDtypeStruct((rows, 2 * LANES), jnp.bfloat16)
    weight = jax.ShapeDtypeStruct((2 * LANES, 1024), jnp.float32)
    dk, dv, kept = before
    arrays = (win, back, kept, dk, dv)
    return pl.pallas_call(
        functools.partial(last_kernel, capacity),
        grid=(1,),
        in_specs=[smem()] * 4 + [whole(x.shape) for x in arrays],
        out_specs=(whole(out.shape), whole(out.shape), whole(weight.shape)),
        out_shape=(out, out, weight),
        scratch_shapes=[pltpu.VMEM((2, rows, LANES), jnp.float32)],
        compiler_params=params(),
        cost_estimate=pl.CostEstimate(flops=4 << 20, bytes_accessed=12 << 20, transcendentals=0),
    )(idx, used, glob, me, *arrays)


def weight_kernel(at_ref, c0, c1, *refs):
    pieces, out_ref, acc = refs[:5], refs[5], refs[6]

    @pl.when(pl.program_id(0) == 0)
    def _():
        acc[...] = jnp.zeros_like(acc)

    width = pieces[0].shape[1]
    values = ring_values(pieces)
    for r, c in enumerate((c0, c1)):
        for i, g in enumerate(values):
            acc[r * LANES : (r + 1) * LANES, i * width : (i + 1) * width] += dot(c[...], g, TN)

    @pl.when(pl.program_id(0) == pl.num_programs(0) - 1)
    def _():
        for i in range(4):
            to = pl.multiple_of(((at_ref[0] + i) % 4) * width, width)
            out_ref[:, pl.ds(to, width)] = acc[:, i * width : (i + 1) * width].astype(jnp.bfloat16)


def weight_terms(at, contexts, pieces):
    rows, width = pieces[0].shape
    shape = (2 * LANES, 4 * width)
    return pl.pallas_call(
        weight_kernel,
        grid=(rows // TILE,),
        in_specs=[smem()] + [pl.BlockSpec((TILE, LANES), lambda i: (i, 0))] * 2 + ring_specs(rows, width),
        out_specs=pl.BlockSpec(shape, lambda i: (0, 0)),
        out_shape=jax.ShapeDtypeStruct(shape, jnp.bfloat16),
        scratch_shapes=[pltpu.VMEM(shape, jnp.float32)],
        compiler_params=params(),
        cost_estimate=pl.CostEstimate(flops=2 * rows * 1024 * 256, bytes_accessed=16 << 20, transcendentals=0),
    )(at, *contexts, *pieces)


def carried_spec(devices, rows):
    return pl.BlockSpec((devices, 32, LANES), lambda i: (0, (rows - CARRIED) // 32 + i, 0))


def load_kernel(own_ref, other_ref, s0, s1, part_ref, out_ref):
    del part_ref
    devices = out_ref.shape[0]
    step = pl.program_id(0)

    @pl.when(step < pl.num_programs(0) - 1)
    def _():
        total = (own_ref[...].astype(jnp.float32) + other_ref[...].astype(jnp.float32)).astype(jnp.bfloat16)
        for d in range(devices):
            out_ref[d, 0:16, :] = total[16 * d : 16 * (d + 1), :LANES]
            out_ref[d, 16:32, :] = total[16 * d : 16 * (d + 1), LANES:]

    @pl.when(step == pl.num_programs(0) - 1)
    def _():
        for d in range(devices):
            out_ref[d, 0:16, :] = s0[16 * d : 16 * (d + 1), :]
            out_ref[d, 16:32, :] = s1[16 * d : 16 * (d + 1), :]


def load_terms(own, other, sums, part):
    devices, rows, _ = part.shape
    columns = pl.BlockSpec((own.shape[0], 2 * LANES), lambda i: (0, jnp.minimum(i, 3)))
    return pl.pallas_call(
        load_kernel,
        grid=(CARRIED // 32,),
        in_specs=[columns, columns] + [whole(x.shape) for x in sums] + [pl.BlockSpec(memory_space=pl.ANY)],
        out_specs=carried_spec(devices, rows),
        out_shape=jax.ShapeDtypeStruct(part.shape, part.dtype),
        input_output_aliases={4: 0},
        compiler_params=params(),
        cost_estimate=pl.CostEstimate(flops=1 << 18, bytes_accessed=4 << 20, transcendentals=0),
    )(own, other, *sums, part)


def sum_kernel(back_ref, part_ref, out_ref):
    del part_ref
    total = jnp.sum(back_ref[...].astype(jnp.float32), axis=0).astype(jnp.bfloat16)
    for d in range(out_ref.shape[0]):
        out_ref[d] = total


def load_sums(back, part):
    devices, rows, _ = part.shape
    return pl.pallas_call(
        sum_kernel,
        grid=(CARRIED // 32,),
        in_specs=[carried_spec(devices, rows), pl.BlockSpec(memory_space=pl.ANY)],
        out_specs=carried_spec(devices, rows),
        out_shape=jax.ShapeDtypeStruct(part.shape, part.dtype),
        input_output_aliases={1: 0},
        compiler_params=params(),
        cost_estimate=pl.CostEstimate(flops=1 << 18, bytes_accessed=4 << 20, transcendentals=0),
    )(back, part)


def project_kernel(*refs):
    weights, out_ref = refs[10:14], refs[14]
    halves = ring_values(refs[:5]), ring_values(refs[5:10])
    total = None
    for i in range(4):
        for h in range(2):
            term = dot(halves[h][i], weights[i][h * LANES : (h + 1) * LANES, :], NN)
            total = term if total is None else total + term
    out_ref[...] = total.astype(jnp.bfloat16)


def project(pieces_a, pieces_b, weights):
    rows = pieces_a[0].shape[0]
    width = weights[0].shape[1]
    return pl.pallas_call(
        project_kernel,
        grid=(rows // TILE,),
        in_specs=ring_specs(rows, LANES) * 2 + [pl.BlockSpec(w.shape, lambda i: (0, 0)) for w in weights],
        out_specs=pl.BlockSpec((TILE, width), lambda i: (i, 0)),
        out_shape=jax.ShapeDtypeStruct((rows, width), jnp.bfloat16),
        compiler_params=params(),
        cost_estimate=pl.CostEstimate(flops=2 * rows * 1024 * width, bytes_accessed=18 << 20, transcendentals=0),
    )(*pieces_a, *pieces_b, *weights)


def shifted(array, axis, by):
    size = lax.axis_size(axis)
    return lax.ppermute(array, axis, [((i + by) % size, i) for i in range(size)])


def ring_near(array, axis):
    return shifted(array, axis, 1), shifted(array, axis, -1)


def ring_far(near, axis):
    following, previous = near
    half = following.shape[0] // 2
    return shifted(following[:half], axis, 1), shifted(previous[half:], axis, -1)


def passed_along(array, axis, by):
    size = lax.axis_size(axis)
    pairs = [(i, i + by) for i in range(size) if 0 <= i + by < size]
    return lax.ppermute(array, axis, pairs)


def one_of_four(array, stride):
    span = 4 * stride
    total = array
    for by in (1, 3, 2):
        pairs = [(i, i // span * span + (i + by * stride) % span) for i in range(16)]
        total = total + lax.ppermute(array, "ctx", pairs)
    return total


def per_device(
    queries, key_vectors, value_vectors, grad_output, out_weight, random_ids, random_valid, global_ids
):
    ctx_count = lax.axis_size("ctx")
    tp_count = lax.axis_size("tp")
    me = lax.axis_index("ctx")
    tp_me = lax.axis_index("tp")
    q, k, v, g_out = queries[0], key_vectors[0], value_vectors[0], grad_output[0]
    rows, width = q.shape
    blocks = rows // BLK
    requests = blocks * R
    capacity = requests // (ctx_count * 3 // 4)
    slots = ctx_count * capacity
    barrier = lax.optimization_barrier
    at, tp_at = me.reshape(1), tp_me.reshape(1)
    glob_at = global_ids[0]

    def exchange(parts):
        return lax.all_to_all(parts, "ctx", split_axis=0, concat_axis=0, tiled=True)

    glob = one_of_four(pick_global(glob_at, at, k, v), 1)

    ids = random_ids[0].reshape(ctx_count, requests)
    owner = ids // blocks
    local = ids % blocks
    order = jnp.arange(requests, dtype=jnp.int32)
    earlier = order[None, :] < order[:, None]
    mine = owner == me
    rank = jnp.sum((mine[:, None, :] & earlier[None]).astype(jnp.int32), axis=2)
    hit = mine[:, None, :] & (rank[:, None, :] == jnp.arange(capacity, dtype=jnp.int32)[None, :, None])
    send_idx = jnp.sum(jnp.where(hit, local[:, None, :], 0), axis=2).reshape(slots)
    send_a = pick_blocks(send_idx, k, v, 0, slots)

    send_a, glob = barrier((send_a, glob))
    fetched_a = exchange(send_a.reshape(ctx_count, -1, LANES)).reshape(send_a.shape)
    near = ring_near(g_out, "tp")
    glob = one_of_four(glob, 4).reshape(G, 2, BLK, width)
    before = passed_along(jnp.stack([k[rows - BLK :], v[rows - BLK :]]), "ctx", 1)
    after = passed_along(jnp.stack([k[:BLK], v[:BLK]]), "ctx", -1)
    send_b = pick_blocks(send_idx, k, v, 1, slots)
    pieces = (g_out, *near, *ring_far(near, "tp"))
    grad_context = grad_context_of(tp_at, pieces, out_weight)
    used = jnp.sum(mine.astype(jnp.int32), axis=1)
    my_owner = lax.dynamic_index_in_dim(owner, me, 0, keepdims=False)
    my_rank = jnp.sum(((my_owner[:, None] == my_owner[None, :]) & earlier).astype(jnp.int32), axis=1)
    my_slot = my_owner * capacity + my_rank
    part_size = capacity // 2
    my_part = my_rank // part_size
    my_place = (my_part * ctx_count + my_owner) * part_size + my_rank % part_size
    valid = lax.dynamic_slice_in_dim(random_valid[0], me * blocks, blocks, 0).reshape(-1)

    ready = barrier((send_b, fetched_a, grad_context, glob, before, after, used, my_slot, my_place, valid))
    send_b, fetched_a, grad_context, glob, before, after, used, my_slot, my_place, valid = ready

    fetched_b = exchange(send_b.reshape(ctx_count, -1, LANES)).reshape(send_b.shape)
    wcols = [None] * tp_count
    for by in range(tp_count):
        part = lax.dynamic_slice_in_dim(out_weight, (tp_me + by) % tp_count * width, width, 1)
        wcols[-by % tp_count] = shifted(part, "tp", -by) if by else part
    last_block = blocks * ctx_count - 1

    def half(to, fetched, dq_in, column):
        return attend(
            last_block, at, my_slot, to, valid, q, k, v, grad_context, before, after, glob, fetched, dq_in, column
        )

    ctx_a, dq_a, win_a, up_a, down_a, gsum_a, ret_a = half(my_slot, fetched_a, None, 0)
    near_a = ring_near(ctx_a, "tp")
    ret_a, fetched_b, wcols, near_a = barrier((ret_a, fetched_b, wcols, near_a))

    back_a = exchange(ret_a.reshape(ctx_count, -1, LANES))
    pieces_a = (ctx_a, *near_a, *ring_far(near_a, "tp"))
    up_a, down_a = passed_along(up_a, "ctx", -1), passed_along(down_a, "ctx", 1)
    ctx_b, grad_q, win_b, up_b, down_b, gsum_b, ret_b, ret_c = half(my_place, fetched_b, dq_a, 1)
    near_b = ring_near(ctx_b, "tp")
    terms = weight_terms(tp_at, (ctx_a, ctx_b), pieces)
    ret_b = load_terms(terms, shifted(terms, "dp", 1), (gsum_a, gsum_b), ret_b)
    ret_b, back_a, up_a, down_a, near_b = barrier((ret_b, back_a, up_a, down_a, near_b))

    back_b = exchange(ret_b)
    up_b, down_b = passed_along(up_b, "ctx", -1), passed_along(down_b, "ctx", 1)
    pieces_b = (ctx_b, *near_b, *ring_far(near_b, "tp"))
    first = collect_first(
        send_idx, used, glob_at, win_a, back_a, up_a, down_a, capacity
    )
    ret_c = load_sums(back_b, ret_c)
    ret_c, up_b, down_b, pieces_b, first = barrier((ret_c, up_b, down_b, pieces_b, first))

    back_c = exchange(ret_c)
    projected = project(pieces_a, pieces_b, wcols)
    win_b = collect_middle(send_idx, used, win_b, back_b, up_b, down_b, capacity)
    projected, win_b, back_c = barrier((projected, win_b, back_c))
    grad_k, grad_v, grad_weight = collect_last(send_idx, used, glob_at, at, win_b, back_c, first, capacity)
    return projected[None], grad_q[None], grad_k[None], grad_v[None], grad_weight


def solution(mesh):
    tokens = P("dp", "ctx", "tp")
    in_specs = (
        tokens, tokens, tokens, tokens, P("tp", None), P("dp", None, None), P("dp", None, None), P("dp", None),
    )
    out_specs = (tokens, tokens, tokens, tokens, P("tp", None))
    return jax.shard_map(per_device, mesh=mesh, in_specs=in_specs, out_specs=out_specs, check_vma=False)
```

```python
import functools

import jax
import jax.numpy as jnp
from jax import lax
from jax.experimental import pallas as pl
from jax.experimental.pallas import tpu as pltpu
from jax.sharding import PartitionSpec as P

HD = 64
BLK = 64
R = 3
G = 2
LANES = 128
NEG_FILL = -1e30
VMEM_LIMIT = 56 * 1024 * 1024
CARRIED = 160

NT = (((1,), (1,)), ((), ()))
NN = (((1,), (0,)), ((), ()))
TN = (((0,), (0,)), ((), ()))


def dot(a, b, dims):
    return lax.dot_general(a, b, dims, preferred_element_type=jnp.float32)


def smem():
    return pl.BlockSpec(memory_space=pltpu.SMEM)


def whole(shape, column=None):
    if column is None:
        return pl.BlockSpec(shape, lambda i: (0,) * len(shape))
    return pl.BlockSpec(shape, lambda i: (0,) * (len(shape) - 1) + (column,))


def params(**more):
    return pltpu.CompilerParams(vmem_limit_bytes=VMEM_LIMIT, **more)


def pick_kernel(slots, idx_ref, k_ref, v_ref, out_ref):
    def body(s, _):
        src = pl.multiple_of(idx_ref[s] * BLK, BLK)
        dst = pl.multiple_of(s * 2 * BLK, 2 * BLK)
        out_ref[pl.ds(dst, BLK), :] = k_ref[pl.ds(src, BLK), :]
        out_ref[pl.ds(dst + BLK, BLK), :] = v_ref[pl.ds(src, BLK), :]
        return 0

    lax.fori_loop(0, slots, body, 0, unroll=4)


def pick_blocks(idx, keys, values, column, slots):
    rows = keys.shape[0]
    return pl.pallas_call(
        functools.partial(pick_kernel, slots),
        grid=(1,),
        in_specs=[smem(), whole((rows, LANES), column), whole((rows, LANES), column)],
        out_specs=whole((slots * 2 * BLK, LANES)),
        out_shape=jax.ShapeDtypeStruct((slots * 2 * BLK, LANES), jnp.bfloat16),
        compiler_params=params(),
        cost_estimate=pl.CostEstimate(flops=0, bytes_accessed=10 << 20, transcendentals=0),
    )(idx, keys, values)


def pick_global_kernel(blocks, glob_ref, me_ref, k0, v0, k1, v1, k_first, v_first, k_last, v_last, up_ref, down_ref, out_ref):
    for e, pair in enumerate(((k0, v0), (k1, v1))):
        owned = glob_ref[e] // blocks == me_ref[0]
        for t, x in enumerate(pair):
            at = (e * 2 + t) * BLK
            picked = jnp.where(owned, x[...], jnp.zeros_like(x))
            for ref in (up_ref, down_ref, out_ref):
                ref[at : at + BLK, :] = picked
    at = 2 * G * BLK
    up_ref[at : at + BLK, :] = k_last[...]
    up_ref[at + BLK : at + 2 * BLK, :] = v_last[...]
    down_ref[at : at + BLK, :] = k_first[...]
    down_ref[at + BLK : at + 2 * BLK, :] = v_first[...]


def pick_global(glob, me, keys, values):
    rows, width = keys.shape
    blocks = rows // BLK

    def block(place):
        return [pl.BlockSpec((BLK, width), lambda i, glob, me: (place(glob), 0))] * 2

    specs = block(lambda glob: glob[0] % blocks) + block(lambda glob: glob[1] % blocks)
    specs += block(lambda glob: 0) + block(lambda glob: blocks - 1)
    sizes = (2 * G + 2) * BLK, (2 * G + 2) * BLK, 2 * G * BLK
    return pl.pallas_call(
        functools.partial(pick_global_kernel, blocks),
        grid_spec=pltpu.PrefetchScalarGridSpec(
            num_scalar_prefetch=2,
            grid=(1,),
            in_specs=specs,
            out_specs=tuple(pl.BlockSpec((n, width), lambda i, glob, me: (0, 0)) for n in sizes),
        ),
        out_shape=tuple(jax.ShapeDtypeStruct((n, width), jnp.bfloat16) for n in sizes),
        compiler_params=params(),
        cost_estimate=pl.CostEstimate(flops=0, bytes_accessed=1 << 19, transcendentals=0),
    )(glob, me, *[keys, values] * 4)


def sum_four_kernel(a, b, c, d, out_ref):
    out_ref[...] = a[...] + b[...] + c[...] + d[...]


def sum_four(arrays):
    shape = arrays[0].shape
    return pl.pallas_call(
        sum_four_kernel,
        grid=(1,),
        in_specs=[whole(shape)] * 4,
        out_specs=whole(shape),
        out_shape=jax.ShapeDtypeStruct(shape, jnp.bfloat16),
        compiler_params=params(),
        cost_estimate=pl.CostEstimate(flops=0, bytes_accessed=60 << 20, transcendentals=0),
    )(*arrays)


TILE = 512


def ring_specs(rows, width):
    last = rows // TILE // 2
    full = pl.BlockSpec((TILE, width), lambda i, *_: (i, 0))
    upper = pl.BlockSpec((TILE, width), lambda i, *_: (jnp.minimum(i, last - 1), 0))
    lower = pl.BlockSpec((TILE, width), lambda i, *_: (jnp.maximum(i - last, 0), 0))
    return [full, full, full, upper, lower]


def ring_values(refs):
    own, following, previous, upper, lower = refs
    top = pl.program_id(0) < pl.num_programs(0) // 2
    return own[...], following[...], jnp.where(top, upper[...], lower[...]), previous[...]


def pair_specs(rows, width):
    last = rows // TILE // 2
    specs = [pl.BlockSpec((TILE, width), lambda i, at: (i, 0))]
    for d in range(2):
        full = pl.BlockSpec((TILE, width), functools.partial(lambda d, i, at: (jnp.where(at[1] == d, i, 0), 0), d))
        upper = functools.partial(lambda d, i, at: (jnp.where(at[1] == d, jnp.minimum(i, last - 1), 0), 0), d)
        lower = functools.partial(lambda d, i, at: (jnp.where(at[1] == d, jnp.maximum(i - last, 0), 0), 0), d)
        specs += [full, full, pl.BlockSpec((TILE, width), upper), pl.BlockSpec((TILE, width), lower)]
    return specs


def pair_values(at_ref, refs):
    top = pl.program_id(0) < pl.num_programs(0) // 2
    zero = at_ref[1] == 0

    def chosen(j):
        return jnp.where(zero, refs[1 + j][...], refs[5 + j][...])

    return refs[0][...], chosen(0), jnp.where(top, chosen(2), chosen(3)), chosen(1)


def grad_context_kernel(at_ref, *refs):
    total = None
    for g, w in zip(pair_values(at_ref, refs[:9]), refs[9:13]):
        term = dot(g, w[...], NT)
        total = term if total is None else total + term
    refs[13][...] = total.astype(jnp.bfloat16)


def grad_context_of(at, pieces, weight):
    rows, width = pieces[0].shape
    heads = weight.shape[0]
    turned = [
        pl.BlockSpec((heads, width), functools.partial(lambda j, i, at: (0, (at[0] + j) % 4), j))
        for j in range(4)
    ]
    return pl.pallas_call(
        grad_context_kernel,
        grid_spec=pltpu.PrefetchScalarGridSpec(
            num_scalar_prefetch=1,
            grid=(rows // TILE,),
            in_specs=pair_specs(rows, width) + turned,
            out_specs=pl.BlockSpec((TILE, heads), lambda i, at: (i, 0)),
        ),
        out_shape=jax.ShapeDtypeStruct((rows, heads), jnp.bfloat16),
        compiler_params=params(),
        cost_estimate=pl.CostEstimate(flops=2 * rows * 1024 * heads, bytes_accessed=16 << 20, transcendentals=0),
    )(at, *pieces, weight, weight, weight, weight)


def attend_kernel(
    blocks, last_block, me_ref, slot_ref, to_ref, valid_ref, q_ref, k_ref, v_ref, g_ref, before_ref, after_ref, glob_ref,
    fetched_ref, dq_in_ref, ctx_ref, dq_ref, win_out_ref, up_ref, down_ref, gsum_out_ref, *more,
):
    del dq_in_ref
    parts_out, (kpad, vpad, win_ref, gsum_ref) = more[:-4], more[-4:]
    if len(parts_out) == 1:
        ret_ref = parts_out[0]
    else:
        *parts_out, ret_ref = parts_out
    rows = blocks * BLK
    kpad[0:BLK, :] = before_ref[0:BLK, :]
    vpad[0:BLK, :] = before_ref[BLK : 2 * BLK, :]
    kpad[rows + BLK : rows + 2 * BLK, :] = after_ref[0:BLK, :]
    vpad[rows + BLK : rows + 2 * BLK, :] = after_ref[BLK : 2 * BLK, :]
    kpad[BLK : rows + BLK, :] = k_ref[...]
    vpad[BLK : rows + BLK, :] = v_ref[...]
    win_ref[...] = jnp.zeros_like(win_ref)
    gsum_ref[...] = jnp.zeros_like(gsum_ref)
    low = lax.broadcasted_iota(jnp.int32, (BLK, LANES), 1) < HD

    def body(i, _):
        row = pl.multiple_of(i * BLK, BLK)
        q = q_ref[pl.ds(row, BLK), :] * jnp.bfloat16(0.125)
        g = g_ref[pl.ds(row, BLK), :]
        zero = jnp.zeros_like(q)
        qbd = jnp.concatenate([jnp.where(low, q, zero), jnp.where(low, zero, q)], axis=0)
        gbd = jnp.concatenate([jnp.where(low, g, zero), jnp.where(low, zero, g)], axis=0)
        starts = [pl.multiple_of(slot_ref[i * R + r] * 2 * BLK, 2 * BLK) for r in range(R)]
        kcat = jnp.concatenate(
            [kpad[pl.ds(row, 3 * BLK), :]]
            + [fetched_ref[pl.ds(s, BLK), :] for s in starts]
            + [glob_ref[0, 0], glob_ref[1, 0]],
            axis=0,
        )
        vcat = jnp.concatenate(
            [vpad[pl.ds(row, 3 * BLK), :]]
            + [fetched_ref[pl.ds(s + BLK, BLK), :] for s in starts]
            + [glob_ref[0, 1], glob_ref[1, 1]],
            axis=0,
        )
        scores = dot(kcat, qbd, NT)
        block = me_ref[0] * blocks + i
        present = [block > 0, None, block < last_block]
        present += [valid_ref[i * R + r] == 1 for r in range(R)] + [None] * G
        parts = []
        for e, there in enumerate(present):
            part = scores[e * BLK : (e + 1) * BLK]
            parts.append(part if there is None else part + jnp.where(there, 0.0, NEG_FILL))
        scores = jnp.concatenate(parts, axis=0)
        peak = jnp.max(scores, axis=0, keepdims=True)
        terms = jnp.exp(scores - peak)
        probs = terms * (1.0 / jnp.sum(terms, axis=0, keepdims=True))
        probs_low = probs.astype(jnp.bfloat16)
        grad_probs = dot(vcat, gbd, NT)
        delta = jnp.sum(probs * grad_probs, axis=0, keepdims=True)
        grad_scores = (probs * (grad_probs - delta)).astype(jnp.bfloat16)
        context = dot(probs_low, vcat, TN)
        grad_q = dot(grad_scores, kcat, TN)
        grad_k = dot(grad_scores, qbd, NN)
        grad_v = dot(probs_low, gbd, NN)
        ctx_ref[pl.ds(row, BLK), :] = jnp.where(low, context[:BLK], context[BLK:]).astype(jnp.bfloat16)
        dq_ref[pl.ds(row, BLK), :] = (
            jnp.where(low, grad_q[:BLK], grad_q[BLK:]) * 0.125
        ).astype(jnp.bfloat16)
        win_ref[0, pl.ds(row, 3 * BLK), :] += grad_k[: 3 * BLK]
        win_ref[1, pl.ds(row, 3 * BLK), :] += grad_v[: 3 * BLK]
        for r in range(R):
            part = slice((3 + r) * BLK, (4 + r) * BLK)
            to = pl.multiple_of(to_ref[i * R + r] * 2 * BLK, 2 * BLK)
            ret_ref[pl.ds(to, BLK), :] = grad_k[part].astype(jnp.bfloat16)
            ret_ref[pl.ds(to + BLK, BLK), :] = grad_v[part].astype(jnp.bfloat16)
        for e in range(G):
            part = slice((3 + R + e) * BLK, (4 + R + e) * BLK)
            gsum_ref[e, 0] += grad_k[part]
            gsum_ref[e, 1] += grad_v[part]
        return 0

    lax.fori_loop(0, blocks, body, 0, unroll=2)
    win_out_ref[...] = win_ref[:, BLK : rows + BLK, :]
    up_ref[...] = win_ref[:, 0:BLK, :].astype(jnp.bfloat16)
    down_ref[...] = win_ref[:, rows + BLK : rows + 2 * BLK, :].astype(jnp.bfloat16)
    gsum_out_ref[...] = gsum_ref[...].reshape(G * 2 * BLK, LANES).astype(jnp.bfloat16)
    if len(parts_out) > 1:
        devices, _, lanes = parts_out[0].shape
        count = ret_ref.shape[0] // 2 // devices
        for p, part_ref in enumerate(parts_out):
            for d in range(devices):
                start = (p * devices + d) * count
                part_ref[d, CARRIED : CARRIED + count, :] = ret_ref[start : start + count, :]


def attend(last_block, me, slot, to, valid, q, k, v, g, before, after, glob, fetched, dq_in, column):
    rows, width = q.shape
    blocks = rows // BLK
    half = whole((rows, LANES), column)
    first = dq_in is None
    shapes = [
        ((rows, LANES), jnp.bfloat16),
        ((rows, width), jnp.bfloat16),
        ((2, rows, LANES), jnp.float32),
        ((2, BLK, LANES), jnp.bfloat16),
        ((2, BLK, LANES), jnp.bfloat16),
        ((G * 2 * BLK, LANES), jnp.bfloat16),
    ]
    scratch = [
        pltpu.VMEM((rows + 2 * BLK, LANES), jnp.bfloat16),
        pltpu.VMEM((rows + 2 * BLK, LANES), jnp.bfloat16),
        pltpu.VMEM((2, rows + 2 * BLK, LANES), jnp.float32),
        pltpu.VMEM((G, 2, BLK, LANES), jnp.float32),
    ]
    if first:
        dq_in = jnp.zeros((16, 128), jnp.bfloat16)
        shapes.append((fetched.shape, jnp.bfloat16))
    else:
        shapes += [((16, fetched.shape[0] // 32 + CARRIED, LANES), jnp.bfloat16)] * 2
        scratch.insert(0, pltpu.VMEM(fetched.shape, jnp.bfloat16))
    specs = [whole(shape) for shape, _ in shapes]
    specs[1] = half
    return pl.pallas_call(
        functools.partial(attend_kernel, blocks, last_block),
        grid=(1,),
        in_specs=[
            smem(), smem(), smem(), smem(), half, half, half, half,
            pl.BlockSpec((2 * BLK, LANES), lambda i: (G, column)),
            pl.BlockSpec((2 * BLK, LANES), lambda i: (G, column)),
            whole((G, 2, BLK, LANES), column),
            whole(fetched.shape),
            pl.BlockSpec(memory_space=pl.ANY),
        ],
        out_specs=tuple(specs),
        out_shape=tuple(jax.ShapeDtypeStruct(*shape) for shape in shapes),
        scratch_shapes=scratch,
        input_output_aliases={} if first else {12: 1},
        compiler_params=params(),
        cost_estimate=pl.CostEstimate(
            flops=12 * blocks * 512 * 128 * 128 * 2, bytes_accessed=80 << 20, transcendentals=blocks * 512 * 128
        ),
    )(me, slot, to, valid, q, k, v, g, before, after, glob, fetched, dq_in)


def land(entries, idx_ref, used_ref, back_ref, acc):
    first, end, capacity, skipped = entries

    def body(a, _):
        @pl.when(used_ref[a] > 0)
        def _():
            for c in range(first, end):
                at = pl.multiple_of(idx_ref[a * capacity + c] * BLK, BLK)
                src = skipped + (c - first) * 2 * BLK
                acc[0, pl.ds(at, BLK), :] += back_ref[a, src : src + BLK, :].astype(jnp.float32)
                acc[1, pl.ds(at, BLK), :] += back_ref[a, src + BLK : src + 2 * BLK, :].astype(jnp.float32)

        return 0

    lax.fori_loop(0, back_ref.shape[0], body, 0)


def edges(up_ref, down_ref, acc):
    rows = acc.shape[1]
    acc[:, rows - BLK : rows, :] += up_ref[...].astype(jnp.float32)
    acc[:, 0:BLK, :] += down_ref[...].astype(jnp.float32)


def first_kernel(
    capacity, idx_ref, used_ref, glob_ref, win_ref, back_ref, up_ref, down_ref, dk_ref, dv_ref, kept_ref, acc
):
    acc[...] = win_ref[...]
    edges(up_ref, down_ref, acc)
    land((0, capacity, capacity, 0), idx_ref, used_ref, back_ref, acc)
    dk_ref[...] = acc[0].astype(jnp.bfloat16)
    dv_ref[...] = acc[1].astype(jnp.bfloat16)
    blocks = acc.shape[1] // BLK
    for e in range(G):
        at = pl.multiple_of(glob_ref[e] % blocks * BLK, BLK)
        kept_ref[e] = acc[:, pl.ds(at, BLK), :]


def middle_kernel(capacity, idx_ref, used_ref, win_ref, back_ref, up_ref, down_ref, acc):
    acc[...] = win_ref[...]
    edges(up_ref, down_ref, acc)
    land((0, capacity // 2, capacity, CARRIED), idx_ref, used_ref, back_ref, acc)


def last_kernel(
    capacity, idx_ref, used_ref, glob_ref, me_ref, win_ref, back_ref, kept_ref, dk_in_ref, dv_in_ref,
    dk_ref, dv_ref, acc,
):
    acc[...] = win_ref[...]
    land((capacity // 2, capacity, capacity, CARRIED), idx_ref, used_ref, back_ref, acc)
    blocks = acc.shape[1] // BLK
    sums = CARRIED - 32

    def total(half, e):
        found = [
            jnp.concatenate(
                [
                    back_ref[(e * 2 + t) * 4 + d, sums + half * 16 : sums + (half + 1) * 16, :].astype(jnp.float32)
                    for d in range(4)
                ]
            )
            for t in range(2)
        ]
        return jnp.stack(found)

    for e in range(G):

        @pl.when(glob_ref[e] // blocks == me_ref[0])
        def _():
            at = pl.multiple_of(glob_ref[e] % blocks * BLK, BLK)
            acc[:, pl.ds(at, BLK), :] += total(1, e)

    dk_ref[:, LANES:] = acc[0].astype(jnp.bfloat16)
    dv_ref[:, LANES:] = acc[1].astype(jnp.bfloat16)
    dk_ref[:, :LANES] = dk_in_ref[...]
    dv_ref[:, :LANES] = dv_in_ref[...]
    for e in range(G):

        @pl.when(glob_ref[e] // blocks == me_ref[0])
        def _():
            at = pl.multiple_of(glob_ref[e] % blocks * BLK, BLK)
            both = (kept_ref[e] + total(0, e)).astype(jnp.bfloat16)
            dk_ref[pl.ds(at, BLK), :LANES] = both[0]
            dv_ref[pl.ds(at, BLK), :LANES] = both[1]


def collect_first(idx, used, glob, win, back, up, down, capacity):
    rows = win.shape[1]
    out = jax.ShapeDtypeStruct((rows, LANES), jnp.bfloat16)
    kept = jax.ShapeDtypeStruct((G, 2, BLK, LANES), jnp.float32)
    return pl.pallas_call(
        functools.partial(first_kernel, capacity),
        grid=(1,),
        in_specs=[smem()] * 3 + [whole(x.shape) for x in (win, back, up, down)],
        out_specs=(whole(out.shape), whole(out.shape), whole(kept.shape)),
        out_shape=(out, out, kept),
        scratch_shapes=[pltpu.VMEM((2, rows, LANES), jnp.float32)],
        compiler_params=params(),
        cost_estimate=pl.CostEstimate(flops=4 << 20, bytes_accessed=16 << 20, transcendentals=0),
    )(idx, used, glob, win, back, up, down)


def collect_middle(idx, used, win, back, up, down, capacity):
    return pl.pallas_call(
        functools.partial(middle_kernel, capacity),
        grid=(1,),
        in_specs=[smem()] * 2 + [whole(x.shape) for x in (win, back, up, down)],
        out_specs=whole(win.shape),
        out_shape=jax.ShapeDtypeStruct(win.shape, jnp.float32),
        compiler_params=params(),
        cost_estimate=pl.CostEstimate(flops=4 << 20, bytes_accessed=14 << 20, transcendentals=0),
    )(idx, used, win, back, up, down)


def collect_last(idx, used, glob, me, win, back, before, capacity):
    rows = win.shape[1]
    out = jax.ShapeDtypeStruct((rows, 2 * LANES), jnp.bfloat16)
    dk, dv, kept = before
    arrays = (win, back, kept, dk, dv)
    return pl.pallas_call(
        functools.partial(last_kernel, capacity),
        grid=(1,),
        in_specs=[smem()] * 4 + [whole(x.shape) for x in arrays],
        out_specs=(whole(out.shape), whole(out.shape)),
        out_shape=(out, out),
        scratch_shapes=[pltpu.VMEM((2, rows, LANES), jnp.float32)],
        compiler_params=params(),
        cost_estimate=pl.CostEstimate(flops=4 << 20, bytes_accessed=12 << 20, transcendentals=0),
    )(idx, used, glob, me, *arrays)


def weight_kernel(at_ref, c0, c1, *refs):
    pieces, out_ref, acc = refs[:9], refs[9], refs[10]

    @pl.when(pl.program_id(0) == 0)
    def _():
        acc[...] = jnp.zeros_like(acc)

    width = pieces[0].shape[1]
    values = pair_values(at_ref, pieces)
    for r, c in enumerate((c0, c1)):
        for i, g in enumerate(values):
            acc[r * LANES : (r + 1) * LANES, i * width : (i + 1) * width] += dot(c[...], g, TN)

    @pl.when(pl.program_id(0) == pl.num_programs(0) - 1)
    def _():
        for i in range(4):
            to = pl.multiple_of(((at_ref[0] + i) % 4) * width, width)
            out_ref[:, pl.ds(to, width)] = acc[:, i * width : (i + 1) * width].astype(jnp.bfloat16)


def weight_terms(at, contexts, pieces):
    rows, width = pieces[0].shape
    shape = (2 * LANES, 4 * width)
    return pl.pallas_call(
        weight_kernel,
        grid_spec=pltpu.PrefetchScalarGridSpec(
            num_scalar_prefetch=1,
            grid=(rows // TILE,),
            in_specs=[pl.BlockSpec((TILE, LANES), lambda i, at: (i, 0))] * 2 + pair_specs(rows, width),
            out_specs=pl.BlockSpec(shape, lambda i, at: (0, 0)),
            scratch_shapes=[pltpu.VMEM(shape, jnp.float32)],
        ),
        out_shape=jax.ShapeDtypeStruct(shape, jnp.bfloat16),
        compiler_params=params(),
        cost_estimate=pl.CostEstimate(flops=2 * rows * 1024 * 256, bytes_accessed=16 << 20, transcendentals=0),
    )(at, *contexts, *pieces)


def carried(array):
    return whole((array.shape[0], CARRIED, LANES))


def load_kernel(terms_ref, s0, s1, part_ref, out_ref):
    del part_ref
    for d in range(out_ref.shape[0]):
        rows = slice(16 * d, 16 * (d + 1))
        for j in range(terms_ref.shape[1] // LANES):
            out_ref[d, 16 * j : 16 * (j + 1), :] = terms_ref[rows, j * LANES : (j + 1) * LANES]
        out_ref[d, CARRIED - 32 : CARRIED - 16, :] = s0[rows, :]
        out_ref[d, CARRIED - 16 :, :] = s1[rows, :]


def load_terms(terms, sums, part):
    return pl.pallas_call(
        load_kernel,
        grid=(1,),
        in_specs=[whole(x.shape) for x in (terms, *sums)] + [pl.BlockSpec(memory_space=pl.ANY)],
        out_specs=carried(part),
        out_shape=jax.ShapeDtypeStruct(part.shape, part.dtype),
        input_output_aliases={3: 0},
        compiler_params=params(),
        cost_estimate=pl.CostEstimate(flops=1 << 18, bytes_accessed=4 << 20, transcendentals=0),
    )(terms, *sums, part)


def sum_kernel(back_ref, part_ref, out_ref):
    del part_ref
    total = jnp.sum(back_ref[...].astype(jnp.float32), axis=0).astype(jnp.bfloat16)
    for d in range(out_ref.shape[0]):
        out_ref[d] = total


def load_sums(back, part):
    return pl.pallas_call(
        sum_kernel,
        grid=(1,),
        in_specs=[carried(back), pl.BlockSpec(memory_space=pl.ANY)],
        out_specs=carried(part),
        out_shape=jax.ShapeDtypeStruct(part.shape, part.dtype),
        input_output_aliases={1: 0},
        compiler_params=params(),
        cost_estimate=pl.CostEstimate(flops=1 << 18, bytes_accessed=4 << 20, transcendentals=0),
    )(back, part)


def weight_sum_kernel(own_ref, other_ref, out_ref):
    total = own_ref[...].astype(jnp.float32) + other_ref[...].astype(jnp.float32)
    for d in range(total.shape[0]):
        for j in range(out_ref.shape[1] // LANES):
            out_ref[16 * d : 16 * (d + 1), j * LANES : (j + 1) * LANES] = total[d, 16 * j : 16 * (j + 1), :]


def weight_sum(own, other):
    shape = (2 * LANES, 1024)
    return pl.pallas_call(
        weight_sum_kernel,
        grid=(1,),
        in_specs=[whole(own.shape), whole(other.shape)],
        out_specs=whole(shape),
        out_shape=jax.ShapeDtypeStruct(shape, jnp.float32),
        compiler_params=params(),
        cost_estimate=pl.CostEstimate(flops=1 << 18, bytes_accessed=2 << 20, transcendentals=0),
    )(own, other)


def project_kernel(*refs):
    weights, out_ref = refs[10:14], refs[14]
    halves = ring_values(refs[:5]), ring_values(refs[5:10])
    total = None
    for i in range(4):
        for h in range(2):
            term = dot(halves[h][i], weights[i][h * LANES : (h + 1) * LANES, :], NN)
            total = term if total is None else total + term
    out_ref[...] = total.astype(jnp.bfloat16)


def project(pieces_a, pieces_b, weights):
    rows = pieces_a[0].shape[0]
    width = weights[0].shape[1]
    return pl.pallas_call(
        project_kernel,
        grid=(rows // TILE,),
        in_specs=ring_specs(rows, LANES) * 2 + [pl.BlockSpec(w.shape, lambda i: (0, 0)) for w in weights],
        out_specs=pl.BlockSpec((TILE, width), lambda i: (i, 0)),
        out_shape=jax.ShapeDtypeStruct((rows, width), jnp.bfloat16),
        compiler_params=params(),
        cost_estimate=pl.CostEstimate(flops=2 * rows * 1024 * width, bytes_accessed=18 << 20, transcendentals=0),
    )(*pieces_a, *pieces_b, *weights)


def shifted(array, axis, by):
    size = lax.axis_size(axis)
    return lax.ppermute(array, axis, [((i + by) % size, i) for i in range(size)])


def ring_near(array, axis):
    return shifted(array, axis, 1), shifted(array, axis, -1)


def ring_far(near, axis):
    following, previous = near
    half = following.shape[0] // 2
    return shifted(following[:half], axis, 1), shifted(previous[half:], axis, -1)


def passed_along(array, axis, by):
    size = lax.axis_size(axis)
    pairs = [(i, i + by) for i in range(size) if 0 <= i + by < size]
    return lax.ppermute(array, axis, pairs)


def core_ring(array, d):
    size = lax.axis_size("tp")

    def moved(x, by):
        return lax.ppermute(x, ("dp", "tp"), [(d * size + (i + by) % size, d * size + i) for i in range(size)])

    half = array.shape[0] // 2
    following, previous = moved(array, 1), moved(array, -1)
    return following, previous, moved(following[:half], 1), moved(previous[half:], -1)


def per_device(
    queries, key_vectors, value_vectors, grad_output, out_weight, random_ids, random_valid, global_ids
):
    ctx_count = lax.axis_size("ctx")
    tp_count = lax.axis_size("tp")
    me = lax.axis_index("ctx")
    tp_me = lax.axis_index("tp")
    q, k, v, g_out = queries[0], key_vectors[0], value_vectors[0], grad_output[0]
    rows, width = q.shape
    blocks = rows // BLK
    requests = blocks * R
    capacity = requests // (ctx_count * 3 // 4)
    slots = ctx_count * capacity
    barrier = lax.optimization_barrier
    at = me.reshape(1)
    tp_at = jnp.stack([tp_me, lax.axis_index("dp")])
    glob_at = global_ids[0]

    def exchange(parts):
        return lax.all_to_all(parts, "ctx", split_axis=0, concat_axis=0, tiled=True)

    up, down, picked = pick_global(glob_at, at, k, v)
    before, after = shifted(up, "ctx", -1), shifted(down, "ctx", 1)
    glob = sum_four((picked, before, after, shifted(picked, "ctx", 2)))

    ids = random_ids[0].reshape(ctx_count, requests)
    owner = ids // blocks
    local = ids % blocks
    order = jnp.arange(requests, dtype=jnp.int32)
    earlier = order[None, :] < order[:, None]
    mine = owner == me
    rank = jnp.sum((mine[:, None, :] & earlier[None]).astype(jnp.int32), axis=2)
    hit = mine[:, None, :] & (rank[:, None, :] == jnp.arange(capacity, dtype=jnp.int32)[None, :, None])
    send_idx = jnp.sum(jnp.where(hit, local[:, None, :], 0), axis=2).reshape(slots)
    send_a = pick_blocks(send_idx, k, v, 0, slots)

    later = core_ring(g_out, 1)
    send_a, glob, before, after, later, g_now = barrier((send_a, glob, before, after, later, g_out))
    fetched_a = exchange(send_a.reshape(ctx_count, -1, LANES)).reshape(send_a.shape)
    pieces = (g_out, *core_ring(g_now, 0), *later)
    glob = sum_four((glob, *[shifted(glob, "ctx", 4 * by) for by in (1, 3, 2)])).reshape(G, 2, BLK, width)
    send_b = pick_blocks(send_idx, k, v, 1, slots)
    used = jnp.sum(mine.astype(jnp.int32), axis=1)
    my_owner = lax.dynamic_index_in_dim(owner, me, 0, keepdims=False)
    my_rank = jnp.sum(((my_owner[:, None] == my_owner[None, :]) & earlier).astype(jnp.int32), axis=1)
    my_slot = my_owner * capacity + my_rank
    part_size = capacity // 2
    my_part = my_rank // part_size
    my_place = (my_part * ctx_count + my_owner) * part_size + my_rank % part_size
    valid = lax.dynamic_slice_in_dim(random_valid[0], me * blocks, blocks, 0).reshape(-1)

    ready = barrier((send_b, fetched_a, pieces, glob, used, my_slot, my_place, valid))
    send_b, fetched_a, pieces, glob, used, my_slot, my_place, valid = ready
    grad_context = grad_context_of(tp_at, pieces, out_weight)

    fetched_b = exchange(send_b.reshape(ctx_count, -1, LANES)).reshape(send_b.shape)
    wcols = [None] * tp_count
    for by in range(tp_count):
        part = lax.dynamic_slice_in_dim(out_weight, (tp_me + by) % tp_count * width, width, 1)
        wcols[-by % tp_count] = shifted(part, "tp", -by) if by else part
    last_block = blocks * ctx_count - 1

    def half(to, fetched, dq_in, column):
        return attend(
            last_block, at, my_slot, to, valid, q, k, v, grad_context, before, after, glob, fetched, dq_in, column
        )

    ctx_a, dq_a, win_a, up_a, down_a, gsum_a, ret_a = half(my_slot, fetched_a, None, 0)
    near_a = ring_near(ctx_a, "tp")
    ret_a, fetched_b, wcols, near_a = barrier((ret_a, fetched_b, wcols, near_a))

    back_a = exchange(ret_a.reshape(ctx_count, -1, LANES))
    pieces_a = (ctx_a, *near_a, *ring_far(near_a, "tp"))
    up_a, down_a = passed_along(up_a, "ctx", -1), passed_along(down_a, "ctx", 1)
    ctx_b, grad_q, win_b, up_b, down_b, gsum_b, ret_b, ret_c = half(my_place, fetched_b, dq_a, 1)
    near_b = ring_near(ctx_b, "tp")
    terms = weight_terms(tp_at, (ctx_a, ctx_b), pieces)
    ret_b = load_terms(terms, (gsum_a, gsum_b), ret_b)
    ret_b, back_a, up_a, down_a, near_b = barrier((ret_b, back_a, up_a, down_a, near_b))

    back_b = exchange(ret_b)
    up_b, down_b = passed_along(up_b, "ctx", -1), passed_along(down_b, "ctx", 1)
    pieces_b = (ctx_b, *near_b, *ring_far(near_b, "tp"))
    first = collect_first(
        send_idx, used, glob_at, win_a, back_a, up_a, down_a, capacity
    )
    ret_c = load_sums(back_b, ret_c)
    ret_c, up_b, down_b, pieces_b, first = barrier((ret_c, up_b, down_b, pieces_b, first))

    back_c = exchange(ret_c)
    projected = project(pieces_a, pieces_b, wcols)
    win_b = collect_middle(send_idx, used, win_b, back_b, up_b, down_b, capacity)
    projected, win_b, back_c = barrier((projected, win_b, back_c))
    weight_own = back_c[:, : CARRIED - 32]
    grad_weight = weight_sum(weight_own, shifted(weight_own, "dp", 1))
    grad_k, grad_v = collect_last(send_idx, used, glob_at, at, win_b, back_c, first, capacity)
    return projected[None], grad_q[None], grad_k[None], grad_v[None], grad_weight


def solution(mesh):
    tokens = P("dp", "ctx", "tp")
    in_specs = (
        tokens, tokens, tokens, tokens, P("tp", None), P("dp", None, None), P("dp", None, None), P("dp", None),
    )
    out_specs = (tokens, tokens, tokens, tokens, P("tp", None))
    return jax.shard_map(per_device, mesh=mesh, in_specs=in_specs, out_specs=out_specs, check_vma=False)
```

```python
import functools

import jax
import jax.numpy as jnp
from jax import lax
from jax.experimental import pallas as pl
from jax.experimental.pallas import tpu as pltpu
from jax.sharding import PartitionSpec as P

HD = 64
BLK = 64
R = 3
G = 2
LANES = 128
NEG_FILL = -1e30
VMEM_LIMIT = 56 * 1024 * 1024
CARRIED = 160

NT = (((1,), (1,)), ((), ()))
NN = (((1,), (0,)), ((), ()))
TN = (((0,), (0,)), ((), ()))


def dot(a, b, dims):
    return lax.dot_general(a, b, dims, preferred_element_type=jnp.float32)


def smem():
    return pl.BlockSpec(memory_space=pltpu.SMEM)


def whole(shape, column=None):
    if column is None:
        return pl.BlockSpec(shape, lambda i: (0,) * len(shape))
    return pl.BlockSpec(shape, lambda i: (0,) * (len(shape) - 1) + (column,))


def params(**more):
    return pltpu.CompilerParams(vmem_limit_bytes=VMEM_LIMIT, **more)


def pick_kernel(slots, idx_ref, k_ref, v_ref, out_ref):
    def body(s, _):
        src = pl.multiple_of(idx_ref[s] * BLK, BLK)
        dst = pl.multiple_of(s * 2 * BLK, 2 * BLK)
        out_ref[pl.ds(dst, BLK), :] = k_ref[pl.ds(src, BLK), :]
        out_ref[pl.ds(dst + BLK, BLK), :] = v_ref[pl.ds(src, BLK), :]
        return 0

    lax.fori_loop(0, slots, body, 0, unroll=4)


def pick_blocks(idx, keys, values, column, slots):
    rows = keys.shape[0]
    return pl.pallas_call(
        functools.partial(pick_kernel, slots),
        grid=(1,),
        in_specs=[smem(), whole((rows, LANES), column), whole((rows, LANES), column)],
        out_specs=whole((slots * 2 * BLK, LANES)),
        out_shape=jax.ShapeDtypeStruct((slots * 2 * BLK, LANES), jnp.bfloat16),
        compiler_params=params(),
        cost_estimate=pl.CostEstimate(flops=0, bytes_accessed=10 << 20, transcendentals=0),
    )(idx, keys, values)


def pick_global_kernel(blocks, glob_ref, me_ref, k0, v0, k1, v1, k_first, v_first, k_last, v_last, up_ref, down_ref, out_ref):
    for e, pair in enumerate(((k0, v0), (k1, v1))):
        owned = glob_ref[e] // blocks == me_ref[0]
        for t, x in enumerate(pair):
            at = (e * 2 + t) * BLK
            picked = jnp.where(owned, x[...], jnp.zeros_like(x))
            for ref in (up_ref, down_ref, out_ref):
                ref[at : at + BLK, :] = picked
    at = 2 * G * BLK
    up_ref[at : at + BLK, :] = k_last[...]
    up_ref[at + BLK : at + 2 * BLK, :] = v_last[...]
    down_ref[at : at + BLK, :] = k_first[...]
    down_ref[at + BLK : at + 2 * BLK, :] = v_first[...]


def pick_global(glob, me, keys, values):
    rows, width = keys.shape
    blocks = rows // BLK

    def block(place):
        return [pl.BlockSpec((BLK, width), lambda i, glob, me: (place(glob), 0))] * 2

    specs = block(lambda glob: glob[0] % blocks) + block(lambda glob: glob[1] % blocks)
    specs += block(lambda glob: 0) + block(lambda glob: blocks - 1)
    sizes = (2 * G + 2) * BLK, (2 * G + 2) * BLK, 2 * G * BLK
    return pl.pallas_call(
        functools.partial(pick_global_kernel, blocks),
        grid_spec=pltpu.PrefetchScalarGridSpec(
            num_scalar_prefetch=2,
            grid=(1,),
            in_specs=specs,
            out_specs=tuple(pl.BlockSpec((n, width), lambda i, glob, me: (0, 0)) for n in sizes),
        ),
        out_shape=tuple(jax.ShapeDtypeStruct((n, width), jnp.bfloat16) for n in sizes),
        compiler_params=params(),
        cost_estimate=pl.CostEstimate(flops=0, bytes_accessed=1 << 19, transcendentals=0),
    )(glob, me, *[keys, values] * 4)


def sum_four_kernel(a, b, c, d, out_ref):
    out_ref[...] = a[...] + b[...] + c[...] + d[...]


def sum_four(arrays):
    shape = arrays[0].shape
    return pl.pallas_call(
        sum_four_kernel,
        grid=(1,),
        in_specs=[whole(shape)] * 4,
        out_specs=whole(shape),
        out_shape=jax.ShapeDtypeStruct(shape, jnp.bfloat16),
        compiler_params=params(),
        cost_estimate=pl.CostEstimate(flops=0, bytes_accessed=60 << 20, transcendentals=0),
    )(*arrays)


TILE = 512


def ring_specs(rows, width):
    last = rows // TILE // 2
    full = pl.BlockSpec((TILE, width), lambda i, *_: (i, 0))
    upper = pl.BlockSpec((TILE, width), lambda i, *_: (jnp.minimum(i, last - 1), 0))
    lower = pl.BlockSpec((TILE, width), lambda i, *_: (jnp.maximum(i - last, 0), 0))
    return [full, full, full, upper, lower]


def ring_values(refs):
    own, following, previous, upper, lower = refs
    top = pl.program_id(0) < pl.num_programs(0) // 2
    return own[...], following[...], jnp.where(top, upper[...], lower[...]), previous[...]


def pair_specs(rows, width):
    last = rows // TILE // 2
    specs = [pl.BlockSpec((TILE, width), lambda i, at: (i, 0))]
    for d in range(2):
        full = pl.BlockSpec((TILE, width), functools.partial(lambda d, i, at: (jnp.where(at[1] == d, i, 0), 0), d))
        upper = functools.partial(lambda d, i, at: (jnp.where(at[1] == d, jnp.minimum(i, last - 1), 0), 0), d)
        lower = functools.partial(lambda d, i, at: (jnp.where(at[1] == d, jnp.maximum(i - last, 0), 0), 0), d)
        specs += [full, full, pl.BlockSpec((TILE, width), upper), pl.BlockSpec((TILE, width), lower)]
    return specs


def pair_values(at_ref, refs):
    top = pl.program_id(0) < pl.num_programs(0) // 2
    zero = at_ref[1] == 0

    def chosen(j):
        return jnp.where(zero, refs[1 + j][...], refs[5 + j][...])

    return refs[0][...], chosen(0), jnp.where(top, chosen(2), chosen(3)), chosen(1)


def grad_context_kernel(at_ref, *refs):
    total = None
    for g, w in zip(pair_values(at_ref, refs[:9]), refs[9:13]):
        term = dot(g, w[...], NT)
        total = term if total is None else total + term
    refs[13][...] = total.astype(jnp.bfloat16)


def grad_context_of(at, pieces, weight):
    rows, width = pieces[0].shape
    heads = weight.shape[0]
    turned = [
        pl.BlockSpec((heads, width), functools.partial(lambda j, i, at: (0, (at[0] + j) % 4), j))
        for j in range(4)
    ]
    return pl.pallas_call(
        grad_context_kernel,
        grid_spec=pltpu.PrefetchScalarGridSpec(
            num_scalar_prefetch=1,
            grid=(rows // TILE,),
            in_specs=pair_specs(rows, width) + turned,
            out_specs=pl.BlockSpec((TILE, heads), lambda i, at: (i, 0)),
        ),
        out_shape=jax.ShapeDtypeStruct((rows, heads), jnp.bfloat16),
        compiler_params=params(),
        cost_estimate=pl.CostEstimate(flops=2 * rows * 1024 * heads, bytes_accessed=16 << 20, transcendentals=0),
    )(at, *pieces, weight, weight, weight, weight)


def attend_kernel(
    blocks, last_block, me_ref, slot_ref, to_ref, valid_ref, q_ref, k_ref, v_ref, g_ref, before_ref, after_ref, glob_ref,
    fetched_ref, dq_in_ref, ctx_ref, dq_ref, win_out_ref, up_ref, down_ref, gsum_out_ref, *more,
):
    del dq_in_ref
    parts_out, (kpad, vpad, win_ref, gsum_ref) = more[:-4], more[-4:]
    if len(parts_out) == 1:
        ret_ref = parts_out[0]
    else:
        *parts_out, ret_ref = parts_out
    rows = blocks * BLK
    kpad[0:BLK, :] = before_ref[0:BLK, :]
    vpad[0:BLK, :] = before_ref[BLK : 2 * BLK, :]
    kpad[rows + BLK : rows + 2 * BLK, :] = after_ref[0:BLK, :]
    vpad[rows + BLK : rows + 2 * BLK, :] = after_ref[BLK : 2 * BLK, :]
    kpad[BLK : rows + BLK, :] = k_ref[...]
    vpad[BLK : rows + BLK, :] = v_ref[...]
    win_ref[...] = jnp.zeros_like(win_ref)
    gsum_ref[...] = jnp.zeros_like(gsum_ref)
    low = lax.broadcasted_iota(jnp.int32, (BLK, LANES), 1) < HD

    def body(i, _):
        row = pl.multiple_of(i * BLK, BLK)
        q = q_ref[pl.ds(row, BLK), :] * jnp.bfloat16(0.125)
        g = g_ref[pl.ds(row, BLK), :]
        zero = jnp.zeros_like(q)
        qbd = jnp.concatenate([jnp.where(low, q, zero), jnp.where(low, zero, q)], axis=0)
        gbd = jnp.concatenate([jnp.where(low, g, zero), jnp.where(low, zero, g)], axis=0)
        starts = [pl.multiple_of(slot_ref[i * R + r] * 2 * BLK, 2 * BLK) for r in range(R)]
        kcat = jnp.concatenate(
            [kpad[pl.ds(row, 3 * BLK), :]]
            + [fetched_ref[pl.ds(s, BLK), :] for s in starts]
            + [glob_ref[0, 0], glob_ref[1, 0]],
            axis=0,
        )
        vcat = jnp.concatenate(
            [vpad[pl.ds(row, 3 * BLK), :]]
            + [fetched_ref[pl.ds(s + BLK, BLK), :] for s in starts]
            + [glob_ref[0, 1], glob_ref[1, 1]],
            axis=0,
        )
        scores = dot(kcat, qbd, NT)
        block = me_ref[0] * blocks + i
        present = [block > 0, None, block < last_block]
        present += [valid_ref[i * R + r] == 1 for r in range(R)] + [None] * G
        parts = []
        for e, there in enumerate(present):
            part = scores[e * BLK : (e + 1) * BLK]
            parts.append(part if there is None else part + jnp.where(there, 0.0, NEG_FILL))
        scores = jnp.concatenate(parts, axis=0)
        peak = jnp.max(scores, axis=0, keepdims=True)
        terms = jnp.exp(scores - peak)
        probs = terms * (1.0 / jnp.sum(terms, axis=0, keepdims=True))
        probs_low = probs.astype(jnp.bfloat16)
        grad_probs = dot(vcat, gbd, NT)
        delta = jnp.sum(probs * grad_probs, axis=0, keepdims=True)
        grad_scores = (probs * (grad_probs - delta)).astype(jnp.bfloat16)
        context = dot(probs_low, vcat, TN)
        grad_q = dot(grad_scores, kcat, TN)
        grad_k = dot(grad_scores, qbd, NN)
        grad_v = dot(probs_low, gbd, NN)
        ctx_ref[pl.ds(row, BLK), :] = jnp.where(low, context[:BLK], context[BLK:]).astype(jnp.bfloat16)
        dq_ref[pl.ds(row, BLK), :] = (
            jnp.where(low, grad_q[:BLK], grad_q[BLK:]) * 0.125
        ).astype(jnp.bfloat16)
        win_ref[0, pl.ds(row, 3 * BLK), :] += grad_k[: 3 * BLK]
        win_ref[1, pl.ds(row, 3 * BLK), :] += grad_v[: 3 * BLK]
        for r in range(R):
            part = slice((3 + r) * BLK, (4 + r) * BLK)
            to = pl.multiple_of(to_ref[i * R + r] * 2 * BLK, 2 * BLK)
            ret_ref[pl.ds(to, BLK), :] = grad_k[part].astype(jnp.bfloat16)
            ret_ref[pl.ds(to + BLK, BLK), :] = grad_v[part].astype(jnp.bfloat16)
        for e in range(G):
            part = slice((3 + R + e) * BLK, (4 + R + e) * BLK)
            gsum_ref[e, 0] += grad_k[part]
            gsum_ref[e, 1] += grad_v[part]
        return 0

    lax.fori_loop(0, blocks, body, 0, unroll=2)
    win_out_ref[...] = win_ref[:, BLK : rows + BLK, :]
    up_ref[...] = win_ref[:, 0:BLK, :].astype(jnp.bfloat16)
    down_ref[...] = win_ref[:, rows + BLK : rows + 2 * BLK, :].astype(jnp.bfloat16)
    gsum_out_ref[...] = gsum_ref[...].reshape(G * 2 * BLK, LANES).astype(jnp.bfloat16)
    if len(parts_out) > 1:
        devices, _, lanes = parts_out[0].shape
        count = ret_ref.shape[0] // 2 // devices
        for p, part_ref in enumerate(parts_out):
            for d in range(devices):
                start = (p * devices + d) * count
                part_ref[d, CARRIED : CARRIED + count, :] = ret_ref[start : start + count, :]


def attend(last_block, me, slot, to, valid, q, k, v, g, before, after, glob, fetched, dq_in, column):
    rows, width = q.shape
    blocks = rows // BLK
    half = whole((rows, LANES), column)
    first = dq_in is None
    shapes = [
        ((rows, LANES), jnp.bfloat16),
        ((rows, width), jnp.bfloat16),
        ((2, rows, LANES), jnp.float32),
        ((2, BLK, LANES), jnp.bfloat16),
        ((2, BLK, LANES), jnp.bfloat16),
        ((G * 2 * BLK, LANES), jnp.bfloat16),
    ]
    scratch = [
        pltpu.VMEM((rows + 2 * BLK, LANES), jnp.bfloat16),
        pltpu.VMEM((rows + 2 * BLK, LANES), jnp.bfloat16),
        pltpu.VMEM((2, rows + 2 * BLK, LANES), jnp.float32),
        pltpu.VMEM((G, 2, BLK, LANES), jnp.float32),
    ]
    if first:
        dq_in = jnp.zeros((16, 128), jnp.bfloat16)
        shapes.append((fetched.shape, jnp.bfloat16))
    else:
        shapes += [((16, fetched.shape[0] // 32 + CARRIED, LANES), jnp.bfloat16)] * 2
        scratch.insert(0, pltpu.VMEM(fetched.shape, jnp.bfloat16))
    specs = [whole(shape) for shape, _ in shapes]
    specs[1] = half
    return pl.pallas_call(
        functools.partial(attend_kernel, blocks, last_block),
        grid=(1,),
        in_specs=[
            smem(), smem(), smem(), smem(), half, half, half, half,
            pl.BlockSpec((2 * BLK, LANES), lambda i: (G, column)),
            pl.BlockSpec((2 * BLK, LANES), lambda i: (G, column)),
            whole((G, 2, BLK, LANES), column),
            whole(fetched.shape),
            pl.BlockSpec(memory_space=pl.ANY),
        ],
        out_specs=tuple(specs),
        out_shape=tuple(jax.ShapeDtypeStruct(*shape) for shape in shapes),
        scratch_shapes=scratch,
        input_output_aliases={} if first else {12: 1},
        compiler_params=params(),
        cost_estimate=pl.CostEstimate(
            flops=12 * blocks * 512 * 128 * 128 * 2, bytes_accessed=80 << 20, transcendentals=blocks * 512 * 128
        ),
    )(me, slot, to, valid, q, k, v, g, before, after, glob, fetched, dq_in)


def land(entries, idx_ref, used_ref, back_ref, acc):
    first, end, capacity, skipped = entries

    def body(a, _):
        @pl.when(used_ref[a] > 0)
        def _():
            for c in range(first, end):
                at = pl.multiple_of(idx_ref[a * capacity + c] * BLK, BLK)
                src = skipped + (c - first) * 2 * BLK
                acc[0, pl.ds(at, BLK), :] += back_ref[a, src : src + BLK, :].astype(jnp.float32)
                acc[1, pl.ds(at, BLK), :] += back_ref[a, src + BLK : src + 2 * BLK, :].astype(jnp.float32)

        return 0

    lax.fori_loop(0, back_ref.shape[0], body, 0)


def edges(up_ref, down_ref, acc):
    rows = acc.shape[1]
    acc[:, rows - BLK : rows, :] += up_ref[...].astype(jnp.float32)
    acc[:, 0:BLK, :] += down_ref[...].astype(jnp.float32)


def first_kernel(
    capacity, idx_ref, used_ref, glob_ref, win_ref, back_ref, up_ref, down_ref, dk_ref, dv_ref, kept_ref, acc
):
    acc[...] = win_ref[...]
    edges(up_ref, down_ref, acc)
    land((0, capacity, capacity, 0), idx_ref, used_ref, back_ref, acc)
    dk_ref[...] = acc[0].astype(jnp.bfloat16)
    dv_ref[...] = acc[1].astype(jnp.bfloat16)
    blocks = acc.shape[1] // BLK
    for e in range(G):
        at = pl.multiple_of(glob_ref[e] % blocks * BLK, BLK)
        kept_ref[e] = acc[:, pl.ds(at, BLK), :]


def middle_kernel(capacity, idx_ref, used_ref, win_ref, back_ref, up_ref, down_ref, acc):
    acc[...] = win_ref[...]
    edges(up_ref, down_ref, acc)
    land((0, capacity // 2, capacity, CARRIED), idx_ref, used_ref, back_ref, acc)


def last_kernel(
    capacity, idx_ref, used_ref, glob_ref, me_ref, win_ref, back_ref, kept_ref, dk_in_ref, dv_in_ref,
    dk_ref, dv_ref, acc,
):
    acc[...] = win_ref[...]
    land((capacity // 2, capacity, capacity, CARRIED), idx_ref, used_ref, back_ref, acc)
    blocks = acc.shape[1] // BLK
    sums = CARRIED - 32

    def total(half, e):
        found = [
            jnp.concatenate(
                [
                    back_ref[(e * 2 + t) * 4 + d, sums + half * 16 : sums + (half + 1) * 16, :].astype(jnp.float32)
                    for d in range(4)
                ]
            )
            for t in range(2)
        ]
        return jnp.stack(found)

    for e in range(G):

        @pl.when(glob_ref[e] // blocks == me_ref[0])
        def _():
            at = pl.multiple_of(glob_ref[e] % blocks * BLK, BLK)
            acc[:, pl.ds(at, BLK), :] += total(1, e)

    dk_ref[:, LANES:] = acc[0].astype(jnp.bfloat16)
    dv_ref[:, LANES:] = acc[1].astype(jnp.bfloat16)
    dk_ref[:, :LANES] = dk_in_ref[...]
    dv_ref[:, :LANES] = dv_in_ref[...]
    for e in range(G):

        @pl.when(glob_ref[e] // blocks == me_ref[0])
        def _():
            at = pl.multiple_of(glob_ref[e] % blocks * BLK, BLK)
            both = (kept_ref[e] + total(0, e)).astype(jnp.bfloat16)
            dk_ref[pl.ds(at, BLK), :LANES] = both[0]
            dv_ref[pl.ds(at, BLK), :LANES] = both[1]


def collect_first(idx, used, glob, win, back, up, down, capacity):
    rows = win.shape[1]
    out = jax.ShapeDtypeStruct((rows, LANES), jnp.bfloat16)
    kept = jax.ShapeDtypeStruct((G, 2, BLK, LANES), jnp.float32)
    return pl.pallas_call(
        functools.partial(first_kernel, capacity),
        grid=(1,),
        in_specs=[smem()] * 3 + [whole(x.shape) for x in (win, back, up, down)],
        out_specs=(whole(out.shape), whole(out.shape), whole(kept.shape)),
        out_shape=(out, out, kept),
        scratch_shapes=[pltpu.VMEM((2, rows, LANES), jnp.float32)],
        compiler_params=params(),
        cost_estimate=pl.CostEstimate(flops=4 << 20, bytes_accessed=16 << 20, transcendentals=0),
    )(idx, used, glob, win, back, up, down)


def collect_middle(idx, used, win, back, up, down, capacity):
    return pl.pallas_call(
        functools.partial(middle_kernel, capacity),
        grid=(1,),
        in_specs=[smem()] * 2 + [whole(x.shape) for x in (win, back, up, down)],
        out_specs=whole(win.shape),
        out_shape=jax.ShapeDtypeStruct(win.shape, jnp.float32),
        compiler_params=params(),
        cost_estimate=pl.CostEstimate(flops=4 << 20, bytes_accessed=14 << 20, transcendentals=0),
    )(idx, used, win, back, up, down)


def collect_last(idx, used, glob, me, win, back, before, capacity):
    rows = win.shape[1]
    out = jax.ShapeDtypeStruct((rows, 2 * LANES), jnp.bfloat16)
    dk, dv, kept = before
    arrays = (win, back, kept, dk, dv)
    return pl.pallas_call(
        functools.partial(last_kernel, capacity),
        grid=(1,),
        in_specs=[smem()] * 4 + [whole(x.shape) for x in arrays],
        out_specs=(whole(out.shape), whole(out.shape)),
        out_shape=(out, out),
        scratch_shapes=[pltpu.VMEM((2, rows, LANES), jnp.float32)],
        compiler_params=params(),
        cost_estimate=pl.CostEstimate(flops=4 << 20, bytes_accessed=12 << 20, transcendentals=0),
    )(idx, used, glob, me, *arrays)


def weight_kernel(at_ref, c0, c1, *refs):
    pieces, out_ref, acc = refs[:9], refs[9], refs[10]

    @pl.when(pl.program_id(0) == 0)
    def _():
        acc[...] = jnp.zeros_like(acc)

    width = pieces[0].shape[1]
    values = pair_values(at_ref, pieces)
    for r, c in enumerate((c0, c1)):
        for i, g in enumerate(values):
            acc[r * LANES : (r + 1) * LANES, i * width : (i + 1) * width] += dot(c[...], g, TN)

    @pl.when(pl.program_id(0) == pl.num_programs(0) - 1)
    def _():
        for i in range(4):
            to = pl.multiple_of(((at_ref[0] + i) % 4) * width, width)
            out_ref[:, pl.ds(to, width)] = acc[:, i * width : (i + 1) * width].astype(jnp.bfloat16)


def weight_terms(at, contexts, pieces):
    rows, width = pieces[0].shape
    shape = (2 * LANES, 4 * width)
    return pl.pallas_call(
        weight_kernel,
        grid_spec=pltpu.PrefetchScalarGridSpec(
            num_scalar_prefetch=1,
            grid=(rows // TILE,),
            in_specs=[pl.BlockSpec((TILE, LANES), lambda i, at: (i, 0))] * 2 + pair_specs(rows, width),
            out_specs=pl.BlockSpec(shape, lambda i, at: (0, 0)),
            scratch_shapes=[pltpu.VMEM(shape, jnp.float32)],
        ),
        out_shape=jax.ShapeDtypeStruct(shape, jnp.bfloat16),
        compiler_params=params(),
        cost_estimate=pl.CostEstimate(flops=2 * rows * 1024 * 256, bytes_accessed=16 << 20, transcendentals=0),
    )(at, *contexts, *pieces)


def carried(array):
    return whole((array.shape[0], CARRIED, LANES))


def load_kernel(terms_ref, s0, s1, part_ref, out_ref):
    del part_ref
    for d in range(out_ref.shape[0]):
        rows = slice(16 * d, 16 * (d + 1))
        for j in range(terms_ref.shape[1] // LANES):
            out_ref[d, 16 * j : 16 * (j + 1), :] = terms_ref[rows, j * LANES : (j + 1) * LANES]
        out_ref[d, CARRIED - 32 : CARRIED - 16, :] = s0[rows, :]
        out_ref[d, CARRIED - 16 :, :] = s1[rows, :]


def load_terms(terms, sums, part):
    return pl.pallas_call(
        load_kernel,
        grid=(1,),
        in_specs=[whole(x.shape) for x in (terms, *sums)] + [pl.BlockSpec(memory_space=pl.ANY)],
        out_specs=carried(part),
        out_shape=jax.ShapeDtypeStruct(part.shape, part.dtype),
        input_output_aliases={3: 0},
        compiler_params=params(),
        cost_estimate=pl.CostEstimate(flops=1 << 18, bytes_accessed=4 << 20, transcendentals=0),
    )(terms, *sums, part)


def sum_kernel(back_ref, part_ref, out_ref):
    del part_ref
    total = jnp.sum(back_ref[...].astype(jnp.float32), axis=0).astype(jnp.bfloat16)
    for d in range(out_ref.shape[0]):
        out_ref[d] = total


def load_sums(back, part):
    return pl.pallas_call(
        sum_kernel,
        grid=(1,),
        in_specs=[carried(back), pl.BlockSpec(memory_space=pl.ANY)],
        out_specs=carried(part),
        out_shape=jax.ShapeDtypeStruct(part.shape, part.dtype),
        input_output_aliases={1: 0},
        compiler_params=params(),
        cost_estimate=pl.CostEstimate(flops=1 << 18, bytes_accessed=4 << 20, transcendentals=0),
    )(back, part)


def weight_sum_kernel(own_ref, other_ref, out_ref):
    total = own_ref[...].astype(jnp.float32) + other_ref[...].astype(jnp.float32)
    for d in range(total.shape[0]):
        for j in range(out_ref.shape[1] // LANES):
            out_ref[16 * d : 16 * (d + 1), j * LANES : (j + 1) * LANES] = total[d, 16 * j : 16 * (j + 1), :]


def weight_sum(own, other):
    shape = (2 * LANES, 1024)
    return pl.pallas_call(
        weight_sum_kernel,
        grid=(1,),
        in_specs=[whole(own.shape), whole(other.shape)],
        out_specs=whole(shape),
        out_shape=jax.ShapeDtypeStruct(shape, jnp.float32),
        compiler_params=params(),
        cost_estimate=pl.CostEstimate(flops=1 << 18, bytes_accessed=2 << 20, transcendentals=0),
    )(own, other)


def project_kernel(*refs):
    weights, out_ref = [refs[10][...]] + [refs[10 + j][...] + refs[13 + j][...] for j in range(1, 4)], refs[17]
    halves = ring_values(refs[:5]), ring_values(refs[5:10])
    total = None
    for i in range(4):
        for h in range(2):
            term = dot(halves[h][i], weights[i][h * LANES : (h + 1) * LANES, :], NN)
            total = term if total is None else total + term
    out_ref[...] = total.astype(jnp.bfloat16)


def project(pieces_a, pieces_b, weights):
    rows = pieces_a[0].shape[0]
    width = weights[0].shape[1]
    return pl.pallas_call(
        project_kernel,
        grid=(rows // TILE,),
        in_specs=ring_specs(rows, LANES) * 2 + [pl.BlockSpec(w.shape, lambda i: (0, 0)) for w in weights],
        out_specs=pl.BlockSpec((TILE, width), lambda i: (i, 0)),
        out_shape=jax.ShapeDtypeStruct((rows, width), jnp.bfloat16),
        compiler_params=params(),
        cost_estimate=pl.CostEstimate(flops=2 * rows * 1024 * width, bytes_accessed=18 << 20, transcendentals=0),
    )(*pieces_a, *pieces_b, *weights)


def shifted(array, axis, by):
    size = lax.axis_size(axis)
    return lax.ppermute(array, axis, [((i + by) % size, i) for i in range(size)])


def ring_near(array, axis):
    return shifted(array, axis, 1), shifted(array, axis, -1)


def ring_far(near, axis):
    following, previous = near
    half = following.shape[0] // 2
    return shifted(following[:half], axis, 1), shifted(previous[half:], axis, -1)


def passed_along(array, axis, by):
    size = lax.axis_size(axis)
    pairs = [(i, i + by) for i in range(size) if 0 <= i + by < size]
    return lax.ppermute(array, axis, pairs)


def core_shifted(array, d, by):
    size = lax.axis_size("tp")
    return lax.ppermute(array, ("dp", "tp"), [(d * size + (i + by) % size, d * size + i) for i in range(size)])


def core_ring(array, d):
    half = array.shape[0] // 2
    following, previous = core_shifted(array, d, 1), core_shifted(array, d, -1)
    return following, previous, core_shifted(following[:half], d, 1), core_shifted(previous[half:], d, -1)


def per_device(
    queries, key_vectors, value_vectors, grad_output, out_weight, random_ids, random_valid, global_ids
):
    ctx_count = lax.axis_size("ctx")
    tp_count = lax.axis_size("tp")
    me = lax.axis_index("ctx")
    tp_me = lax.axis_index("tp")
    q, k, v, g_out = queries[0], key_vectors[0], value_vectors[0], grad_output[0]
    rows, width = q.shape
    blocks = rows // BLK
    requests = blocks * R
    capacity = requests // (ctx_count * 3 // 4)
    slots = ctx_count * capacity
    barrier = lax.optimization_barrier
    at = me.reshape(1)
    tp_at = jnp.stack([tp_me, lax.axis_index("dp")])
    glob_at = global_ids[0]

    def exchange(parts):
        return lax.all_to_all(parts, "ctx", split_axis=0, concat_axis=0, tiled=True)

    up, down, picked = pick_global(glob_at, at, k, v)
    before, after = shifted(up, "ctx", -1), shifted(down, "ctx", 1)
    across = shifted(picked, "ctx", 2)

    ids = random_ids[0].reshape(ctx_count, requests)
    owner = ids // blocks
    local = ids % blocks
    order = jnp.arange(requests, dtype=jnp.int32)
    earlier = order[None, :] < order[:, None]
    mine = owner == me
    rank = jnp.sum((mine[:, None, :] & earlier[None]).astype(jnp.int32), axis=2)
    hit = mine[:, None, :] & (rank[:, None, :] == jnp.arange(capacity, dtype=jnp.int32)[None, :, None])
    send_idx = jnp.sum(jnp.where(hit, local[:, None, :], 0), axis=2).reshape(slots)
    send_a = pick_blocks(send_idx, k, v, 0, slots)

    later = core_ring(g_out, 1)
    wparts = [lax.dynamic_slice_in_dim(out_weight, (tp_me + by) % tp_count * width, width, 1) for by in range(tp_count)]
    wparts, later = barrier((wparts, later))
    wcols_later = [core_shifted(wparts[-j % tp_count], 1, j) for j in range(1, tp_count)]
    ready = barrier((send_a, picked, across, before, after, later, wcols_later, g_out))
    send_a, picked, across, before, after, later, wcols_later, g_now = ready
    fetched_a = exchange(send_a.reshape(ctx_count, -1, LANES)).reshape(send_a.shape)
    pieces = (g_out, *core_ring(g_now, 0), *later)
    glob = sum_four((picked, before, after, across))
    glob = sum_four((glob, *[shifted(glob, "ctx", 4 * by) for by in (1, 3, 2)])).reshape(G, 2, BLK, width)
    send_b = pick_blocks(send_idx, k, v, 1, slots)
    used = jnp.sum(mine.astype(jnp.int32), axis=1)
    my_owner = lax.dynamic_index_in_dim(owner, me, 0, keepdims=False)
    my_rank = jnp.sum(((my_owner[:, None] == my_owner[None, :]) & earlier).astype(jnp.int32), axis=1)
    my_slot = my_owner * capacity + my_rank
    part_size = capacity // 2
    my_part = my_rank // part_size
    my_place = (my_part * ctx_count + my_owner) * part_size + my_rank % part_size
    valid = lax.dynamic_slice_in_dim(random_valid[0], me * blocks, blocks, 0).reshape(-1)

    ready = barrier((send_b, fetched_a, pieces, glob, used, my_slot, my_place, valid))
    send_b, fetched_a, pieces, glob, used, my_slot, my_place, valid = ready
    grad_context = grad_context_of(tp_at, pieces, out_weight)

    fetched_b = exchange(send_b.reshape(ctx_count, -1, LANES)).reshape(send_b.shape)
    wcols = [wparts[0]] + [core_shifted(wparts[-j % tp_count], 0, j) for j in range(1, tp_count)] + wcols_later
    last_block = blocks * ctx_count - 1

    def half(to, fetched, dq_in, column):
        return attend(
            last_block, at, my_slot, to, valid, q, k, v, grad_context, before, after, glob, fetched, dq_in, column
        )

    ctx_a, dq_a, win_a, up_a, down_a, gsum_a, ret_a = half(my_slot, fetched_a, None, 0)
    near_a = ring_near(ctx_a, "tp")
    ret_a, fetched_b, wcols, near_a = barrier((ret_a, fetched_b, wcols, near_a))

    back_a = exchange(ret_a.reshape(ctx_count, -1, LANES))
    pieces_a = (ctx_a, *near_a, *ring_far(near_a, "tp"))
    up_a, down_a = passed_along(up_a, "ctx", -1), passed_along(down_a, "ctx", 1)
    ctx_b, grad_q, win_b, up_b, down_b, gsum_b, ret_b, ret_c = half(my_place, fetched_b, dq_a, 1)
    near_b = ring_near(ctx_b, "tp")
    terms = weight_terms(tp_at, (ctx_a, ctx_b), pieces)
    ret_b = load_terms(terms, (gsum_a, gsum_b), ret_b)
    ret_b, back_a, up_a, down_a, near_b = barrier((ret_b, back_a, up_a, down_a, near_b))

    back_b = exchange(ret_b)
    up_b, down_b = passed_along(up_b, "ctx", -1), passed_along(down_b, "ctx", 1)
    pieces_b = (ctx_b, *near_b, *ring_far(near_b, "tp"))
    first = collect_first(
        send_idx, used, glob_at, win_a, back_a, up_a, down_a, capacity
    )
    ret_c = load_sums(back_b, ret_c)
    ret_c, up_b, down_b, pieces_b, first = barrier((ret_c, up_b, down_b, pieces_b, first))

    back_c = exchange(ret_c)
    projected = project(pieces_a, pieces_b, wcols)
    win_b = collect_middle(send_idx, used, win_b, back_b, up_b, down_b, capacity)
    projected, win_b, back_c = barrier((projected, win_b, back_c))
    weight_own = back_c[:, : CARRIED - 32]
    grad_weight = weight_sum(weight_own, shifted(weight_own, "dp", 1))
    grad_k, grad_v = collect_last(send_idx, used, glob_at, at, win_b, back_c, first, capacity)
    return projected[None], grad_q[None], grad_k[None], grad_v[None], grad_weight


def solution(mesh):
    tokens = P("dp", "ctx", "tp")
    in_specs = (
        tokens, tokens, tokens, tokens, P("tp", None), P("dp", None, None), P("dp", None, None), P("dp", None),
    )
    out_specs = (tokens, tokens, tokens, tokens, P("tp", None))
    return jax.shard_map(per_device, mesh=mesh, in_specs=in_specs, out_specs=out_specs, check_vma=False)
```

```python
import functools

import jax
import jax.numpy as jnp
from jax import lax
from jax.experimental import pallas as pl
from jax.experimental.pallas import tpu as pltpu
from jax.sharding import PartitionSpec as P

HD = 64
BLK = 64
R = 3
G = 2
LANES = 128
NEG_FILL = -1e30
VMEM_LIMIT = 56 * 1024 * 1024
CARRIED = 160

NT = (((1,), (1,)), ((), ()))
NN = (((1,), (0,)), ((), ()))
TN = (((0,), (0,)), ((), ()))


def dot(a, b, dims):
    return lax.dot_general(a, b, dims, preferred_element_type=jnp.float32)


def smem():
    return pl.BlockSpec(memory_space=pltpu.SMEM)


def whole(shape, column=None):
    if column is None:
        return pl.BlockSpec(shape, lambda i: (0,) * len(shape))
    return pl.BlockSpec(shape, lambda i: (0,) * (len(shape) - 1) + (column,))


def params(**more):
    return pltpu.CompilerParams(vmem_limit_bytes=VMEM_LIMIT, **more)


def pick_kernel(slots, idx_ref, k_ref, v_ref, out_ref):
    def body(s, _):
        src = pl.multiple_of(idx_ref[s] * BLK, BLK)
        dst = pl.multiple_of(s * 2 * BLK, 2 * BLK)
        out_ref[pl.ds(dst, BLK), :] = k_ref[pl.ds(src, BLK), :]
        out_ref[pl.ds(dst + BLK, BLK), :] = v_ref[pl.ds(src, BLK), :]
        return 0

    lax.fori_loop(0, slots, body, 0, unroll=4)


def pick_blocks(idx, keys, values, column, slots):
    rows = keys.shape[0]
    return pl.pallas_call(
        functools.partial(pick_kernel, slots),
        grid=(1,),
        in_specs=[smem(), whole((rows, LANES), column), whole((rows, LANES), column)],
        out_specs=whole((slots * 2 * BLK, LANES)),
        out_shape=jax.ShapeDtypeStruct((slots * 2 * BLK, LANES), jnp.bfloat16),
        compiler_params=params(),
        cost_estimate=pl.CostEstimate(flops=0, bytes_accessed=10 << 20, transcendentals=0),
    )(idx, keys, values)


def pick_global_kernel(blocks, glob_ref, me_ref, k0, v0, k1, v1, k_first, v_first, k_last, v_last, up_ref, down_ref, out_ref):
    for e, pair in enumerate(((k0, v0), (k1, v1))):
        owned = glob_ref[e] // blocks == me_ref[0]
        for t, x in enumerate(pair):
            at = (e * 2 + t) * BLK
            picked = jnp.where(owned, x[...], jnp.zeros_like(x))
            for ref in (up_ref, down_ref, out_ref):
                ref[at : at + BLK, :] = picked
    at = 2 * G * BLK
    up_ref[at : at + BLK, :] = k_last[...]
    up_ref[at + BLK : at + 2 * BLK, :] = v_last[...]
    down_ref[at : at + BLK, :] = k_first[...]
    down_ref[at + BLK : at + 2 * BLK, :] = v_first[...]


def pick_global(glob, me, keys, values):
    rows, width = keys.shape
    blocks = rows // BLK

    def block(place):
        return [pl.BlockSpec((BLK, width), lambda i, glob, me: (place(glob), 0))] * 2

    specs = block(lambda glob: glob[0] % blocks) + block(lambda glob: glob[1] % blocks)
    specs += block(lambda glob: 0) + block(lambda glob: blocks - 1)
    sizes = (2 * G + 2) * BLK, (2 * G + 2) * BLK, 2 * G * BLK
    return pl.pallas_call(
        functools.partial(pick_global_kernel, blocks),
        grid_spec=pltpu.PrefetchScalarGridSpec(
            num_scalar_prefetch=2,
            grid=(1,),
            in_specs=specs,
            out_specs=tuple(pl.BlockSpec((n, width), lambda i, glob, me: (0, 0)) for n in sizes),
        ),
        out_shape=tuple(jax.ShapeDtypeStruct((n, width), jnp.bfloat16) for n in sizes),
        compiler_params=params(),
        cost_estimate=pl.CostEstimate(flops=0, bytes_accessed=1 << 19, transcendentals=0),
    )(glob, me, *[keys, values] * 4)


def sum_four_kernel(a, b, c, d, out_ref):
    out_ref[...] = a[...] + b[...] + c[...] + d[...]


def sum_four(arrays):
    shape = arrays[0].shape
    return pl.pallas_call(
        sum_four_kernel,
        grid=(1,),
        in_specs=[whole(shape)] * 4,
        out_specs=whole(shape),
        out_shape=jax.ShapeDtypeStruct(shape, jnp.bfloat16),
        compiler_params=params(),
        cost_estimate=pl.CostEstimate(flops=0, bytes_accessed=60 << 20, transcendentals=0),
    )(*arrays)


TILE = 512


def ring_specs(rows, width):
    last = rows // TILE // 2
    full = pl.BlockSpec((TILE, width), lambda i, *_: (i, 0))
    upper = pl.BlockSpec((TILE, width), lambda i, *_: (jnp.minimum(i, last - 1), 0))
    lower = pl.BlockSpec((TILE, width), lambda i, *_: (jnp.maximum(i - last, 0), 0))
    return [full, full, full, upper, lower]


def ring_values(refs):
    own, following, previous, upper, lower = refs
    top = pl.program_id(0) < pl.num_programs(0) // 2
    return own[...], following[...], jnp.where(top, upper[...], lower[...]), previous[...]


def grad_context_kernel(at_ref, *refs):
    del at_ref
    total = None
    for g, w in zip(ring_values(refs[:5]), refs[5:9]):
        term = dot(g, w[...], NT)
        total = term if total is None else total + term
    refs[9][...] = total.astype(jnp.bfloat16)


def grad_context_of(at, pieces, weight):
    rows, width = pieces[0].shape
    heads = weight.shape[0]
    turned = [
        pl.BlockSpec((heads, width), functools.partial(lambda j, i, at: (0, (at[0] + j) % 4), j))
        for j in range(4)
    ]
    return pl.pallas_call(
        grad_context_kernel,
        grid_spec=pltpu.PrefetchScalarGridSpec(
            num_scalar_prefetch=1,
            grid=(rows // TILE,),
            in_specs=ring_specs(rows, width) + turned,
            out_specs=pl.BlockSpec((TILE, heads), lambda i, at: (i, 0)),
        ),
        out_shape=jax.ShapeDtypeStruct((rows, heads), jnp.bfloat16),
        compiler_params=params(),
        cost_estimate=pl.CostEstimate(flops=2 * rows * 1024 * heads, bytes_accessed=16 << 20, transcendentals=0),
    )(at, *pieces, weight, weight, weight, weight)


def attend_kernel(
    blocks, last_block, me_ref, slot_ref, to_ref, valid_ref, q_ref, k_ref, v_ref, g_ref, before_ref, after_ref, glob_ref,
    fetched_ref, dq_in_ref, ctx_ref, dq_ref, win_out_ref, up_ref, down_ref, gsum_out_ref, *more,
):
    del dq_in_ref
    parts_out, (kpad, vpad, win_ref, gsum_ref) = more[:-4], more[-4:]
    if len(parts_out) == 1:
        ret_ref = parts_out[0]
    else:
        *parts_out, ret_ref = parts_out
    rows = blocks * BLK
    kpad[0:BLK, :] = before_ref[0:BLK, :]
    vpad[0:BLK, :] = before_ref[BLK : 2 * BLK, :]
    kpad[rows + BLK : rows + 2 * BLK, :] = after_ref[0:BLK, :]
    vpad[rows + BLK : rows + 2 * BLK, :] = after_ref[BLK : 2 * BLK, :]
    kpad[BLK : rows + BLK, :] = k_ref[...]
    vpad[BLK : rows + BLK, :] = v_ref[...]
    win_ref[...] = jnp.zeros_like(win_ref)
    gsum_ref[...] = jnp.zeros_like(gsum_ref)
    low = lax.broadcasted_iota(jnp.int32, (BLK, LANES), 1) < HD

    def body(i, _):
        row = pl.multiple_of(i * BLK, BLK)
        q = q_ref[pl.ds(row, BLK), :] * jnp.bfloat16(0.125)
        g = g_ref[pl.ds(row, BLK), :]
        zero = jnp.zeros_like(q)
        qbd = jnp.concatenate([jnp.where(low, q, zero), jnp.where(low, zero, q)], axis=0)
        gbd = jnp.concatenate([jnp.where(low, g, zero), jnp.where(low, zero, g)], axis=0)
        starts = [pl.multiple_of(slot_ref[i * R + r] * 2 * BLK, 2 * BLK) for r in range(R)]
        kcat = jnp.concatenate(
            [kpad[pl.ds(row, 3 * BLK), :]]
            + [fetched_ref[pl.ds(s, BLK), :] for s in starts]
            + [glob_ref[0, 0], glob_ref[1, 0]],
            axis=0,
        )
        vcat = jnp.concatenate(
            [vpad[pl.ds(row, 3 * BLK), :]]
            + [fetched_ref[pl.ds(s + BLK, BLK), :] for s in starts]
            + [glob_ref[0, 1], glob_ref[1, 1]],
            axis=0,
        )
        scores = dot(kcat, qbd, NT)
        block = me_ref[0] * blocks + i
        present = [block > 0, None, block < last_block]
        present += [valid_ref[i * R + r] == 1 for r in range(R)] + [None] * G
        parts = []
        for e, there in enumerate(present):
            part = scores[e * BLK : (e + 1) * BLK]
            parts.append(part if there is None else part + jnp.where(there, 0.0, NEG_FILL))
        scores = jnp.concatenate(parts, axis=0)
        peak = jnp.max(scores, axis=0, keepdims=True)
        terms = jnp.exp(scores - peak)
        probs = terms * (1.0 / jnp.sum(terms, axis=0, keepdims=True))
        probs_low = probs.astype(jnp.bfloat16)
        grad_probs = dot(vcat, gbd, NT)
        delta = jnp.sum(probs * grad_probs, axis=0, keepdims=True)
        grad_scores = (probs * (grad_probs - delta)).astype(jnp.bfloat16)
        context = dot(probs_low, vcat, TN)
        grad_q = dot(grad_scores, kcat, TN)
        grad_k = dot(grad_scores, qbd, NN)
        grad_v = dot(probs_low, gbd, NN)
        ctx_ref[pl.ds(row, BLK), :] = jnp.where(low, context[:BLK], context[BLK:]).astype(jnp.bfloat16)
        dq_ref[pl.ds(row, BLK), :] = (
            jnp.where(low, grad_q[:BLK], grad_q[BLK:]) * 0.125
        ).astype(jnp.bfloat16)
        win_ref[0, pl.ds(row, 3 * BLK), :] += grad_k[: 3 * BLK]
        win_ref[1, pl.ds(row, 3 * BLK), :] += grad_v[: 3 * BLK]
        for r in range(R):
            part = slice((3 + r) * BLK, (4 + r) * BLK)
            to = pl.multiple_of(to_ref[i * R + r] * 2 * BLK, 2 * BLK)
            ret_ref[pl.ds(to, BLK), :] = grad_k[part].astype(jnp.bfloat16)
            ret_ref[pl.ds(to + BLK, BLK), :] = grad_v[part].astype(jnp.bfloat16)
        for e in range(G):
            part = slice((3 + R + e) * BLK, (4 + R + e) * BLK)
            gsum_ref[e, 0] += grad_k[part]
            gsum_ref[e, 1] += grad_v[part]
        return 0

    lax.fori_loop(0, blocks, body, 0, unroll=2)
    win_out_ref[...] = win_ref[:, BLK : rows + BLK, :]
    up_ref[...] = win_ref[:, 0:BLK, :].astype(jnp.bfloat16)
    down_ref[...] = win_ref[:, rows + BLK : rows + 2 * BLK, :].astype(jnp.bfloat16)
    gsum_out_ref[...] = gsum_ref[...].reshape(G * 2 * BLK, LANES).astype(jnp.bfloat16)
    if len(parts_out) > 1:
        devices, _, lanes = parts_out[0].shape
        count = ret_ref.shape[0] // 2 // devices
        for p, part_ref in enumerate(parts_out):
            for d in range(devices):
                start = (p * devices + d) * count
                part_ref[d, CARRIED : CARRIED + count, :] = ret_ref[start : start + count, :]


def attend(last_block, me, slot, to, valid, q, k, v, g, before, after, glob, fetched, dq_in, column):
    rows, width = q.shape
    blocks = rows // BLK
    half = whole((rows, LANES), column)
    first = dq_in is None
    shapes = [
        ((rows, LANES), jnp.bfloat16),
        ((rows, width), jnp.bfloat16),
        ((2, rows, LANES), jnp.float32),
        ((2, BLK, LANES), jnp.bfloat16),
        ((2, BLK, LANES), jnp.bfloat16),
        ((G * 2 * BLK, LANES), jnp.bfloat16),
    ]
    scratch = [
        pltpu.VMEM((rows + 2 * BLK, LANES), jnp.bfloat16),
        pltpu.VMEM((rows + 2 * BLK, LANES), jnp.bfloat16),
        pltpu.VMEM((2, rows + 2 * BLK, LANES), jnp.float32),
        pltpu.VMEM((G, 2, BLK, LANES), jnp.float32),
    ]
    if first:
        dq_in = jnp.zeros((16, 128), jnp.bfloat16)
        shapes.append((fetched.shape, jnp.bfloat16))
    else:
        shapes += [((16, fetched.shape[0] // 32 + CARRIED, LANES), jnp.bfloat16)] * 2
        scratch.insert(0, pltpu.VMEM(fetched.shape, jnp.bfloat16))
    specs = [whole(shape) for shape, _ in shapes]
    specs[1] = half
    return pl.pallas_call(
        functools.partial(attend_kernel, blocks, last_block),
        grid=(1,),
        in_specs=[
            smem(), smem(), smem(), smem(), half, half, half, half,
            pl.BlockSpec((2 * BLK, LANES), lambda i: (G, column)),
            pl.BlockSpec((2 * BLK, LANES), lambda i: (G, column)),
            whole((G, 2, BLK, LANES), column),
            whole(fetched.shape),
            pl.BlockSpec(memory_space=pl.ANY),
        ],
        out_specs=tuple(specs),
        out_shape=tuple(jax.ShapeDtypeStruct(*shape) for shape in shapes),
        scratch_shapes=scratch,
        input_output_aliases={} if first else {12: 1},
        compiler_params=params(),
        cost_estimate=pl.CostEstimate(
            flops=12 * blocks * 512 * 128 * 128 * 2, bytes_accessed=80 << 20, transcendentals=blocks * 512 * 128
        ),
    )(me, slot, to, valid, q, k, v, g, before, after, glob, fetched, dq_in)


def land(entries, idx_ref, used_ref, back_ref, acc):
    first, end, capacity, skipped = entries

    def body(a, _):
        @pl.when(used_ref[a] > 0)
        def _():
            for c in range(first, end):
                at = pl.multiple_of(idx_ref[a * capacity + c] * BLK, BLK)
                src = skipped + (c - first) * 2 * BLK
                acc[0, pl.ds(at, BLK), :] += back_ref[a, src : src + BLK, :].astype(jnp.float32)
                acc[1, pl.ds(at, BLK), :] += back_ref[a, src + BLK : src + 2 * BLK, :].astype(jnp.float32)

        return 0

    lax.fori_loop(0, back_ref.shape[0], body, 0)


def edges(up_ref, down_ref, acc):
    rows = acc.shape[1]
    acc[:, rows - BLK : rows, :] += up_ref[...].astype(jnp.float32)
    acc[:, 0:BLK, :] += down_ref[...].astype(jnp.float32)


def first_kernel(
    capacity, idx_ref, used_ref, glob_ref, win_ref, back_ref, up_ref, down_ref, dk_ref, dv_ref, kept_ref, acc
):
    acc[...] = win_ref[...]
    edges(up_ref, down_ref, acc)
    land((0, capacity, capacity, 0), idx_ref, used_ref, back_ref, acc)
    dk_ref[...] = acc[0].astype(jnp.bfloat16)
    dv_ref[...] = acc[1].astype(jnp.bfloat16)
    blocks = acc.shape[1] // BLK
    for e in range(G):
        at = pl.multiple_of(glob_ref[e] % blocks * BLK, BLK)
        kept_ref[e] = acc[:, pl.ds(at, BLK), :]


def middle_kernel(capacity, idx_ref, used_ref, win_ref, back_ref, up_ref, down_ref, acc):
    acc[...] = win_ref[...]
    edges(up_ref, down_ref, acc)
    land((0, capacity // 2, capacity, CARRIED), idx_ref, used_ref, back_ref, acc)


def last_kernel(
    capacity, idx_ref, used_ref, glob_ref, me_ref, win_ref, back_ref, kept_ref, dk_in_ref, dv_in_ref,
    dk_ref, dv_ref, gw_ref, acc,
):
    acc[...] = win_ref[...]
    land((capacity // 2, capacity, capacity, CARRIED), idx_ref, used_ref, back_ref, acc)
    blocks = acc.shape[1] // BLK
    sums = CARRIED - 32

    def total(half, e):
        found = [
            jnp.concatenate(
                [
                    back_ref[(e * 2 + t) * 4 + d, sums + half * 16 : sums + (half + 1) * 16, :].astype(jnp.float32)
                    for d in range(4)
                ]
            )
            for t in range(2)
        ]
        return jnp.stack(found)

    for e in range(G):

        @pl.when(glob_ref[e] // blocks == me_ref[0])
        def _():
            at = pl.multiple_of(glob_ref[e] % blocks * BLK, BLK)
            acc[:, pl.ds(at, BLK), :] += total(1, e)

    dk_ref[:, LANES:] = acc[0].astype(jnp.bfloat16)
    dv_ref[:, LANES:] = acc[1].astype(jnp.bfloat16)
    dk_ref[:, :LANES] = dk_in_ref[...]
    dv_ref[:, :LANES] = dv_in_ref[...]
    for e in range(G):

        @pl.when(glob_ref[e] // blocks == me_ref[0])
        def _():
            at = pl.multiple_of(glob_ref[e] % blocks * BLK, BLK)
            both = (kept_ref[e] + total(0, e)).astype(jnp.bfloat16)
            dk_ref[pl.ds(at, BLK), :LANES] = both[0]
            dv_ref[pl.ds(at, BLK), :LANES] = both[1]

    for d in range(back_ref.shape[0]):
        for j in range(gw_ref.shape[1] // LANES):
            rows = back_ref[d, 16 * j : 16 * (j + 1), :]
            gw_ref[16 * d : 16 * (d + 1), j * LANES : (j + 1) * LANES] = rows.astype(jnp.float32)


def collect_first(idx, used, glob, win, back, up, down, capacity):
    rows = win.shape[1]
    out = jax.ShapeDtypeStruct((rows, LANES), jnp.bfloat16)
    kept = jax.ShapeDtypeStruct((G, 2, BLK, LANES), jnp.float32)
    return pl.pallas_call(
        functools.partial(first_kernel, capacity),
        grid=(1,),
        in_specs=[smem()] * 3 + [whole(x.shape) for x in (win, back, up, down)],
        out_specs=(whole(out.shape), whole(out.shape), whole(kept.shape)),
        out_shape=(out, out, kept),
        scratch_shapes=[pltpu.VMEM((2, rows, LANES), jnp.float32)],
        compiler_params=params(),
        cost_estimate=pl.CostEstimate(flops=4 << 20, bytes_accessed=16 << 20, transcendentals=0),
    )(idx, used, glob, win, back, up, down)


def collect_middle(idx, used, win, back, up, down, capacity):
    return pl.pallas_call(
        functools.partial(middle_kernel, capacity),
        grid=(1,),
        in_specs=[smem()] * 2 + [whole(x.shape) for x in (win, back, up, down)],
        out_specs=whole(win.shape),
        out_shape=jax.ShapeDtypeStruct(win.shape, jnp.float32),
        compiler_params=params(),
        cost_estimate=pl.CostEstimate(flops=4 << 20, bytes_accessed=14 << 20, transcendentals=0),
    )(idx, used, win, back, up, down)


def collect_last(idx, used, glob, me, win, back, before, capacity):
    rows = win.shape[1]
    out = jax.ShapeDtypeStruct((rows, 2 * LANES), jnp.bfloat16)
    weight = jax.ShapeDtypeStruct((2 * LANES, 1024), jnp.float32)
    dk, dv, kept = before
    arrays = (win, back, kept, dk, dv)
    return pl.pallas_call(
        functools.partial(last_kernel, capacity),
        grid=(1,),
        in_specs=[smem()] * 4 + [whole(x.shape) for x in arrays],
        out_specs=(whole(out.shape), whole(out.shape), whole(weight.shape)),
        out_shape=(out, out, weight),
        scratch_shapes=[pltpu.VMEM((2, rows, LANES), jnp.float32)],
        compiler_params=params(),
        cost_estimate=pl.CostEstimate(flops=4 << 20, bytes_accessed=12 << 20, transcendentals=0),
    )(idx, used, glob, me, *arrays)


def weight_kernel(at_ref, c0, c1, *refs):
    pieces, out_ref, acc = refs[:5], refs[5], refs[6]

    @pl.when(pl.program_id(0) == 0)
    def _():
        acc[...] = jnp.zeros_like(acc)

    width = pieces[0].shape[1]
    values = ring_values(pieces)
    for r, c in enumerate((c0, c1)):
        for i, g in enumerate(values):
            acc[r * LANES : (r + 1) * LANES, i * width : (i + 1) * width] += dot(c[...], g, TN)

    @pl.when(pl.program_id(0) == pl.num_programs(0) - 1)
    def _():
        for i in range(4):
            to = pl.multiple_of(((at_ref[0] + i) % 4) * width, width)
            out_ref[:, pl.ds(to, width)] = acc[:, i * width : (i + 1) * width].astype(jnp.bfloat16)


def weight_terms(at, contexts, pieces):
    rows, width = pieces[0].shape
    shape = (2 * LANES, 4 * width)
    return pl.pallas_call(
        weight_kernel,
        grid_spec=pltpu.PrefetchScalarGridSpec(
            num_scalar_prefetch=1,
            grid=(rows // TILE,),
            in_specs=[pl.BlockSpec((TILE, LANES), lambda i, at: (i, 0))] * 2 + ring_specs(rows, width),
            out_specs=pl.BlockSpec(shape, lambda i, at: (0, 0)),
            scratch_shapes=[pltpu.VMEM(shape, jnp.float32)],
        ),
        out_shape=jax.ShapeDtypeStruct(shape, jnp.bfloat16),
        compiler_params=params(),
        cost_estimate=pl.CostEstimate(flops=2 * rows * 1024 * 256, bytes_accessed=16 << 20, transcendentals=0),
    )(at, *contexts, *pieces)


def carried(array):
    return whole((array.shape[0], CARRIED, LANES))


def load_kernel(own_ref, other_ref, s0, s1, part_ref, out_ref):
    del part_ref
    terms = (own_ref[...].astype(jnp.float32) + other_ref[...].astype(jnp.float32)).astype(jnp.bfloat16)
    for d in range(out_ref.shape[0]):
        rows = slice(16 * d, 16 * (d + 1))
        for j in range(terms.shape[1] // LANES):
            out_ref[d, 16 * j : 16 * (j + 1), :] = terms[rows, j * LANES : (j + 1) * LANES]
        out_ref[d, CARRIED - 32 : CARRIED - 16, :] = s0[rows, :]
        out_ref[d, CARRIED - 16 :, :] = s1[rows, :]


def load_terms(own, other, sums, part):
    return pl.pallas_call(
        load_kernel,
        grid=(1,),
        in_specs=[whole(x.shape) for x in (own, other, *sums)] + [pl.BlockSpec(memory_space=pl.ANY)],
        out_specs=carried(part),
        out_shape=jax.ShapeDtypeStruct(part.shape, part.dtype),
        input_output_aliases={4: 0},
        compiler_params=params(),
        cost_estimate=pl.CostEstimate(flops=1 << 18, bytes_accessed=4 << 20, transcendentals=0),
    )(own, other, *sums, part)


def sum_kernel(back_ref, part_ref, out_ref):
    del part_ref
    total = jnp.sum(back_ref[...].astype(jnp.float32), axis=0).astype(jnp.bfloat16)
    for d in range(out_ref.shape[0]):
        out_ref[d] = total


def load_sums(back, part):
    return pl.pallas_call(
        sum_kernel,
        grid=(1,),
        in_specs=[carried(back), pl.BlockSpec(memory_space=pl.ANY)],
        out_specs=carried(part),
        out_shape=jax.ShapeDtypeStruct(part.shape, part.dtype),
        input_output_aliases={1: 0},
        compiler_params=params(),
        cost_estimate=pl.CostEstimate(flops=1 << 18, bytes_accessed=4 << 20, transcendentals=0),
    )(back, part)


def project_kernel(*refs):
    weights, out_ref = refs[10:14], refs[14]
    halves = ring_values(refs[:5]), ring_values(refs[5:10])
    total = None
    for i in range(4):
        for h in range(2):
            term = dot(halves[h][i], weights[i][h * LANES : (h + 1) * LANES, :], NN)
            total = term if total is None else total + term
    out_ref[...] = total.astype(jnp.bfloat16)


def project(pieces_a, pieces_b, weights):
    rows = pieces_a[0].shape[0]
    width = weights[0].shape[1]
    return pl.pallas_call(
        project_kernel,
        grid=(rows // TILE,),
        in_specs=ring_specs(rows, LANES) * 2 + [pl.BlockSpec(w.shape, lambda i: (0, 0)) for w in weights],
        out_specs=pl.BlockSpec((TILE, width), lambda i: (i, 0)),
        out_shape=jax.ShapeDtypeStruct((rows, width), jnp.bfloat16),
        compiler_params=params(),
        cost_estimate=pl.CostEstimate(flops=2 * rows * 1024 * width, bytes_accessed=18 << 20, transcendentals=0),
    )(*pieces_a, *pieces_b, *weights)


def shifted(array, axis, by):
    size = lax.axis_size(axis)
    return lax.ppermute(array, axis, [((i + by) % size, i) for i in range(size)])


def ring_near(array, axis):
    return shifted(array, axis, 1), shifted(array, axis, -1)


def ring_far(near, axis):
    following, previous = near
    half = following.shape[0] // 2
    return shifted(following[:half], axis, 1), shifted(previous[half:], axis, -1)


def passed_along(array, axis, by):
    size = lax.axis_size(axis)
    pairs = [(i, i + by) for i in range(size) if 0 <= i + by < size]
    return lax.ppermute(array, axis, pairs)


def per_device(
    queries, key_vectors, value_vectors, grad_output, out_weight, random_ids, random_valid, global_ids
):
    ctx_count = lax.axis_size("ctx")
    tp_count = lax.axis_size("tp")
    me = lax.axis_index("ctx")
    tp_me = lax.axis_index("tp")
    q, k, v, g_out = queries[0], key_vectors[0], value_vectors[0], grad_output[0]
    rows, width = q.shape
    blocks = rows // BLK
    requests = blocks * R
    capacity = requests // (ctx_count * 3 // 4)
    slots = ctx_count * capacity
    barrier = lax.optimization_barrier
    at = me.reshape(1)
    tp_at = tp_me.reshape(1)
    glob_at = global_ids[0]

    def exchange(parts):
        return lax.all_to_all(parts, "ctx", split_axis=0, concat_axis=0, tiled=True)

    up, down, picked = pick_global(glob_at, at, k, v)
    before, after = shifted(up, "ctx", -1), shifted(down, "ctx", 1)
    across = shifted(picked, "ctx", 2)

    ids = random_ids[0].reshape(ctx_count, requests)
    owner = ids // blocks
    local = ids % blocks
    order = jnp.arange(requests, dtype=jnp.int32)
    earlier = order[None, :] < order[:, None]
    mine = owner == me
    rank = jnp.sum((mine[:, None, :] & earlier[None]).astype(jnp.int32), axis=2)
    hit = mine[:, None, :] & (rank[:, None, :] == jnp.arange(capacity, dtype=jnp.int32)[None, :, None])
    send_idx = jnp.sum(jnp.where(hit, local[:, None, :], 0), axis=2).reshape(slots)
    send_a = pick_blocks(send_idx, k, v, 0, slots)

    send_a, picked, across, before, after, g_now = barrier((send_a, picked, across, before, after, g_out))
    fetched_a = exchange(send_a.reshape(ctx_count, -1, LANES)).reshape(send_a.shape)
    near = ring_near(g_now, "tp")
    pieces = (g_out, *near, *ring_far(near, "tp"))
    glob = sum_four((picked, before, after, across))
    glob = sum_four((glob, *[shifted(glob, "ctx", 4 * by) for by in (1, 3, 2)])).reshape(G, 2, BLK, width)
    send_b = pick_blocks(send_idx, k, v, 1, slots)
    used = jnp.sum(mine.astype(jnp.int32), axis=1)
    my_owner = lax.dynamic_index_in_dim(owner, me, 0, keepdims=False)
    my_rank = jnp.sum(((my_owner[:, None] == my_owner[None, :]) & earlier).astype(jnp.int32), axis=1)
    my_slot = my_owner * capacity + my_rank
    part_size = capacity // 2
    my_part = my_rank // part_size
    my_place = (my_part * ctx_count + my_owner) * part_size + my_rank % part_size
    valid = lax.dynamic_slice_in_dim(random_valid[0], me * blocks, blocks, 0).reshape(-1)

    ready = barrier((send_b, fetched_a, pieces, glob, used, my_slot, my_place, valid))
    send_b, fetched_a, pieces, glob, used, my_slot, my_place, valid = ready
    grad_context = grad_context_of(tp_at, pieces, out_weight)

    fetched_b = exchange(send_b.reshape(ctx_count, -1, LANES)).reshape(send_b.shape)
    wcols = [None] * tp_count
    for by in range(tp_count):
        part = lax.dynamic_slice_in_dim(out_weight, (tp_me + by) % tp_count * width, width, 1)
        wcols[-by % tp_count] = shifted(part, "tp", -by) if by else part
    last_block = blocks * ctx_count - 1

    def half(to, fetched, dq_in, column):
        return attend(
            last_block, at, my_slot, to, valid, q, k, v, grad_context, before, after, glob, fetched, dq_in, column
        )

    ctx_a, dq_a, win_a, up_a, down_a, gsum_a, ret_a = half(my_slot, fetched_a, None, 0)
    near_a = ring_near(ctx_a, "tp")
    ret_a, fetched_b, wcols, near_a = barrier((ret_a, fetched_b, wcols, near_a))

    back_a = exchange(ret_a.reshape(ctx_count, -1, LANES))
    pieces_a = (ctx_a, *near_a, *ring_far(near_a, "tp"))
    up_a, down_a = passed_along(up_a, "ctx", -1), passed_along(down_a, "ctx", 1)
    ctx_b, grad_q, win_b, up_b, down_b, gsum_b, ret_b, ret_c = half(my_place, fetched_b, dq_a, 1)
    near_b = ring_near(ctx_b, "tp")
    terms = weight_terms(tp_at, (ctx_a, ctx_b), pieces)
    ret_b = load_terms(terms, shifted(terms, "dp", 1), (gsum_a, gsum_b), ret_b)
    ret_b, back_a, up_a, down_a, near_b = barrier((ret_b, back_a, up_a, down_a, near_b))

    back_b = exchange(ret_b)
    up_b, down_b = passed_along(up_b, "ctx", -1), passed_along(down_b, "ctx", 1)
    pieces_b = (ctx_b, *near_b, *ring_far(near_b, "tp"))
    first = collect_first(
        send_idx, used, glob_at, win_a, back_a, up_a, down_a, capacity
    )
    ret_c = load_sums(back_b, ret_c)
    ret_c, up_b, down_b, pieces_b, first = barrier((ret_c, up_b, down_b, pieces_b, first))

    back_c = exchange(ret_c)
    projected = project(pieces_a, pieces_b, wcols)
    win_b = collect_middle(send_idx, used, win_b, back_b, up_b, down_b, capacity)
    projected, win_b, back_c = barrier((projected, win_b, back_c))
    grad_k, grad_v, grad_weight = collect_last(send_idx, used, glob_at, at, win_b, back_c, first, capacity)
    return projected[None], grad_q[None], grad_k[None], grad_v[None], grad_weight


def solution(mesh):
    tokens = P("dp", "ctx", "tp")
    in_specs = (
        tokens, tokens, tokens, tokens, P("tp", None), P("dp", None, None), P("dp", None, None), P("dp", None),
    )
    out_specs = (tokens, tokens, tokens, tokens, P("tp", None))
    return jax.shard_map(per_device, mesh=mesh, in_specs=in_specs, out_specs=out_specs, check_vma=False)
```

```python
import functools

import jax
import jax.numpy as jnp
from jax import lax
from jax.experimental import pallas as pl
from jax.experimental.pallas import tpu as pltpu
from jax.sharding import PartitionSpec as P

HD = 64
BLK = 64
R = 3
G = 2
LANES = 128
NEG_FILL = -1e30
VMEM_LIMIT = 60 * 1024 * 1024
CARRIED = 160

NT = (((1,), (1,)), ((), ()))
NN = (((1,), (0,)), ((), ()))
TN = (((0,), (0,)), ((), ()))


def dot(a, b, dims):
    return lax.dot_general(a, b, dims, preferred_element_type=jnp.float32)


def smem():
    return pl.BlockSpec(memory_space=pltpu.SMEM)


def whole(shape, column=None):
    if column is None:
        return pl.BlockSpec(shape, lambda i: (0,) * len(shape))
    return pl.BlockSpec(shape, lambda i: (0,) * (len(shape) - 1) + (column,))


def params(**more):
    return pltpu.CompilerParams(vmem_limit_bytes=VMEM_LIMIT, **more)


def pick_kernel(slots, idx_ref, k_ref, v_ref, out_ref):
    def body(s, _):
        src = pl.multiple_of(idx_ref[s] * BLK, BLK)
        dst = pl.multiple_of(s * 2 * BLK, 2 * BLK)
        out_ref[pl.ds(dst, BLK), :] = k_ref[pl.ds(src, BLK), :]
        out_ref[pl.ds(dst + BLK, BLK), :] = v_ref[pl.ds(src, BLK), :]
        return 0

    lax.fori_loop(0, slots, body, 0, unroll=4)


def pick_blocks(idx, keys, values, column, slots):
    rows = keys.shape[0]
    return pl.pallas_call(
        functools.partial(pick_kernel, slots),
        grid=(1,),
        in_specs=[smem(), whole((rows, LANES), column), whole((rows, LANES), column)],
        out_specs=whole((slots * 2 * BLK, LANES)),
        out_shape=jax.ShapeDtypeStruct((slots * 2 * BLK, LANES), jnp.bfloat16),
        compiler_params=params(),
        cost_estimate=pl.CostEstimate(flops=0, bytes_accessed=10 << 20, transcendentals=0),
    )(idx, keys, values)


def pick_global_kernel(blocks, glob_ref, me_ref, k0, v0, k1, v1, k_first, v_first, k_last, v_last, up_ref, down_ref, out_ref):
    for e, pair in enumerate(((k0, v0), (k1, v1))):
        owned = glob_ref[e] // blocks == me_ref[0]
        for t, x in enumerate(pair):
            at = (e * 2 + t) * BLK
            picked = jnp.where(owned, x[...], jnp.zeros_like(x))
            for ref in (up_ref, down_ref, out_ref):
                ref[at : at + BLK, :] = picked
    at = 2 * G * BLK
    up_ref[at : at + BLK, :] = k_last[...]
    up_ref[at + BLK : at + 2 * BLK, :] = v_last[...]
    down_ref[at : at + BLK, :] = k_first[...]
    down_ref[at + BLK : at + 2 * BLK, :] = v_first[...]


def pick_global(glob, me, keys, values):
    rows, width = keys.shape
    blocks = rows // BLK

    def block(place):
        return [pl.BlockSpec((BLK, width), lambda i, glob, me: (place(glob), 0))] * 2

    specs = block(lambda glob: glob[0] % blocks) + block(lambda glob: glob[1] % blocks)
    specs += block(lambda glob: 0) + block(lambda glob: blocks - 1)
    sizes = (2 * G + 2) * BLK, (2 * G + 2) * BLK, 2 * G * BLK
    return pl.pallas_call(
        functools.partial(pick_global_kernel, blocks),
        grid_spec=pltpu.PrefetchScalarGridSpec(
            num_scalar_prefetch=2,
            grid=(1,),
            in_specs=specs,
            out_specs=tuple(pl.BlockSpec((n, width), lambda i, glob, me: (0, 0)) for n in sizes),
        ),
        out_shape=tuple(jax.ShapeDtypeStruct((n, width), jnp.bfloat16) for n in sizes),
        compiler_params=params(),
        cost_estimate=pl.CostEstimate(flops=0, bytes_accessed=1 << 19, transcendentals=0),
    )(glob, me, *[keys, values] * 4)


def sum_four_kernel(a, b, c, d, out_ref):
    out_ref[...] = a[...] + b[...] + c[...] + d[...]


def sum_four(arrays):
    shape = arrays[0].shape
    return pl.pallas_call(
        sum_four_kernel,
        grid=(1,),
        in_specs=[whole(shape)] * 4,
        out_specs=whole(shape),
        out_shape=jax.ShapeDtypeStruct(shape, jnp.bfloat16),
        compiler_params=params(),
        cost_estimate=pl.CostEstimate(flops=0, bytes_accessed=60 << 20, transcendentals=0),
    )(*arrays)


TILE = 512


def ring_specs(rows, width):
    last = rows // TILE // 2
    full = pl.BlockSpec((TILE, width), lambda i, *_: (i, 0))
    upper = pl.BlockSpec((TILE, width), lambda i, *_: (jnp.minimum(i, last - 1), 0))
    lower = pl.BlockSpec((TILE, width), lambda i, *_: (jnp.maximum(i - last, 0), 0))
    return [full, full, full, upper, lower]


def ring_values(refs):
    own, following, previous, upper, lower = refs
    top = pl.program_id(0) < pl.num_programs(0) // 2
    return own[...], following[...], jnp.where(top, upper[...], lower[...]), previous[...]


def grad_context_kernel(at_ref, *refs):
    del at_ref
    total = None
    for g, w in zip(ring_values(refs[:5]), refs[5:9]):
        term = dot(g, w[...], NT)
        total = term if total is None else total + term
    refs[9][...] = total.astype(jnp.bfloat16)


def grad_context_of(at, pieces, weight):
    rows, width = pieces[0].shape
    heads = weight.shape[0]
    turned = [
        pl.BlockSpec((heads, width), functools.partial(lambda j, i, at: (0, (at[0] + j) % 4), j))
        for j in range(4)
    ]
    return pl.pallas_call(
        grad_context_kernel,
        grid_spec=pltpu.PrefetchScalarGridSpec(
            num_scalar_prefetch=1,
            grid=(rows // TILE,),
            in_specs=ring_specs(rows, width) + turned,
            out_specs=pl.BlockSpec((TILE, heads), lambda i, at: (i, 0)),
        ),
        out_shape=jax.ShapeDtypeStruct((rows, heads), jnp.bfloat16),
        compiler_params=params(),
        cost_estimate=pl.CostEstimate(flops=2 * rows * 1024 * heads, bytes_accessed=16 << 20, transcendentals=0),
    )(at, *pieces, weight, weight, weight, weight)


def attend_kernel(
    blocks, last_block, me_ref, slot_ref, to_ref, valid_ref, q_ref, k_ref, v_ref, g_ref, before_ref, after_ref, glob_ref,
    fetched_ref, dq_in_ref, ctx_ref, dq_ref, win_out_ref, up_ref, down_ref, gsum_out_ref, *more,
):
    del dq_in_ref
    parts_out, (kpad, vpad, win_ref, gsum_ref) = more[:-4], more[-4:]
    if len(parts_out) == 1:
        ret_ref = parts_out[0]
    else:
        *parts_out, ret_ref = parts_out
    rows = blocks * BLK
    kpad[0:BLK, :] = before_ref[0:BLK, :]
    vpad[0:BLK, :] = before_ref[BLK : 2 * BLK, :]
    kpad[rows + BLK : rows + 2 * BLK, :] = after_ref[0:BLK, :]
    vpad[rows + BLK : rows + 2 * BLK, :] = after_ref[BLK : 2 * BLK, :]
    kpad[BLK : rows + BLK, :] = k_ref[...]
    vpad[BLK : rows + BLK, :] = v_ref[...]
    win_ref[...] = jnp.zeros_like(win_ref)
    gsum_ref[...] = jnp.zeros_like(gsum_ref)
    low = lax.broadcasted_iota(jnp.int32, (BLK, LANES), 1) < HD

    def body(i, _):
        row = pl.multiple_of(i * BLK, BLK)
        q = q_ref[pl.ds(row, BLK), :] * jnp.bfloat16(0.125)
        g = g_ref[pl.ds(row, BLK), :]
        zero = jnp.zeros_like(q)
        qbd = jnp.concatenate([jnp.where(low, q, zero), jnp.where(low, zero, q)], axis=0)
        gbd = jnp.concatenate([jnp.where(low, g, zero), jnp.where(low, zero, g)], axis=0)
        starts = [pl.multiple_of(slot_ref[i * R + r] * 2 * BLK, 2 * BLK) for r in range(R)]
        kcat = jnp.concatenate(
            [kpad[pl.ds(row, 3 * BLK), :]]
            + [fetched_ref[pl.ds(s, BLK), :] for s in starts]
            + [glob_ref[0, 0], glob_ref[1, 0]],
            axis=0,
        )
        vcat = jnp.concatenate(
            [vpad[pl.ds(row, 3 * BLK), :]]
            + [fetched_ref[pl.ds(s + BLK, BLK), :] for s in starts]
            + [glob_ref[0, 1], glob_ref[1, 1]],
            axis=0,
        )
        scores = dot(kcat, qbd, NT)
        block = me_ref[0] * blocks + i
        present = [block > 0, None, block < last_block]
        present += [valid_ref[i * R + r] == 1 for r in range(R)] + [None] * G
        parts = []
        for e, there in enumerate(present):
            part = scores[e * BLK : (e + 1) * BLK]
            parts.append(part if there is None else part + jnp.where(there, 0.0, NEG_FILL))
        scores = jnp.concatenate(parts, axis=0)
        peak = jnp.max(scores, axis=0, keepdims=True)
        terms = jnp.exp(scores - peak)
        probs = terms * (1.0 / jnp.sum(terms, axis=0, keepdims=True))
        probs_low = probs.astype(jnp.bfloat16)
        grad_probs = dot(vcat, gbd, NT)
        delta = jnp.sum(probs * grad_probs, axis=0, keepdims=True)
        grad_scores = (probs * (grad_probs - delta)).astype(jnp.bfloat16)
        context = dot(probs_low, vcat, TN)
        grad_q = dot(grad_scores, kcat, TN)
        grad_k = dot(grad_scores, qbd, NN)
        grad_v = dot(probs_low, gbd, NN)
        ctx_ref[pl.ds(row, BLK), :] = jnp.where(low, context[:BLK], context[BLK:]).astype(jnp.bfloat16)
        dq_ref[pl.ds(row, BLK), :] = (
            jnp.where(low, grad_q[:BLK], grad_q[BLK:]) * 0.125
        ).astype(jnp.bfloat16)
        win_ref[0, pl.ds(row, 3 * BLK), :] += grad_k[: 3 * BLK]
        win_ref[1, pl.ds(row, 3 * BLK), :] += grad_v[: 3 * BLK]
        for r in range(R):
            part = slice((3 + r) * BLK, (4 + r) * BLK)
            to = pl.multiple_of(to_ref[i * R + r] * 2 * BLK, 2 * BLK)
            ret_ref[pl.ds(to, BLK), :] = grad_k[part].astype(jnp.bfloat16)
            ret_ref[pl.ds(to + BLK, BLK), :] = grad_v[part].astype(jnp.bfloat16)
        for e in range(G):
            part = slice((3 + R + e) * BLK, (4 + R + e) * BLK)
            gsum_ref[e, 0] += grad_k[part]
            gsum_ref[e, 1] += grad_v[part]
        return 0

    lax.fori_loop(0, blocks, body, 0, unroll=2)
    win_out_ref[...] = win_ref[:, BLK : rows + BLK, :]
    up_ref[...] = win_ref[:, 0:BLK, :].astype(jnp.bfloat16)
    down_ref[...] = win_ref[:, rows + BLK : rows + 2 * BLK, :].astype(jnp.bfloat16)
    gsum_out_ref[...] = gsum_ref[...].reshape(G * 2 * BLK, LANES).astype(jnp.bfloat16)
    if len(parts_out) > 1:
        devices, _, lanes = parts_out[0].shape
        count = ret_ref.shape[0] // 2 // devices
        for p, part_ref in enumerate(parts_out):
            for d in range(devices):
                start = (p * devices + d) * count
                part_ref[d, CARRIED : CARRIED + count, :] = ret_ref[start : start + count, :]


def attend(last_block, me, slot, to, valid, q, k, v, g, before, after, glob, fetched, dq_in, column):
    rows, width = q.shape
    blocks = rows // BLK
    half = whole((rows, LANES), column)
    first = dq_in is None
    shapes = [
        ((rows, LANES), jnp.bfloat16),
        ((rows, width), jnp.bfloat16),
        ((2, rows, LANES), jnp.float32),
        ((2, BLK, LANES), jnp.bfloat16),
        ((2, BLK, LANES), jnp.bfloat16),
        ((G * 2 * BLK, LANES), jnp.bfloat16),
    ]
    scratch = [
        pltpu.VMEM((rows + 2 * BLK, LANES), jnp.bfloat16),
        pltpu.VMEM((rows + 2 * BLK, LANES), jnp.bfloat16),
        pltpu.VMEM((2, rows + 2 * BLK, LANES), jnp.float32),
        pltpu.VMEM((G, 2, BLK, LANES), jnp.float32),
    ]
    if first:
        dq_in = jnp.zeros((16, 128), jnp.bfloat16)
        shapes.append((fetched.shape, jnp.bfloat16))
    else:
        shapes += [((16, fetched.shape[0] // 32 + CARRIED, LANES), jnp.bfloat16)] * 2
        scratch.insert(0, pltpu.VMEM(fetched.shape, jnp.bfloat16))
    specs = [whole(shape) for shape, _ in shapes]
    specs[1] = half
    return pl.pallas_call(
        functools.partial(attend_kernel, blocks, last_block),
        grid=(1,),
        in_specs=[
            smem(), smem(), smem(), smem(), half, half, half, half,
            pl.BlockSpec((2 * BLK, LANES), lambda i: (G, column)),
            pl.BlockSpec((2 * BLK, LANES), lambda i: (G, column)),
            whole((G, 2, BLK, LANES), column),
            whole(fetched.shape),
            pl.BlockSpec(memory_space=pl.ANY),
        ],
        out_specs=tuple(specs),
        out_shape=tuple(jax.ShapeDtypeStruct(*shape) for shape in shapes),
        scratch_shapes=scratch,
        input_output_aliases={} if first else {12: 1},
        compiler_params=params(),
        cost_estimate=pl.CostEstimate(
            flops=12 * blocks * 512 * 128 * 128 * 2, bytes_accessed=80 << 20, transcendentals=blocks * 512 * 128
        ),
    )(me, slot, to, valid, q, k, v, g, before, after, glob, fetched, dq_in)


def land(entries, idx_ref, used_ref, back_ref, acc):
    first, end, capacity, skipped = entries

    def body(a, _):
        @pl.when(used_ref[a] > 0)
        def _():
            for c in range(first, end):
                at = pl.multiple_of(idx_ref[a * capacity + c] * BLK, BLK)
                src = skipped + (c - first) * 2 * BLK
                acc[0, pl.ds(at, BLK), :] += back_ref[a, src : src + BLK, :].astype(jnp.float32)
                acc[1, pl.ds(at, BLK), :] += back_ref[a, src + BLK : src + 2 * BLK, :].astype(jnp.float32)

        return 0

    lax.fori_loop(0, back_ref.shape[0], body, 0)


def edges(up_ref, down_ref, acc):
    rows = acc.shape[1]
    acc[:, rows - BLK : rows, :] += up_ref[...].astype(jnp.float32)
    acc[:, 0:BLK, :] += down_ref[...].astype(jnp.float32)


def first_kernel(
    capacity, idx_ref, used_ref, glob_ref, win_ref, back_ref, up_ref, down_ref, dk_ref, dv_ref, kept_ref, acc
):
    acc[...] = win_ref[...]
    edges(up_ref, down_ref, acc)
    land((0, capacity, capacity, 0), idx_ref, used_ref, back_ref, acc)
    dk_ref[...] = acc[0].astype(jnp.bfloat16)
    dv_ref[...] = acc[1].astype(jnp.bfloat16)
    blocks = acc.shape[1] // BLK
    for e in range(G):
        at = pl.multiple_of(glob_ref[e] % blocks * BLK, BLK)
        kept_ref[e] = acc[:, pl.ds(at, BLK), :]


def middle_kernel(capacity, idx_ref, used_ref, win_ref, back_ref, up_ref, down_ref, acc):
    acc[...] = win_ref[...]
    edges(up_ref, down_ref, acc)
    land((0, capacity // 2, capacity, CARRIED), idx_ref, used_ref, back_ref, acc)


def last_kernel(
    capacity, idx_ref, used_ref, glob_ref, me_ref, win_ref, back_ref, kept_ref, dk_in_ref, dv_in_ref,
    dk_ref, dv_ref, gw_ref, acc,
):
    acc[...] = win_ref[...]
    land((capacity // 2, capacity, capacity, CARRIED), idx_ref, used_ref, back_ref, acc)
    blocks = acc.shape[1] // BLK
    sums = CARRIED - 32

    def total(half, e):
        found = [
            jnp.concatenate(
                [
                    back_ref[(e * 2 + t) * 4 + d, sums + half * 16 : sums + (half + 1) * 16, :].astype(jnp.float32)
                    for d in range(4)
                ]
            )
            for t in range(2)
        ]
        return jnp.stack(found)

    for e in range(G):

        @pl.when(glob_ref[e] // blocks == me_ref[0])
        def _():
            at = pl.multiple_of(glob_ref[e] % blocks * BLK, BLK)
            acc[:, pl.ds(at, BLK), :] += total(1, e)

    dk_ref[:, LANES:] = acc[0].astype(jnp.bfloat16)
    dv_ref[:, LANES:] = acc[1].astype(jnp.bfloat16)
    dk_ref[:, :LANES] = dk_in_ref[...]
    dv_ref[:, :LANES] = dv_in_ref[...]
    for e in range(G):

        @pl.when(glob_ref[e] // blocks == me_ref[0])
        def _():
            at = pl.multiple_of(glob_ref[e] % blocks * BLK, BLK)
            both = (kept_ref[e] + total(0, e)).astype(jnp.bfloat16)
            dk_ref[pl.ds(at, BLK), :LANES] = both[0]
            dv_ref[pl.ds(at, BLK), :LANES] = both[1]

    for d in range(back_ref.shape[0]):
        for j in range(gw_ref.shape[1] // LANES):
            rows = back_ref[d, 16 * j : 16 * (j + 1), :]
            gw_ref[16 * d : 16 * (d + 1), j * LANES : (j + 1) * LANES] = rows.astype(jnp.float32)


def collect_first(idx, used, glob, win, back, up, down, capacity):
    rows = win.shape[1]
    out = jax.ShapeDtypeStruct((rows, LANES), jnp.bfloat16)
    kept = jax.ShapeDtypeStruct((G, 2, BLK, LANES), jnp.float32)
    return pl.pallas_call(
        functools.partial(first_kernel, capacity),
        grid=(1,),
        in_specs=[smem()] * 3 + [whole(x.shape) for x in (win, back, up, down)],
        out_specs=(whole(out.shape), whole(out.shape), whole(kept.shape)),
        out_shape=(out, out, kept),
        scratch_shapes=[pltpu.VMEM((2, rows, LANES), jnp.float32)],
        compiler_params=params(),
        cost_estimate=pl.CostEstimate(flops=4 << 20, bytes_accessed=16 << 20, transcendentals=0),
    )(idx, used, glob, win, back, up, down)


def collect_middle(idx, used, win, back, up, down, capacity):
    return pl.pallas_call(
        functools.partial(middle_kernel, capacity),
        grid=(1,),
        in_specs=[smem()] * 2 + [whole(x.shape) for x in (win, back, up, down)],
        out_specs=whole(win.shape),
        out_shape=jax.ShapeDtypeStruct(win.shape, jnp.float32),
        compiler_params=params(),
        cost_estimate=pl.CostEstimate(flops=4 << 20, bytes_accessed=14 << 20, transcendentals=0),
    )(idx, used, win, back, up, down)


def collect_last(idx, used, glob, me, win, back, before, capacity):
    rows = win.shape[1]
    out = jax.ShapeDtypeStruct((rows, 2 * LANES), jnp.bfloat16)
    weight = jax.ShapeDtypeStruct((2 * LANES, 1024), jnp.float32)
    dk, dv, kept = before
    arrays = (win, back, kept, dk, dv)
    return pl.pallas_call(
        functools.partial(last_kernel, capacity),
        grid=(1,),
        in_specs=[smem()] * 4 + [whole(x.shape) for x in arrays],
        out_specs=(whole(out.shape), whole(out.shape), whole(weight.shape)),
        out_shape=(out, out, weight),
        scratch_shapes=[pltpu.VMEM((2, rows, LANES), jnp.float32)],
        compiler_params=params(),
        cost_estimate=pl.CostEstimate(flops=4 << 20, bytes_accessed=12 << 20, transcendentals=0),
    )(idx, used, glob, me, *arrays)


def weight_kernel(at_ref, c0, c1, *refs):
    pieces, out_ref, acc = refs[:5], refs[5], refs[6]

    @pl.when(pl.program_id(0) == 0)
    def _():
        acc[...] = jnp.zeros_like(acc)

    width = pieces[0].shape[1]
    values = ring_values(pieces)
    for r, c in enumerate((c0, c1)):
        for i, g in enumerate(values):
            acc[r * LANES : (r + 1) * LANES, i * width : (i + 1) * width] += dot(c[...], g, TN)

    @pl.when(pl.program_id(0) == pl.num_programs(0) - 1)
    def _():
        for i in range(4):
            to = pl.multiple_of(((at_ref[0] + i) % 4) * width, width)
            out_ref[:, pl.ds(to, width)] = acc[:, i * width : (i + 1) * width].astype(jnp.bfloat16)


def weight_terms(at, contexts, pieces):
    rows, width = pieces[0].shape
    shape = (2 * LANES, 4 * width)
    return pl.pallas_call(
        weight_kernel,
        grid_spec=pltpu.PrefetchScalarGridSpec(
            num_scalar_prefetch=1,
            grid=(rows // TILE,),
            in_specs=[pl.BlockSpec((TILE, LANES), lambda i, at: (i, 0))] * 2 + ring_specs(rows, width),
            out_specs=pl.BlockSpec(shape, lambda i, at: (0, 0)),
            scratch_shapes=[pltpu.VMEM(shape, jnp.float32)],
        ),
        out_shape=jax.ShapeDtypeStruct(shape, jnp.bfloat16),
        compiler_params=params(),
        cost_estimate=pl.CostEstimate(flops=2 * rows * 1024 * 256, bytes_accessed=16 << 20, transcendentals=0),
    )(at, *contexts, *pieces)


def carried(array):
    return whole((array.shape[0], CARRIED, LANES))


def load_kernel(own_ref, other_ref, s0, s1, part_ref, out_ref):
    del part_ref
    terms = (own_ref[...].astype(jnp.float32) + other_ref[...].astype(jnp.float32)).astype(jnp.bfloat16)
    for d in range(out_ref.shape[0]):
        rows = slice(16 * d, 16 * (d + 1))
        for j in range(terms.shape[1] // LANES):
            out_ref[d, 16 * j : 16 * (j + 1), :] = terms[rows, j * LANES : (j + 1) * LANES]
        out_ref[d, CARRIED - 32 : CARRIED - 16, :] = s0[rows, :]
        out_ref[d, CARRIED - 16 :, :] = s1[rows, :]


def load_terms(own, other, sums, part):
    return pl.pallas_call(
        load_kernel,
        grid=(1,),
        in_specs=[whole(x.shape) for x in (own, other, *sums)] + [pl.BlockSpec(memory_space=pl.ANY)],
        out_specs=carried(part),
        out_shape=jax.ShapeDtypeStruct(part.shape, part.dtype),
        input_output_aliases={4: 0},
        compiler_params=params(),
        cost_estimate=pl.CostEstimate(flops=1 << 18, bytes_accessed=4 << 20, transcendentals=0),
    )(own, other, *sums, part)


def sum_kernel(back_ref, part_ref, out_ref):
    del part_ref
    total = jnp.sum(back_ref[...].astype(jnp.float32), axis=0).astype(jnp.bfloat16)
    for d in range(out_ref.shape[0]):
        out_ref[d] = total


def load_sums(back, part):
    return pl.pallas_call(
        sum_kernel,
        grid=(1,),
        in_specs=[carried(back), pl.BlockSpec(memory_space=pl.ANY)],
        out_specs=carried(part),
        out_shape=jax.ShapeDtypeStruct(part.shape, part.dtype),
        input_output_aliases={1: 0},
        compiler_params=params(),
        cost_estimate=pl.CostEstimate(flops=1 << 18, bytes_accessed=4 << 20, transcendentals=0),
    )(back, part)


def project_kernel(*refs):
    weights, out_ref = refs[10:14], refs[14]
    halves = ring_values(refs[:5]), ring_values(refs[5:10])
    total = None
    for i in range(4):
        for h in range(2):
            term = dot(halves[h][i], weights[i][h * LANES : (h + 1) * LANES, :], NN)
            total = term if total is None else total + term
    out_ref[...] = total.astype(jnp.bfloat16)


def project(pieces_a, pieces_b, weights):
    rows = pieces_a[0].shape[0]
    width = weights[0].shape[1]
    return pl.pallas_call(
        project_kernel,
        grid=(rows // TILE,),
        in_specs=ring_specs(rows, LANES) * 2 + [pl.BlockSpec(w.shape, lambda i: (0, 0)) for w in weights],
        out_specs=pl.BlockSpec((TILE, width), lambda i: (i, 0)),
        out_shape=jax.ShapeDtypeStruct((rows, width), jnp.bfloat16),
        compiler_params=params(),
        cost_estimate=pl.CostEstimate(flops=2 * rows * 1024 * width, bytes_accessed=18 << 20, transcendentals=0),
    )(*pieces_a, *pieces_b, *weights)


def shifted(array, axis, by):
    size = lax.axis_size(axis)
    return lax.ppermute(array, axis, [((i + by) % size, i) for i in range(size)])


def ring_near(array, axis):
    return shifted(array, axis, 1), shifted(array, axis, -1)


def ring_far(near, axis):
    following, previous = near
    half = following.shape[0] // 2
    return shifted(following[:half], axis, 1), shifted(previous[half:], axis, -1)


def passed_along(array, axis, by):
    size = lax.axis_size(axis)
    pairs = [(i, i + by) for i in range(size) if 0 <= i + by < size]
    return lax.ppermute(array, axis, pairs)


def per_device(
    queries, key_vectors, value_vectors, grad_output, out_weight, random_ids, random_valid, global_ids
):
    ctx_count = lax.axis_size("ctx")
    tp_count = lax.axis_size("tp")
    me = lax.axis_index("ctx")
    tp_me = lax.axis_index("tp")
    q, k, v, g_out = queries[0], key_vectors[0], value_vectors[0], grad_output[0]
    rows, width = q.shape
    blocks = rows // BLK
    requests = blocks * R
    capacity = requests // (ctx_count * 3 // 4)
    slots = ctx_count * capacity
    barrier = lax.optimization_barrier
    at = me.reshape(1)
    tp_at = tp_me.reshape(1)
    glob_at = global_ids[0]

    def exchange(parts):
        return lax.all_to_all(parts, "ctx", split_axis=0, concat_axis=0, tiled=True)

    up, down, picked = pick_global(glob_at, at, k, v)
    before, after = shifted(up, "ctx", -1), shifted(down, "ctx", 1)
    across = shifted(picked, "ctx", 2)

    ids = random_ids[0].reshape(ctx_count, requests)
    owner = ids // blocks
    local = ids % blocks
    order = jnp.arange(requests, dtype=jnp.int32)
    earlier = order[None, :] < order[:, None]
    mine = owner == me
    rank = jnp.sum((mine[:, None, :] & earlier[None]).astype(jnp.int32), axis=2)
    hit = mine[:, None, :] & (rank[:, None, :] == jnp.arange(capacity, dtype=jnp.int32)[None, :, None])
    send_idx = jnp.sum(jnp.where(hit, local[:, None, :], 0), axis=2).reshape(slots)
    send_a = pick_blocks(send_idx, k, v, 0, slots)

    send_a, picked, across, before, after, g_now = barrier((send_a, picked, across, before, after, g_out))
    fetched_a = exchange(send_a.reshape(ctx_count, -1, LANES)).reshape(send_a.shape)
    near = ring_near(g_now, "tp")
    glob = sum_four((picked, before, after, across))
    glob = sum_four((glob, *[shifted(glob, "ctx", 4 * by) for by in (1, 3, 2)])).reshape(G, 2, BLK, width)
    send_b = pick_blocks(send_idx, k, v, 1, slots)
    used = jnp.sum(mine.astype(jnp.int32), axis=1)
    my_owner = lax.dynamic_index_in_dim(owner, me, 0, keepdims=False)
    my_rank = jnp.sum(((my_owner[:, None] == my_owner[None, :]) & earlier).astype(jnp.int32), axis=1)
    my_slot = my_owner * capacity + my_rank
    part_size = capacity // 2
    my_part = my_rank // part_size
    my_place = (my_part * ctx_count + my_owner) * part_size + my_rank % part_size
    valid = lax.dynamic_slice_in_dim(random_valid[0], me * blocks, blocks, 0).reshape(-1)

    ready = barrier((send_b, fetched_a, near, glob, used, my_slot, my_place, valid))
    send_b, fetched_a, near, glob, used, my_slot, my_place, valid = ready
    pieces = (g_out, *near, *ring_far(near, "tp"))
    grad_context = grad_context_of(tp_at, pieces, out_weight)

    fetched_b = exchange(send_b.reshape(ctx_count, -1, LANES)).reshape(send_b.shape)
    wcols = [None] * tp_count
    for by in range(tp_count):
        part = lax.dynamic_slice_in_dim(out_weight, (tp_me + by) % tp_count * width, width, 1)
        wcols[-by % tp_count] = shifted(part, "tp", -by) if by else part
    last_block = blocks * ctx_count - 1

    def half(to, fetched, dq_in, column):
        return attend(
            last_block, at, my_slot, to, valid, q, k, v, grad_context, before, after, glob, fetched, dq_in, column
        )

    ctx_a, dq_a, win_a, up_a, down_a, gsum_a, ret_a = half(my_slot, fetched_a, None, 0)
    near_a = ring_near(ctx_a, "tp")
    ret_a, fetched_b, wcols, near_a = barrier((ret_a, fetched_b, wcols, near_a))

    back_a = exchange(ret_a.reshape(ctx_count, -1, LANES))
    pieces_a = (ctx_a, *near_a, *ring_far(near_a, "tp"))
    up_a, down_a = passed_along(up_a, "ctx", -1), passed_along(down_a, "ctx", 1)
    ctx_b, grad_q, win_b, up_b, down_b, gsum_b, ret_b, ret_c = half(my_place, fetched_b, dq_a, 1)
    near_b = ring_near(ctx_b, "tp")
    terms = weight_terms(tp_at, (ctx_a, ctx_b), pieces)
    ret_b = load_terms(terms, shifted(terms, "dp", 1), (gsum_a, gsum_b), ret_b)
    ret_b, back_a, up_a, down_a, near_b = barrier((ret_b, back_a, up_a, down_a, near_b))

    back_b = exchange(ret_b)
    up_b, down_b = passed_along(up_b, "ctx", -1), passed_along(down_b, "ctx", 1)
    pieces_b = (ctx_b, *near_b, *ring_far(near_b, "tp"))
    first = collect_first(
        send_idx, used, glob_at, win_a, back_a, up_a, down_a, capacity
    )
    ret_c = load_sums(back_b, ret_c)
    ret_c, up_b, down_b, pieces_b, first = barrier((ret_c, up_b, down_b, pieces_b, first))

    back_c = exchange(ret_c)
    projected = project(pieces_a, pieces_b, wcols)
    win_b = collect_middle(send_idx, used, win_b, back_b, up_b, down_b, capacity)
    projected, win_b, back_c = barrier((projected, win_b, back_c))
    grad_k, grad_v, grad_weight = collect_last(send_idx, used, glob_at, at, win_b, back_c, first, capacity)
    return projected[None], grad_q[None], grad_k[None], grad_v[None], grad_weight


def solution(mesh):
    tokens = P("dp", "ctx", "tp")
    in_specs = (
        tokens, tokens, tokens, tokens, P("tp", None), P("dp", None, None), P("dp", None, None), P("dp", None),
    )
    out_specs = (tokens, tokens, tokens, tokens, P("tp", None))
    return jax.shard_map(per_device, mesh=mesh, in_specs=in_specs, out_specs=out_specs, check_vma=False)
```

```python
import functools

import jax
import jax.numpy as jnp
from jax import lax
from jax.experimental import pallas as pl
from jax.experimental.pallas import tpu as pltpu
from jax.sharding import PartitionSpec as P

HD = 64
BLK = 64
R = 3
G = 2
LANES = 128
NEG_FILL = -1e30
VMEM_LIMIT = 60 * 1024 * 1024
CARRIED = 160

NT = (((1,), (1,)), ((), ()))
NN = (((1,), (0,)), ((), ()))
TN = (((0,), (0,)), ((), ()))


def dot(a, b, dims):
    return lax.dot_general(a, b, dims, preferred_element_type=jnp.float32)


def smem():
    return pl.BlockSpec(memory_space=pltpu.SMEM)


def whole(shape, column=None):
    if column is None:
        return pl.BlockSpec(shape, lambda i: (0,) * len(shape))
    return pl.BlockSpec(shape, lambda i: (0,) * (len(shape) - 1) + (column,))


def params(**more):
    return pltpu.CompilerParams(vmem_limit_bytes=VMEM_LIMIT, **more)


def pick_kernel(slots, idx_ref, k_ref, v_ref, out_ref):
    def body(s, _):
        src = pl.multiple_of(idx_ref[s] * BLK, BLK)
        dst = pl.multiple_of(s * 2 * BLK, 2 * BLK)
        out_ref[pl.ds(dst, BLK), :] = k_ref[pl.ds(src, BLK), :]
        out_ref[pl.ds(dst + BLK, BLK), :] = v_ref[pl.ds(src, BLK), :]
        return 0

    lax.fori_loop(0, slots, body, 0, unroll=4)


def pick_blocks(idx, keys, values, column, slots):
    rows = keys.shape[0]
    return pl.pallas_call(
        functools.partial(pick_kernel, slots),
        grid=(1,),
        in_specs=[smem(), whole((rows, LANES), column), whole((rows, LANES), column)],
        out_specs=whole((slots * 2 * BLK, LANES)),
        out_shape=jax.ShapeDtypeStruct((slots * 2 * BLK, LANES), jnp.bfloat16),
        compiler_params=params(),
        cost_estimate=pl.CostEstimate(flops=0, bytes_accessed=10 << 20, transcendentals=0),
    )(idx, keys, values)


def pick_global_kernel(blocks, glob_ref, me_ref, k0, v0, k1, v1, k_first, v_first, k_last, v_last, up_ref, down_ref, out_ref):
    for e, pair in enumerate(((k0, v0), (k1, v1))):
        owned = glob_ref[e] // blocks == me_ref[0]
        for t, x in enumerate(pair):
            at = (e * 2 + t) * BLK
            picked = jnp.where(owned, x[...], jnp.zeros_like(x))
            for ref in (up_ref, down_ref, out_ref):
                ref[at : at + BLK, :] = picked
    at = 2 * G * BLK
    up_ref[at : at + BLK, :] = k_last[...]
    up_ref[at + BLK : at + 2 * BLK, :] = v_last[...]
    down_ref[at : at + BLK, :] = k_first[...]
    down_ref[at + BLK : at + 2 * BLK, :] = v_first[...]


def pick_global(glob, me, keys, values):
    rows, width = keys.shape
    blocks = rows // BLK

    def block(place):
        return [pl.BlockSpec((BLK, width), lambda i, glob, me: (place(glob), 0))] * 2

    specs = block(lambda glob: glob[0] % blocks) + block(lambda glob: glob[1] % blocks)
    specs += block(lambda glob: 0) + block(lambda glob: blocks - 1)
    sizes = (2 * G + 2) * BLK, (2 * G + 2) * BLK, 2 * G * BLK
    return pl.pallas_call(
        functools.partial(pick_global_kernel, blocks),
        grid_spec=pltpu.PrefetchScalarGridSpec(
            num_scalar_prefetch=2,
            grid=(1,),
            in_specs=specs,
            out_specs=tuple(pl.BlockSpec((n, width), lambda i, glob, me: (0, 0)) for n in sizes),
        ),
        out_shape=tuple(jax.ShapeDtypeStruct((n, width), jnp.bfloat16) for n in sizes),
        compiler_params=params(),
        cost_estimate=pl.CostEstimate(flops=0, bytes_accessed=1 << 19, transcendentals=0),
    )(glob, me, *[keys, values] * 4)


def sum_four_kernel(a, b, c, d, out_ref):
    out_ref[...] = a[...] + b[...] + c[...] + d[...]


def sum_four(arrays):
    shape = arrays[0].shape
    return pl.pallas_call(
        sum_four_kernel,
        grid=(1,),
        in_specs=[whole(shape)] * 4,
        out_specs=whole(shape),
        out_shape=jax.ShapeDtypeStruct(shape, jnp.bfloat16),
        compiler_params=params(),
        cost_estimate=pl.CostEstimate(flops=0, bytes_accessed=60 << 20, transcendentals=0),
    )(*arrays)


TILE = 512


def ring_specs(rows, width):
    last = rows // TILE // 2
    full = pl.BlockSpec((TILE, width), lambda i, *_: (i, 0))
    upper = pl.BlockSpec((TILE, width), lambda i, *_: (jnp.minimum(i, last - 1), 0))
    lower = pl.BlockSpec((TILE, width), lambda i, *_: (jnp.maximum(i - last, 0), 0))
    return [full, full, full, upper, lower]


def ring_values(refs):
    own, following, previous, upper, lower = refs
    top = pl.program_id(0) < pl.num_programs(0) // 2
    return own[...], following[...], jnp.where(top, upper[...], lower[...]), previous[...]


def grad_context_kernel(at_ref, *refs):
    del at_ref
    total = None
    for g, w in zip(ring_values(refs[:5]), refs[5:9]):
        term = dot(g, w[...], NT)
        total = term if total is None else total + term
    refs[9][...] = total.astype(jnp.bfloat16)


def grad_context_of(at, pieces, weight):
    rows, width = pieces[0].shape
    heads = weight.shape[0]
    turned = [
        pl.BlockSpec((heads, width), functools.partial(lambda j, i, at: (0, (at[0] + j) % 4), j))
        for j in range(4)
    ]
    return pl.pallas_call(
        grad_context_kernel,
        grid_spec=pltpu.PrefetchScalarGridSpec(
            num_scalar_prefetch=1,
            grid=(rows // TILE,),
            in_specs=ring_specs(rows, width) + turned,
            out_specs=pl.BlockSpec((TILE, heads), lambda i, at: (i, 0)),
        ),
        out_shape=jax.ShapeDtypeStruct((rows, heads), jnp.bfloat16),
        compiler_params=params(),
        cost_estimate=pl.CostEstimate(flops=2 * rows * 1024 * heads, bytes_accessed=16 << 20, transcendentals=0),
    )(at, *pieces, weight, weight, weight, weight)


def attend_kernel(
    blocks, last_block, handed_on, me_ref, slot_ref, to_ref, valid_ref, q_ref, k_ref, v_ref, g_ref, before_ref,
    after_ref, glob_ref, fetched_ref, *more,
):
    ctx_ref, dq_ref, win_out_ref, up_ref, down_ref, gsum_out_ref, *more = more[handed_on:]
    parts_out, (kpad, vpad, win_ref, gsum_ref) = more[:-4], more[-4:]
    if len(parts_out) == 1:
        ret_ref = parts_out[0]
    else:
        *parts_out, ret_ref = parts_out
    rows = blocks * BLK
    kpad[0:BLK, :] = before_ref[0:BLK, :]
    vpad[0:BLK, :] = before_ref[BLK : 2 * BLK, :]
    kpad[rows + BLK : rows + 2 * BLK, :] = after_ref[0:BLK, :]
    vpad[rows + BLK : rows + 2 * BLK, :] = after_ref[BLK : 2 * BLK, :]
    kpad[BLK : rows + BLK, :] = k_ref[...]
    vpad[BLK : rows + BLK, :] = v_ref[...]
    win_ref[...] = jnp.zeros_like(win_ref)
    gsum_ref[...] = jnp.zeros_like(gsum_ref)
    low = lax.broadcasted_iota(jnp.int32, (BLK, LANES), 1) < HD

    def body(i, _):
        row = pl.multiple_of(i * BLK, BLK)
        q = q_ref[pl.ds(row, BLK), :] * jnp.bfloat16(0.125)
        g = g_ref[pl.ds(row, BLK), :]
        zero = jnp.zeros_like(q)
        qbd = jnp.concatenate([jnp.where(low, q, zero), jnp.where(low, zero, q)], axis=0)
        gbd = jnp.concatenate([jnp.where(low, g, zero), jnp.where(low, zero, g)], axis=0)
        starts = [pl.multiple_of(slot_ref[i * R + r] * 2 * BLK, 2 * BLK) for r in range(R)]
        kcat = jnp.concatenate(
            [kpad[pl.ds(row, 3 * BLK), :]]
            + [fetched_ref[pl.ds(s, BLK), :] for s in starts]
            + [glob_ref[0, 0], glob_ref[1, 0]],
            axis=0,
        )
        vcat = jnp.concatenate(
            [vpad[pl.ds(row, 3 * BLK), :]]
            + [fetched_ref[pl.ds(s + BLK, BLK), :] for s in starts]
            + [glob_ref[0, 1], glob_ref[1, 1]],
            axis=0,
        )
        scores = dot(kcat, qbd, NT)
        block = me_ref[0] * blocks + i
        present = [block > 0, None, block < last_block]
        present += [valid_ref[i * R + r] == 1 for r in range(R)] + [None] * G
        parts = []
        for e, there in enumerate(present):
            part = scores[e * BLK : (e + 1) * BLK]
            parts.append(part if there is None else part + jnp.where(there, 0.0, NEG_FILL))
        scores = jnp.concatenate(parts, axis=0)
        peak = jnp.max(scores, axis=0, keepdims=True)
        terms = jnp.exp(scores - peak)
        probs = terms * (1.0 / jnp.sum(terms, axis=0, keepdims=True))
        probs_low = probs.astype(jnp.bfloat16)
        grad_probs = dot(vcat, gbd, NT)
        delta = jnp.sum(probs * grad_probs, axis=0, keepdims=True)
        grad_scores = (probs * (grad_probs - delta)).astype(jnp.bfloat16)
        context = dot(probs_low, vcat, TN)
        grad_q = dot(grad_scores, kcat, TN)
        grad_k = dot(grad_scores, qbd, NN)
        grad_v = dot(probs_low, gbd, NN)
        ctx_ref[pl.ds(row, BLK), :] = jnp.where(low, context[:BLK], context[BLK:]).astype(jnp.bfloat16)
        dq_ref[pl.ds(row, BLK), :] = (
            jnp.where(low, grad_q[:BLK], grad_q[BLK:]) * 0.125
        ).astype(jnp.bfloat16)
        win_ref[0, pl.ds(row, 3 * BLK), :] += grad_k[: 3 * BLK]
        win_ref[1, pl.ds(row, 3 * BLK), :] += grad_v[: 3 * BLK]
        for r in range(R):
            part = slice((3 + r) * BLK, (4 + r) * BLK)
            to = pl.multiple_of(to_ref[i * R + r] * 2 * BLK, 2 * BLK)
            ret_ref[pl.ds(to, BLK), :] = grad_k[part].astype(jnp.bfloat16)
            ret_ref[pl.ds(to + BLK, BLK), :] = grad_v[part].astype(jnp.bfloat16)
        for e in range(G):
            part = slice((3 + R + e) * BLK, (4 + R + e) * BLK)
            gsum_ref[e, 0] += grad_k[part]
            gsum_ref[e, 1] += grad_v[part]
        return 0

    lax.fori_loop(0, blocks, body, 0, unroll=2)
    win_out_ref[...] = win_ref[:, BLK : rows + BLK, :]
    up_ref[...] = win_ref[:, 0:BLK, :].astype(jnp.bfloat16)
    down_ref[...] = win_ref[:, rows + BLK : rows + 2 * BLK, :].astype(jnp.bfloat16)
    gsum_out_ref[...] = gsum_ref[...].reshape(G * 2 * BLK, LANES).astype(jnp.bfloat16)
    if len(parts_out) > 1:
        devices, _, lanes = parts_out[0].shape
        count = ret_ref.shape[0] // 2 // devices
        for p, part_ref in enumerate(parts_out):
            for d in range(devices):
                start = (p * devices + d) * count
                part_ref[d, CARRIED : CARRIED + count, :] = ret_ref[start : start + count, :]


def attend(last_block, me, slot, to, valid, q, k, v, g, before, after, glob, fetched, handed, column):
    rows, width = q.shape
    blocks = rows // BLK
    half = whole((rows, LANES), column)
    shapes = [
        ((rows, width), jnp.bfloat16),
        ((rows, width), jnp.bfloat16),
        ((2, rows, LANES), jnp.float32),
        ((2, BLK, width), jnp.bfloat16),
        ((2, BLK, width), jnp.bfloat16),
        ((G * 2 * BLK, LANES), jnp.bfloat16),
    ]
    scratch = [
        pltpu.VMEM((rows + 2 * BLK, LANES), jnp.bfloat16),
        pltpu.VMEM((rows + 2 * BLK, LANES), jnp.bfloat16),
        pltpu.VMEM((2, rows + 2 * BLK, LANES), jnp.float32),
        pltpu.VMEM((G, 2, BLK, LANES), jnp.float32),
    ]
    if not handed:
        shapes.append((fetched.shape, jnp.bfloat16))
    else:
        shapes += [((16, fetched.shape[0] // 32 + CARRIED, LANES), jnp.bfloat16)] * 2
        scratch.insert(0, pltpu.VMEM(fetched.shape, jnp.bfloat16))
    specs = [whole(shape) for shape, _ in shapes]
    specs[0] = specs[1] = half
    specs[3] = specs[4] = whole((2, BLK, LANES), column)
    return pl.pallas_call(
        functools.partial(attend_kernel, blocks, last_block, len(handed)),
        grid=(1,),
        in_specs=[
            smem(), smem(), smem(), smem(), half, half, half, half,
            pl.BlockSpec((2 * BLK, LANES), lambda i: (G, column)),
            pl.BlockSpec((2 * BLK, LANES), lambda i: (G, column)),
            whole((G, 2, BLK, LANES), column),
            whole(fetched.shape),
        ]
        + [pl.BlockSpec(memory_space=pl.ANY)] * len(handed),
        out_specs=tuple(specs),
        out_shape=tuple(jax.ShapeDtypeStruct(*shape) for shape in shapes),
        scratch_shapes=scratch,
        input_output_aliases={12: 0, 13: 1, 14: 3, 15: 4} if handed else {},
        compiler_params=params(),
        cost_estimate=pl.CostEstimate(
            flops=12 * blocks * 512 * 128 * 128 * 2, bytes_accessed=80 << 20, transcendentals=blocks * 512 * 128
        ),
    )(me, slot, to, valid, q, k, v, g, before, after, glob, fetched, *handed)


def land(entries, idx_ref, used_ref, back_ref, acc):
    first, end, capacity, skipped = entries

    def body(a, _):
        @pl.when(used_ref[a] > 0)
        def _():
            for c in range(first, end):
                at = pl.multiple_of(idx_ref[a * capacity + c] * BLK, BLK)
                src = skipped + (c - first) * 2 * BLK
                acc[0, pl.ds(at, BLK), :] += back_ref[a, src : src + BLK, :].astype(jnp.float32)
                acc[1, pl.ds(at, BLK), :] += back_ref[a, src + BLK : src + 2 * BLK, :].astype(jnp.float32)

        return 0

    lax.fori_loop(0, back_ref.shape[0], body, 0)


def edges(up_ref, down_ref, acc):
    rows = acc.shape[1]
    acc[:, rows - BLK : rows, :] += up_ref[...].astype(jnp.float32)
    acc[:, 0:BLK, :] += down_ref[...].astype(jnp.float32)


def first_kernel(
    capacity, idx_ref, used_ref, glob_ref, win_ref, back_ref, up_ref, down_ref, dk_ref, dv_ref, kept_ref, acc
):
    acc[...] = win_ref[...]
    edges(up_ref, down_ref, acc)
    land((0, capacity, capacity, 0), idx_ref, used_ref, back_ref, acc)
    dk_ref[...] = acc[0].astype(jnp.bfloat16)
    dv_ref[...] = acc[1].astype(jnp.bfloat16)
    blocks = acc.shape[1] // BLK
    for e in range(G):
        at = pl.multiple_of(glob_ref[e] % blocks * BLK, BLK)
        kept_ref[e] = acc[:, pl.ds(at, BLK), :]


def middle_kernel(capacity, idx_ref, used_ref, win_ref, back_ref, up_ref, down_ref, acc):
    acc[...] = win_ref[...]
    edges(up_ref, down_ref, acc)
    land((0, capacity // 2, capacity, CARRIED), idx_ref, used_ref, back_ref, acc)


def last_kernel(
    capacity, idx_ref, used_ref, glob_ref, me_ref, win_ref, back_ref, kept_ref, dk_in_ref, dv_in_ref,
    dk_ref, dv_ref, gw_ref, acc,
):
    acc[...] = win_ref[...]
    land((capacity // 2, capacity, capacity, CARRIED), idx_ref, used_ref, back_ref, acc)
    blocks = acc.shape[1] // BLK
    sums = CARRIED - 32

    def total(half, e):
        found = [
            jnp.concatenate(
                [
                    back_ref[(e * 2 + t) * 4 + d, sums + half * 16 : sums + (half + 1) * 16, :].astype(jnp.float32)
                    for d in range(4)
                ]
            )
            for t in range(2)
        ]
        return jnp.stack(found)

    for e in range(G):

        @pl.when(glob_ref[e] // blocks == me_ref[0])
        def _():
            at = pl.multiple_of(glob_ref[e] % blocks * BLK, BLK)
            acc[:, pl.ds(at, BLK), :] += total(1, e)

    dk_ref[:, LANES:] = acc[0].astype(jnp.bfloat16)
    dv_ref[:, LANES:] = acc[1].astype(jnp.bfloat16)
    dk_ref[:, :LANES] = dk_in_ref[...]
    dv_ref[:, :LANES] = dv_in_ref[...]
    for e in range(G):

        @pl.when(glob_ref[e] // blocks == me_ref[0])
        def _():
            at = pl.multiple_of(glob_ref[e] % blocks * BLK, BLK)
            both = (kept_ref[e] + total(0, e)).astype(jnp.bfloat16)
            dk_ref[pl.ds(at, BLK), :LANES] = both[0]
            dv_ref[pl.ds(at, BLK), :LANES] = both[1]

    for d in range(back_ref.shape[0]):
        for j in range(gw_ref.shape[1] // LANES):
            rows = back_ref[d, 16 * j : 16 * (j + 1), :]
            gw_ref[16 * d : 16 * (d + 1), j * LANES : (j + 1) * LANES] = rows.astype(jnp.float32)


def collect_first(idx, used, glob, win, back, up, down, capacity):
    rows = win.shape[1]
    out = jax.ShapeDtypeStruct((rows, LANES), jnp.bfloat16)
    kept = jax.ShapeDtypeStruct((G, 2, BLK, LANES), jnp.float32)
    return pl.pallas_call(
        functools.partial(first_kernel, capacity),
        grid=(1,),
        in_specs=[smem()] * 3 + [whole(x.shape) for x in (win, back)] + [whole((2, BLK, LANES), 0)] * 2,
        out_specs=(whole(out.shape), whole(out.shape), whole(kept.shape)),
        out_shape=(out, out, kept),
        scratch_shapes=[pltpu.VMEM((2, rows, LANES), jnp.float32)],
        compiler_params=params(),
        cost_estimate=pl.CostEstimate(flops=4 << 20, bytes_accessed=16 << 20, transcendentals=0),
    )(idx, used, glob, win, back, up, down)


def collect_middle(idx, used, win, back, up, down, capacity):
    return pl.pallas_call(
        functools.partial(middle_kernel, capacity),
        grid=(1,),
        in_specs=[smem()] * 2 + [whole(x.shape) for x in (win, back)] + [whole((2, BLK, LANES), 1)] * 2,
        out_specs=whole(win.shape),
        out_shape=jax.ShapeDtypeStruct(win.shape, jnp.float32),
        compiler_params=params(),
        cost_estimate=pl.CostEstimate(flops=4 << 20, bytes_accessed=14 << 20, transcendentals=0),
    )(idx, used, win, back, up, down)


def collect_last(idx, used, glob, me, win, back, before, capacity):
    rows = win.shape[1]
    out = jax.ShapeDtypeStruct((rows, 2 * LANES), jnp.bfloat16)
    weight = jax.ShapeDtypeStruct((2 * LANES, 1024), jnp.float32)
    dk, dv, kept = before
    arrays = (win, back, kept, dk, dv)
    return pl.pallas_call(
        functools.partial(last_kernel, capacity),
        grid=(1,),
        in_specs=[smem()] * 4 + [whole(x.shape) for x in arrays],
        out_specs=(whole(out.shape), whole(out.shape), whole(weight.shape)),
        out_shape=(out, out, weight),
        scratch_shapes=[pltpu.VMEM((2, rows, LANES), jnp.float32)],
        compiler_params=params(),
        cost_estimate=pl.CostEstimate(flops=4 << 20, bytes_accessed=12 << 20, transcendentals=0),
    )(idx, used, glob, me, *arrays)


def weight_kernel(at_ref, c_ref, *refs):
    pieces, out_ref, acc = refs[:5], refs[5], refs[6]

    @pl.when(pl.program_id(0) == 0)
    def _():
        acc[...] = jnp.zeros_like(acc)

    width = pieces[0].shape[1]
    values = ring_values(pieces)
    for i, g in enumerate(values):
        acc[:, i * width : (i + 1) * width] += dot(c_ref[...], g, TN)

    @pl.when(pl.program_id(0) == pl.num_programs(0) - 1)
    def _():
        for i in range(4):
            to = pl.multiple_of(((at_ref[0] + i) % 4) * width, width)
            out_ref[:, pl.ds(to, width)] = acc[:, i * width : (i + 1) * width].astype(jnp.bfloat16)


def weight_terms(at, context, pieces):
    rows, width = pieces[0].shape
    shape = (2 * LANES, 4 * width)
    return pl.pallas_call(
        weight_kernel,
        grid_spec=pltpu.PrefetchScalarGridSpec(
            num_scalar_prefetch=1,
            grid=(rows // TILE,),
            in_specs=[pl.BlockSpec((TILE, width), lambda i, at: (i, 0))] + ring_specs(rows, width),
            out_specs=pl.BlockSpec(shape, lambda i, at: (0, 0)),
            scratch_shapes=[pltpu.VMEM(shape, jnp.float32)],
        ),
        out_shape=jax.ShapeDtypeStruct(shape, jnp.bfloat16),
        compiler_params=params(),
        cost_estimate=pl.CostEstimate(flops=2 * rows * 1024 * 256, bytes_accessed=16 << 20, transcendentals=0),
    )(at, context, *pieces)


def carried(array):
    return whole((array.shape[0], CARRIED, LANES))


def load_kernel(own_ref, other_ref, s0, s1, part_ref, out_ref):
    del part_ref
    terms = (own_ref[...].astype(jnp.float32) + other_ref[...].astype(jnp.float32)).astype(jnp.bfloat16)
    for d in range(out_ref.shape[0]):
        rows = slice(16 * d, 16 * (d + 1))
        for j in range(terms.shape[1] // LANES):
            out_ref[d, 16 * j : 16 * (j + 1), :] = terms[rows, j * LANES : (j + 1) * LANES]
        out_ref[d, CARRIED - 32 : CARRIED - 16, :] = s0[rows, :]
        out_ref[d, CARRIED - 16 :, :] = s1[rows, :]


def load_terms(own, other, sums, part):
    return pl.pallas_call(
        load_kernel,
        grid=(1,),
        in_specs=[whole(x.shape) for x in (own, other, *sums)] + [pl.BlockSpec(memory_space=pl.ANY)],
        out_specs=carried(part),
        out_shape=jax.ShapeDtypeStruct(part.shape, part.dtype),
        input_output_aliases={4: 0},
        compiler_params=params(),
        cost_estimate=pl.CostEstimate(flops=1 << 18, bytes_accessed=4 << 20, transcendentals=0),
    )(own, other, *sums, part)


def sum_kernel(back_ref, part_ref, out_ref):
    del part_ref
    total = jnp.sum(back_ref[...].astype(jnp.float32), axis=0).astype(jnp.bfloat16)
    for d in range(out_ref.shape[0]):
        out_ref[d] = total


def load_sums(back, part):
    return pl.pallas_call(
        sum_kernel,
        grid=(1,),
        in_specs=[carried(back), pl.BlockSpec(memory_space=pl.ANY)],
        out_specs=carried(part),
        out_shape=jax.ShapeDtypeStruct(part.shape, part.dtype),
        input_output_aliases={1: 0},
        compiler_params=params(),
        cost_estimate=pl.CostEstimate(flops=1 << 18, bytes_accessed=4 << 20, transcendentals=0),
    )(back, part)


def project_kernel(*refs):
    total = None
    for c, w in zip(ring_values(refs[:5]), refs[5:9]):
        term = dot(c, w[...], NN)
        total = term if total is None else total + term
    refs[9][...] = total.astype(jnp.bfloat16)


def project(pieces, weights):
    rows, width = pieces[0].shape
    return pl.pallas_call(
        project_kernel,
        grid=(rows // TILE,),
        in_specs=ring_specs(rows, width) + [pl.BlockSpec(w.shape, lambda i: (0, 0)) for w in weights],
        out_specs=pl.BlockSpec((TILE, width), lambda i: (i, 0)),
        out_shape=jax.ShapeDtypeStruct((rows, width), jnp.bfloat16),
        compiler_params=params(),
        cost_estimate=pl.CostEstimate(flops=2 * rows * 1024 * width, bytes_accessed=18 << 20, transcendentals=0),
    )(*pieces, *weights)


def shifted(array, axis, by):
    size = lax.axis_size(axis)
    return lax.ppermute(array, axis, [((i + by) % size, i) for i in range(size)])


def ring_near(array, axis):
    return shifted(array, axis, 1), shifted(array, axis, -1)


def ring_far(near, axis):
    following, previous = near
    half = following.shape[0] // 2
    return shifted(following[:half], axis, 1), shifted(previous[half:], axis, -1)


def passed_along(array, axis, by):
    size = lax.axis_size(axis)
    pairs = [(i, i + by) for i in range(size) if 0 <= i + by < size]
    return lax.ppermute(array, axis, pairs)


def per_device(
    queries, key_vectors, value_vectors, grad_output, out_weight, random_ids, random_valid, global_ids
):
    ctx_count = lax.axis_size("ctx")
    tp_count = lax.axis_size("tp")
    me = lax.axis_index("ctx")
    tp_me = lax.axis_index("tp")
    q, k, v, g_out = queries[0], key_vectors[0], value_vectors[0], grad_output[0]
    rows, width = q.shape
    blocks = rows // BLK
    requests = blocks * R
    capacity = requests // (ctx_count * 3 // 4)
    slots = ctx_count * capacity
    barrier = lax.optimization_barrier
    at = me.reshape(1)
    tp_at = tp_me.reshape(1)
    glob_at = global_ids[0]

    def exchange(parts):
        return lax.all_to_all(parts, "ctx", split_axis=0, concat_axis=0, tiled=True)

    up, down, picked = pick_global(glob_at, at, k, v)
    before, after = shifted(up, "ctx", -1), shifted(down, "ctx", 1)
    across = shifted(picked, "ctx", 2)

    ids = random_ids[0].reshape(ctx_count, requests)
    owner = ids // blocks
    local = ids % blocks
    order = jnp.arange(requests, dtype=jnp.int32)
    earlier = order[None, :] < order[:, None]
    mine = owner == me
    rank = jnp.sum((mine[:, None, :] & earlier[None]).astype(jnp.int32), axis=2)
    hit = mine[:, None, :] & (rank[:, None, :] == jnp.arange(capacity, dtype=jnp.int32)[None, :, None])
    send_idx = jnp.sum(jnp.where(hit, local[:, None, :], 0), axis=2).reshape(slots)
    send_a = pick_blocks(send_idx, k, v, 0, slots)

    send_a, picked, across, before, after, g_now = barrier((send_a, picked, across, before, after, g_out))
    fetched_a = exchange(send_a.reshape(ctx_count, -1, LANES)).reshape(send_a.shape)
    near = ring_near(g_now, "tp")
    glob = sum_four((picked, before, after, across))
    glob = sum_four((glob, *[shifted(glob, "ctx", 4 * by) for by in (1, 3, 2)])).reshape(G, 2, BLK, width)
    send_b = pick_blocks(send_idx, k, v, 1, slots)
    used = jnp.sum(mine.astype(jnp.int32), axis=1)
    my_owner = lax.dynamic_index_in_dim(owner, me, 0, keepdims=False)
    my_rank = jnp.sum(((my_owner[:, None] == my_owner[None, :]) & earlier).astype(jnp.int32), axis=1)
    my_slot = my_owner * capacity + my_rank
    part_size = capacity // 2
    my_part = my_rank // part_size
    my_place = (my_part * ctx_count + my_owner) * part_size + my_rank % part_size
    valid = lax.dynamic_slice_in_dim(random_valid[0], me * blocks, blocks, 0).reshape(-1)

    ready = barrier((send_b, fetched_a, near, glob, used, my_slot, my_place, valid))
    send_b, fetched_a, near, glob, used, my_slot, my_place, valid = ready
    pieces = (g_out, *near, *ring_far(near, "tp"))
    grad_context = grad_context_of(tp_at, pieces, out_weight)

    fetched_b = exchange(send_b.reshape(ctx_count, -1, LANES)).reshape(send_b.shape)
    last_block = blocks * ctx_count - 1

    def half(to, fetched, handed, column):
        return attend(
            last_block, at, my_slot, to, valid, q, k, v, grad_context, before, after, glob, fetched, handed, column
        )

    context, grad_q, win_a, up, down, gsum_a, ret_a = half(my_slot, fetched_a, (), 0)
    ret_a, fetched_b = barrier((ret_a, fetched_b))

    back_a = exchange(ret_a.reshape(ctx_count, -1, LANES))
    context, grad_q, win_b, up, down, gsum_b, ret_b, ret_c = half(my_place, fetched_b, (context, grad_q, up, down), 1)
    terms = weight_terms(tp_at, context, pieces)
    ret_b = load_terms(terms, shifted(terms, "dp", 1), (gsum_a, gsum_b), ret_b)
    ret_b, back_a = barrier((ret_b, back_a))

    back_b = exchange(ret_b)
    near = ring_near(context, "tp")
    up, down = passed_along(up, "ctx", -1), passed_along(down, "ctx", 1)
    ret_c = load_sums(back_b, ret_c)
    ret_c, up, down, near, w_now = barrier((ret_c, up, down, near, out_weight))

    back_c = exchange(ret_c)
    first = collect_first(send_idx, used, glob_at, win_a, back_a, up, down, capacity)
    win_b = collect_middle(send_idx, used, win_b, back_b, up, down, capacity)
    wcols = [None] * tp_count
    for by in range(tp_count):
        part = lax.dynamic_slice_in_dim(w_now, (tp_me + by) % tp_count * width, width, 1)
        wcols[-by % tp_count] = shifted(part, "tp", -by) if by else part
    projected = project((context, *near, *ring_far(near, "tp")), wcols)
    projected, win_b, first, back_c = barrier((projected, win_b, first, back_c))
    grad_k, grad_v, grad_weight = collect_last(send_idx, used, glob_at, at, win_b, back_c, first, capacity)
    return projected[None], grad_q[None], grad_k[None], grad_v[None], grad_weight


def solution(mesh):
    tokens = P("dp", "ctx", "tp")
    in_specs = (
        tokens, tokens, tokens, tokens, P("tp", None), P("dp", None, None), P("dp", None, None), P("dp", None),
    )
    out_specs = (tokens, tokens, tokens, tokens, P("tp", None))
    return jax.shard_map(per_device, mesh=mesh, in_specs=in_specs, out_specs=out_specs, check_vma=False)
```

```python
import functools

import jax
import jax.numpy as jnp
from jax import lax
from jax.experimental import pallas as pl
from jax.experimental.pallas import tpu as pltpu
from jax.sharding import PartitionSpec as P

HD = 64
BLK = 64
R = 3
G = 2
LANES = 128
NEG_FILL = -1e30
VMEM_LIMIT = 60 * 1024 * 1024
CARRIED = 160

NT = (((1,), (1,)), ((), ()))
NN = (((1,), (0,)), ((), ()))
TN = (((0,), (0,)), ((), ()))


def dot(a, b, dims):
    return lax.dot_general(a, b, dims, preferred_element_type=jnp.float32)


def smem():
    return pl.BlockSpec(memory_space=pltpu.SMEM)


def whole(shape, column=None):
    if column is None:
        return pl.BlockSpec(shape, lambda i: (0,) * len(shape))
    return pl.BlockSpec(shape, lambda i: (0,) * (len(shape) - 1) + (column,))


def params(**more):
    return pltpu.CompilerParams(vmem_limit_bytes=VMEM_LIMIT, **more)


def pick_kernel(slots, idx_ref, k_ref, v_ref, out_ref):
    first = pl.program_id(0) * slots

    def body(s, _):
        src = pl.multiple_of(idx_ref[first + s] * BLK, BLK)
        dst = pl.multiple_of(s * 2 * BLK, 2 * BLK)
        out_ref[pl.ds(dst, BLK), :] = k_ref[pl.ds(src, BLK), :]
        out_ref[pl.ds(dst + BLK, BLK), :] = v_ref[pl.ds(src, BLK), :]
        return 0

    lax.fori_loop(0, slots, body, 0, unroll=4)


def pick_blocks(idx, keys, values, column, slots):
    rows = keys.shape[0]
    return pl.pallas_call(
        functools.partial(pick_kernel, slots // 4),
        grid=(4,),
        in_specs=[smem(), whole((rows, LANES), column), whole((rows, LANES), column)],
        out_specs=pl.BlockSpec((slots // 4 * 2 * BLK, LANES), lambda i: (i, 0)),
        out_shape=jax.ShapeDtypeStruct((slots * 2 * BLK, LANES), jnp.bfloat16),
        compiler_params=params(),
        cost_estimate=pl.CostEstimate(flops=0, bytes_accessed=10 << 20, transcendentals=0),
    )(idx, keys, values)


def pick_global_kernel(blocks, glob_ref, me_ref, k0, v0, k1, v1, k_first, v_first, k_last, v_last, up_ref, down_ref, out_ref):
    for e, pair in enumerate(((k0, v0), (k1, v1))):
        owned = glob_ref[e] // blocks == me_ref[0]
        for t, x in enumerate(pair):
            at = (e * 2 + t) * BLK
            picked = jnp.where(owned, x[...], jnp.zeros_like(x))
            for ref in (up_ref, down_ref, out_ref):
                ref[at : at + BLK, :] = picked
    at = 2 * G * BLK
    up_ref[at : at + BLK, :] = k_last[...]
    up_ref[at + BLK : at + 2 * BLK, :] = v_last[...]
    down_ref[at : at + BLK, :] = k_first[...]
    down_ref[at + BLK : at + 2 * BLK, :] = v_first[...]


def pick_global(glob, me, keys, values):
    rows, width = keys.shape
    blocks = rows // BLK

    def block(place):
        return [pl.BlockSpec((BLK, width), lambda i, glob, me: (place(glob), 0))] * 2

    specs = block(lambda glob: glob[0] % blocks) + block(lambda glob: glob[1] % blocks)
    specs += block(lambda glob: 0) + block(lambda glob: blocks - 1)
    sizes = (2 * G + 2) * BLK, (2 * G + 2) * BLK, 2 * G * BLK
    return pl.pallas_call(
        functools.partial(pick_global_kernel, blocks),
        grid_spec=pltpu.PrefetchScalarGridSpec(
            num_scalar_prefetch=2,
            grid=(1,),
            in_specs=specs,
            out_specs=tuple(pl.BlockSpec((n, width), lambda i, glob, me: (0, 0)) for n in sizes),
        ),
        out_shape=tuple(jax.ShapeDtypeStruct((n, width), jnp.bfloat16) for n in sizes),
        compiler_params=params(),
        cost_estimate=pl.CostEstimate(flops=0, bytes_accessed=1 << 19, transcendentals=0),
    )(glob, me, *[keys, values] * 4)


def sum_four_kernel(a, b, c, d, out_ref):
    out_ref[...] = a[...] + b[...] + c[...] + d[...]


def sum_four(arrays):
    shape = arrays[0].shape
    return pl.pallas_call(
        sum_four_kernel,
        grid=(1,),
        in_specs=[whole(shape)] * 4,
        out_specs=whole(shape),
        out_shape=jax.ShapeDtypeStruct(shape, jnp.bfloat16),
        compiler_params=params(),
        cost_estimate=pl.CostEstimate(flops=0, bytes_accessed=60 << 20, transcendentals=0),
    )(*arrays)


TILE = 512


def ring_specs(rows, width):
    last = rows // TILE // 2
    full = pl.BlockSpec((TILE, width), lambda i, *_: (i, 0))
    upper = pl.BlockSpec((TILE, width), lambda i, *_: (jnp.minimum(i, last - 1), 0))
    lower = pl.BlockSpec((TILE, width), lambda i, *_: (jnp.maximum(i - last, 0), 0))
    return [full, full, full, upper, lower]


def ring_values(refs):
    own, following, previous, upper, lower = refs
    top = pl.program_id(0) < pl.num_programs(0) // 2
    return own[...], following[...], jnp.where(top, upper[...], lower[...]), previous[...]


def grad_context_kernel(at_ref, *refs):
    del at_ref
    total = None
    for g, w in zip(ring_values(refs[:5]), refs[5:9]):
        term = dot(g, w[...], NT)
        total = term if total is None else total + term
    refs[9][...] = total.astype(jnp.bfloat16)


def grad_context_of(at, pieces, weight):
    rows, width = pieces[0].shape
    heads = weight.shape[0]
    turned = [
        pl.BlockSpec((heads, width), functools.partial(lambda j, i, at: (0, (at[0] + j) % 4), j))
        for j in range(4)
    ]
    return pl.pallas_call(
        grad_context_kernel,
        grid_spec=pltpu.PrefetchScalarGridSpec(
            num_scalar_prefetch=1,
            grid=(rows // TILE,),
            in_specs=ring_specs(rows, width) + turned,
            out_specs=pl.BlockSpec((TILE, heads), lambda i, at: (i, 0)),
        ),
        out_shape=jax.ShapeDtypeStruct((rows, heads), jnp.bfloat16),
        compiler_params=params(),
        cost_estimate=pl.CostEstimate(flops=2 * rows * 1024 * heads, bytes_accessed=16 << 20, transcendentals=0),
    )(at, *pieces, weight, weight, weight, weight)


def attend_kernel(
    blocks, last_block, handed_on, me_ref, slot_ref, to_ref, valid_ref, q_ref, k_ref, v_ref, g_ref, before_ref,
    after_ref, glob_ref, fetched_ref, *more,
):
    ctx_ref, dq_ref, win_out_ref, up_ref, down_ref, gsum_out_ref, *more = more[handed_on:]
    parts_out, (kpad, vpad, win_ref, gsum_ref) = more[:-4], more[-4:]
    if len(parts_out) == 1:
        ret_ref = parts_out[0]
    else:
        *parts_out, ret_ref = parts_out
    rows = blocks * BLK
    kpad[0:BLK, :] = before_ref[0:BLK, :]
    vpad[0:BLK, :] = before_ref[BLK : 2 * BLK, :]
    kpad[rows + BLK : rows + 2 * BLK, :] = after_ref[0:BLK, :]
    vpad[rows + BLK : rows + 2 * BLK, :] = after_ref[BLK : 2 * BLK, :]
    kpad[BLK : rows + BLK, :] = k_ref[...]
    vpad[BLK : rows + BLK, :] = v_ref[...]
    win_ref[...] = jnp.zeros_like(win_ref)
    gsum_ref[...] = jnp.zeros_like(gsum_ref)
    low = lax.broadcasted_iota(jnp.int32, (BLK, LANES), 1) < HD

    def body(i, _):
        row = pl.multiple_of(i * BLK, BLK)
        q = q_ref[pl.ds(row, BLK), :] * jnp.bfloat16(0.125)
        g = g_ref[pl.ds(row, BLK), :]
        zero = jnp.zeros_like(q)
        qbd = jnp.concatenate([jnp.where(low, q, zero), jnp.where(low, zero, q)], axis=0)
        gbd = jnp.concatenate([jnp.where(low, g, zero), jnp.where(low, zero, g)], axis=0)
        starts = [pl.multiple_of(slot_ref[i * R + r] * 2 * BLK, 2 * BLK) for r in range(R)]
        kcat = jnp.concatenate(
            [kpad[pl.ds(row, 3 * BLK), :]]
            + [fetched_ref[pl.ds(s, BLK), :] for s in starts]
            + [glob_ref[0, 0], glob_ref[1, 0]],
            axis=0,
        )
        vcat = jnp.concatenate(
            [vpad[pl.ds(row, 3 * BLK), :]]
            + [fetched_ref[pl.ds(s + BLK, BLK), :] for s in starts]
            + [glob_ref[0, 1], glob_ref[1, 1]],
            axis=0,
        )
        scores = dot(kcat, qbd, NT)
        block = me_ref[0] * blocks + i
        present = [block > 0, None, block < last_block]
        present += [valid_ref[i * R + r] == 1 for r in range(R)] + [None] * G
        parts = []
        for e, there in enumerate(present):
            part = scores[e * BLK : (e + 1) * BLK]
            parts.append(part if there is None else part + jnp.where(there, 0.0, NEG_FILL))
        scores = jnp.concatenate(parts, axis=0)
        peak = jnp.max(scores, axis=0, keepdims=True)
        terms = jnp.exp(scores - peak)
        probs = terms * (1.0 / jnp.sum(terms, axis=0, keepdims=True))
        probs_low = probs.astype(jnp.bfloat16)
        grad_probs = dot(vcat, gbd, NT)
        delta = jnp.sum(probs * grad_probs, axis=0, keepdims=True)
        grad_scores = (probs * (grad_probs - delta)).astype(jnp.bfloat16)
        context = dot(probs_low, vcat, TN)
        grad_q = dot(grad_scores, kcat, TN)
        grad_k = dot(grad_scores, qbd, NN)
        grad_v = dot(probs_low, gbd, NN)
        ctx_ref[pl.ds(row, BLK), :] = jnp.where(low, context[:BLK], context[BLK:]).astype(jnp.bfloat16)
        dq_ref[pl.ds(row, BLK), :] = (
            jnp.where(low, grad_q[:BLK], grad_q[BLK:]) * 0.125
        ).astype(jnp.bfloat16)
        win_ref[0, pl.ds(row, 3 * BLK), :] += grad_k[: 3 * BLK]
        win_ref[1, pl.ds(row, 3 * BLK), :] += grad_v[: 3 * BLK]
        for r in range(R):
            part = slice((3 + r) * BLK, (4 + r) * BLK)
            to = pl.multiple_of(to_ref[i * R + r] * 2 * BLK, 2 * BLK)
            ret_ref[pl.ds(to, BLK), :] = grad_k[part].astype(jnp.bfloat16)
            ret_ref[pl.ds(to + BLK, BLK), :] = grad_v[part].astype(jnp.bfloat16)
        for e in range(G):
            part = slice((3 + R + e) * BLK, (4 + R + e) * BLK)
            gsum_ref[e, 0] += grad_k[part]
            gsum_ref[e, 1] += grad_v[part]
        return 0

    lax.fori_loop(0, blocks, body, 0, unroll=2)
    win_out_ref[...] = win_ref[:, BLK : rows + BLK, :]
    up_ref[...] = win_ref[:, 0:BLK, :].astype(jnp.bfloat16)
    down_ref[...] = win_ref[:, rows + BLK : rows + 2 * BLK, :].astype(jnp.bfloat16)
    gsum_out_ref[...] = gsum_ref[...].reshape(G * 2 * BLK, LANES).astype(jnp.bfloat16)
    if len(parts_out) > 1:
        devices, _, lanes = parts_out[0].shape
        count = ret_ref.shape[0] // 2 // devices
        for p, part_ref in enumerate(parts_out):
            for d in range(devices):
                start = (p * devices + d) * count
                part_ref[d, CARRIED : CARRIED + count, :] = ret_ref[start : start + count, :]


def attend(last_block, me, slot, to, valid, q, k, v, g, before, after, glob, fetched, handed, column):
    rows, width = q.shape
    blocks = rows // BLK
    half = whole((rows, LANES), column)
    shapes = [
        ((rows, width), jnp.bfloat16),
        ((rows, width), jnp.bfloat16),
        ((2, rows, LANES), jnp.float32),
        ((2, BLK, width), jnp.bfloat16),
        ((2, BLK, width), jnp.bfloat16),
        ((G * 2 * BLK, LANES), jnp.bfloat16),
    ]
    scratch = [
        pltpu.VMEM((rows + 2 * BLK, LANES), jnp.bfloat16),
        pltpu.VMEM((rows + 2 * BLK, LANES), jnp.bfloat16),
        pltpu.VMEM((2, rows + 2 * BLK, LANES), jnp.float32),
        pltpu.VMEM((G, 2, BLK, LANES), jnp.float32),
    ]
    if not handed:
        shapes.append((fetched.shape, jnp.bfloat16))
    else:
        shapes += [((16, fetched.shape[0] // 32 + CARRIED, LANES), jnp.bfloat16)] * 2
        scratch.insert(0, pltpu.VMEM(fetched.shape, jnp.bfloat16))
    specs = [whole(shape) for shape, _ in shapes]
    specs[0] = specs[1] = half
    specs[3] = specs[4] = whole((2, BLK, LANES), column)
    return pl.pallas_call(
        functools.partial(attend_kernel, blocks, last_block, len(handed)),
        grid=(1,),
        in_specs=[
            smem(), smem(), smem(), smem(), half, half, half, half,
            pl.BlockSpec((2 * BLK, LANES), lambda i: (G, column)),
            pl.BlockSpec((2 * BLK, LANES), lambda i: (G, column)),
            whole((G, 2, BLK, LANES), column),
            whole(fetched.shape),
        ]
        + [pl.BlockSpec(memory_space=pl.ANY)] * len(handed),
        out_specs=tuple(specs),
        out_shape=tuple(jax.ShapeDtypeStruct(*shape) for shape in shapes),
        scratch_shapes=scratch,
        input_output_aliases={12: 0, 13: 1, 14: 3, 15: 4} if handed else {},
        compiler_params=params(),
        cost_estimate=pl.CostEstimate(
            flops=12 * blocks * 512 * 128 * 128 * 2, bytes_accessed=80 << 20, transcendentals=blocks * 512 * 128
        ),
    )(me, slot, to, valid, q, k, v, g, before, after, glob, fetched, *handed)


def land(entries, idx_ref, used_ref, back_ref, acc):
    first, end, capacity, skipped = entries

    def body(a, _):
        @pl.when(used_ref[a] > 0)
        def _():
            for c in range(first, end):
                at = pl.multiple_of(idx_ref[a * capacity + c] * BLK, BLK)
                src = skipped + (c - first) * 2 * BLK
                acc[0, pl.ds(at, BLK), :] += back_ref[a, src : src + BLK, :].astype(jnp.float32)
                acc[1, pl.ds(at, BLK), :] += back_ref[a, src + BLK : src + 2 * BLK, :].astype(jnp.float32)

        return 0

    lax.fori_loop(0, back_ref.shape[0], body, 0)


def edges(up_ref, down_ref, acc):
    rows = acc.shape[1]
    acc[:, rows - BLK : rows, :] += up_ref[...].astype(jnp.float32)
    acc[:, 0:BLK, :] += down_ref[...].astype(jnp.float32)


def first_kernel(
    capacity, idx_ref, used_ref, glob_ref, win_ref, back_ref, up_ref, down_ref, dk_ref, dv_ref, kept_ref, acc
):
    acc[...] = win_ref[...]
    edges(up_ref, down_ref, acc)
    land((0, capacity, capacity, 0), idx_ref, used_ref, back_ref, acc)
    dk_ref[...] = acc[0].astype(jnp.bfloat16)
    dv_ref[...] = acc[1].astype(jnp.bfloat16)
    blocks = acc.shape[1] // BLK
    for e in range(G):
        at = pl.multiple_of(glob_ref[e] % blocks * BLK, BLK)
        kept_ref[e] = acc[:, pl.ds(at, BLK), :]


def middle_kernel(capacity, idx_ref, used_ref, win_ref, back_ref, up_ref, down_ref, acc):
    acc[...] = win_ref[...]
    edges(up_ref, down_ref, acc)
    land((0, capacity // 2, capacity, CARRIED), idx_ref, used_ref, back_ref, acc)


def last_kernel(
    capacity, idx_ref, used_ref, glob_ref, me_ref, win_ref, back_ref, kept_ref, dk_in_ref, dv_in_ref,
    dk_ref, dv_ref, gw_ref, acc,
):
    acc[...] = win_ref[...]
    land((capacity // 2, capacity, capacity, CARRIED), idx_ref, used_ref, back_ref, acc)
    blocks = acc.shape[1] // BLK
    sums = CARRIED - 32

    def total(half, e):
        found = [
            jnp.concatenate(
                [
                    back_ref[(e * 2 + t) * 4 + d, sums + half * 16 : sums + (half + 1) * 16, :].astype(jnp.float32)
                    for d in range(4)
                ]
            )
            for t in range(2)
        ]
        return jnp.stack(found)

    for e in range(G):

        @pl.when(glob_ref[e] // blocks == me_ref[0])
        def _():
            at = pl.multiple_of(glob_ref[e] % blocks * BLK, BLK)
            acc[:, pl.ds(at, BLK), :] += total(1, e)

    dk_ref[:, LANES:] = acc[0].astype(jnp.bfloat16)
    dv_ref[:, LANES:] = acc[1].astype(jnp.bfloat16)
    dk_ref[:, :LANES] = dk_in_ref[...]
    dv_ref[:, :LANES] = dv_in_ref[...]
    for e in range(G):

        @pl.when(glob_ref[e] // blocks == me_ref[0])
        def _():
            at = pl.multiple_of(glob_ref[e] % blocks * BLK, BLK)
            both = (kept_ref[e] + total(0, e)).astype(jnp.bfloat16)
            dk_ref[pl.ds(at, BLK), :LANES] = both[0]
            dv_ref[pl.ds(at, BLK), :LANES] = both[1]

    for d in range(back_ref.shape[0]):
        for j in range(gw_ref.shape[1] // LANES):
            rows = back_ref[d, 16 * j : 16 * (j + 1), :]
            gw_ref[16 * d : 16 * (d + 1), j * LANES : (j + 1) * LANES] = rows.astype(jnp.float32)


def collect_first(idx, used, glob, win, back, up, down, capacity):
    rows = win.shape[1]
    out = jax.ShapeDtypeStruct((rows, LANES), jnp.bfloat16)
    kept = jax.ShapeDtypeStruct((G, 2, BLK, LANES), jnp.float32)
    return pl.pallas_call(
        functools.partial(first_kernel, capacity),
        grid=(1,),
        in_specs=[smem()] * 3 + [whole(x.shape) for x in (win, back)] + [whole((2, BLK, LANES), 0)] * 2,
        out_specs=(whole(out.shape), whole(out.shape), whole(kept.shape)),
        out_shape=(out, out, kept),
        scratch_shapes=[pltpu.VMEM((2, rows, LANES), jnp.float32)],
        compiler_params=params(),
        cost_estimate=pl.CostEstimate(flops=4 << 20, bytes_accessed=16 << 20, transcendentals=0),
    )(idx, used, glob, win, back, up, down)


def collect_middle(idx, used, win, back, up, down, capacity):
    return pl.pallas_call(
        functools.partial(middle_kernel, capacity),
        grid=(1,),
        in_specs=[smem()] * 2 + [whole(x.shape) for x in (win, back)] + [whole((2, BLK, LANES), 1)] * 2,
        out_specs=whole(win.shape),
        out_shape=jax.ShapeDtypeStruct(win.shape, jnp.float32),
        compiler_params=params(),
        cost_estimate=pl.CostEstimate(flops=4 << 20, bytes_accessed=14 << 20, transcendentals=0),
    )(idx, used, win, back, up, down)


def collect_last(idx, used, glob, me, win, back, before, capacity):
    rows = win.shape[1]
    out = jax.ShapeDtypeStruct((rows, 2 * LANES), jnp.bfloat16)
    weight = jax.ShapeDtypeStruct((2 * LANES, 1024), jnp.float32)
    dk, dv, kept = before
    arrays = (win, back, kept, dk, dv)
    return pl.pallas_call(
        functools.partial(last_kernel, capacity),
        grid=(1,),
        in_specs=[smem()] * 4 + [whole(x.shape) for x in arrays],
        out_specs=(whole(out.shape), whole(out.shape), whole(weight.shape)),
        out_shape=(out, out, weight),
        scratch_shapes=[pltpu.VMEM((2, rows, LANES), jnp.float32)],
        compiler_params=params(),
        cost_estimate=pl.CostEstimate(flops=4 << 20, bytes_accessed=12 << 20, transcendentals=0),
    )(idx, used, glob, me, *arrays)


def weight_kernel(at_ref, c_ref, *refs):
    pieces, out_ref, acc = refs[:5], refs[5], refs[6]

    @pl.when(pl.program_id(0) == 0)
    def _():
        acc[...] = jnp.zeros_like(acc)

    width = pieces[0].shape[1]
    values = ring_values(pieces)
    for i, g in enumerate(values):
        acc[:, i * width : (i + 1) * width] += dot(c_ref[...], g, TN)

    @pl.when(pl.program_id(0) == pl.num_programs(0) - 1)
    def _():
        for i in range(4):
            to = pl.multiple_of(((at_ref[0] + i) % 4) * width, width)
            out_ref[:, pl.ds(to, width)] = acc[:, i * width : (i + 1) * width].astype(jnp.bfloat16)


def weight_terms(at, context, pieces):
    rows, width = pieces[0].shape
    shape = (2 * LANES, 4 * width)
    return pl.pallas_call(
        weight_kernel,
        grid_spec=pltpu.PrefetchScalarGridSpec(
            num_scalar_prefetch=1,
            grid=(rows // TILE,),
            in_specs=[pl.BlockSpec((TILE, width), lambda i, at: (i, 0))] + ring_specs(rows, width),
            out_specs=pl.BlockSpec(shape, lambda i, at: (0, 0)),
            scratch_shapes=[pltpu.VMEM(shape, jnp.float32)],
        ),
        out_shape=jax.ShapeDtypeStruct(shape, jnp.bfloat16),
        compiler_params=params(),
        cost_estimate=pl.CostEstimate(flops=2 * rows * 1024 * 256, bytes_accessed=16 << 20, transcendentals=0),
    )(at, context, *pieces)


def carried(array):
    return whole((array.shape[0], CARRIED, LANES))


def load_kernel(own_ref, other_ref, s0, s1, part_ref, out_ref):
    del part_ref
    terms = (own_ref[...].astype(jnp.float32) + other_ref[...].astype(jnp.float32)).astype(jnp.bfloat16)
    for d in range(out_ref.shape[0]):
        rows = slice(16 * d, 16 * (d + 1))
        for j in range(terms.shape[1] // LANES):
            out_ref[d, 16 * j : 16 * (j + 1), :] = terms[rows, j * LANES : (j + 1) * LANES]
        out_ref[d, CARRIED - 32 : CARRIED - 16, :] = s0[rows, :]
        out_ref[d, CARRIED - 16 :, :] = s1[rows, :]


def load_terms(own, other, sums, part):
    return pl.pallas_call(
        load_kernel,
        grid=(1,),
        in_specs=[whole(x.shape) for x in (own, other, *sums)] + [pl.BlockSpec(memory_space=pl.ANY)],
        out_specs=carried(part),
        out_shape=jax.ShapeDtypeStruct(part.shape, part.dtype),
        input_output_aliases={4: 0},
        compiler_params=params(),
        cost_estimate=pl.CostEstimate(flops=1 << 18, bytes_accessed=4 << 20, transcendentals=0),
    )(own, other, *sums, part)


def load_sums(back, part):
    total = jnp.sum(back[:, :CARRIED].astype(jnp.float32), axis=0).astype(jnp.bfloat16)
    spread = jnp.broadcast_to(total[None], (part.shape[0], CARRIED, LANES))
    return lax.dynamic_update_slice_in_dim(part, spread, 0, 1)


def project_kernel(*refs):
    total = None
    for c, w in zip(ring_values(refs[:5]), refs[5:9]):
        term = dot(c, w[...], NN)
        total = term if total is None else total + term
    refs[9][...] = total.astype(jnp.bfloat16)


def project(pieces, weights):
    rows, width = pieces[0].shape
    return pl.pallas_call(
        project_kernel,
        grid=(rows // TILE,),
        in_specs=ring_specs(rows, width) + [pl.BlockSpec(w.shape, lambda i: (0, 0)) for w in weights],
        out_specs=pl.BlockSpec((TILE, width), lambda i: (i, 0)),
        out_shape=jax.ShapeDtypeStruct((rows, width), jnp.bfloat16),
        compiler_params=params(),
        cost_estimate=pl.CostEstimate(flops=2 * rows * 1024 * width, bytes_accessed=18 << 20, transcendentals=0),
    )(*pieces, *weights)


def shifted(array, axis, by):
    size = lax.axis_size(axis)
    return lax.ppermute(array, axis, [((i + by) % size, i) for i in range(size)])


def ring_near(array, axis):
    return shifted(array, axis, 1), shifted(array, axis, -1)


def ring_far(near, axis):
    following, previous = near
    half = following.shape[0] // 2
    return shifted(following[:half], axis, 1), shifted(previous[half:], axis, -1)


def passed_along(array, axis, by):
    size = lax.axis_size(axis)
    pairs = [(i, i + by) for i in range(size) if 0 <= i + by < size]
    return lax.ppermute(array, axis, pairs)


def per_device(
    queries, key_vectors, value_vectors, grad_output, out_weight, random_ids, random_valid, global_ids
):
    ctx_count = lax.axis_size("ctx")
    tp_count = lax.axis_size("tp")
    me = lax.axis_index("ctx")
    tp_me = lax.axis_index("tp")
    q, k, v, g_out = queries[0], key_vectors[0], value_vectors[0], grad_output[0]
    rows, width = q.shape
    blocks = rows // BLK
    requests = blocks * R
    capacity = requests // (ctx_count * 3 // 4)
    slots = ctx_count * capacity
    barrier = lax.optimization_barrier
    at = me.reshape(1)
    tp_at = tp_me.reshape(1)
    glob_at = global_ids[0]

    def exchange(parts):
        return lax.all_to_all(parts, "ctx", split_axis=0, concat_axis=0, tiled=True)

    up, down, picked = pick_global(glob_at, at, k, v)
    before, after = shifted(up, "ctx", -1), shifted(down, "ctx", 1)
    across = shifted(picked, "ctx", 2)

    ids = random_ids[0].reshape(ctx_count, requests)
    owner = ids // blocks
    local = ids % blocks
    order = jnp.arange(requests, dtype=jnp.int32)
    earlier = order[None, :] < order[:, None]
    mine = owner == me
    rank = jnp.sum((mine[:, None, :] & earlier[None]).astype(jnp.int32), axis=2)
    hit = mine[:, None, :] & (rank[:, None, :] == jnp.arange(capacity, dtype=jnp.int32)[None, :, None])
    send_idx = jnp.sum(jnp.where(hit, local[:, None, :], 0), axis=2).reshape(slots)
    send_a = pick_blocks(send_idx, k, v, 0, slots)

    send_a, picked, across, before, after, g_now = barrier((send_a, picked, across, before, after, g_out))
    fetched_a = exchange(send_a.reshape(ctx_count, -1, LANES)).reshape(send_a.shape)
    near = ring_near(g_now, "tp")
    glob = sum_four((picked, before, after, across))
    globs = [glob] + [shifted(glob, "ctx", 4 * by) for by in (1, 3, 2)]
    send_b = pick_blocks(send_idx, k, v, 1, slots)
    used = jnp.sum(mine.astype(jnp.int32), axis=1)
    my_owner = lax.dynamic_index_in_dim(owner, me, 0, keepdims=False)
    my_rank = jnp.sum(((my_owner[:, None] == my_owner[None, :]) & earlier).astype(jnp.int32), axis=1)
    my_slot = my_owner * capacity + my_rank
    part_size = capacity // 2
    my_part = my_rank // part_size
    my_place = (my_part * ctx_count + my_owner) * part_size + my_rank % part_size
    valid = lax.dynamic_slice_in_dim(random_valid[0], me * blocks, blocks, 0).reshape(-1)

    ready = barrier((send_b, fetched_a, near, globs, used, my_slot, my_place, valid))
    send_b, fetched_a, near, globs, used, my_slot, my_place, valid = ready
    glob = sum_four(globs).reshape(G, 2, BLK, width)
    pieces = (g_out, *near, *ring_far(near, "tp"))
    grad_context = grad_context_of(tp_at, pieces, out_weight)

    fetched_b = exchange(send_b.reshape(ctx_count, -1, LANES)).reshape(send_b.shape)
    last_block = blocks * ctx_count - 1

    def half(to, fetched, handed, column):
        return attend(
            last_block, at, my_slot, to, valid, q, k, v, grad_context, before, after, glob, fetched, handed, column
        )

    context, grad_q, win_a, up, down, gsum_a, ret_a = half(my_slot, fetched_a, (), 0)
    ret_a, fetched_b = barrier((ret_a, fetched_b))

    back_a = exchange(ret_a.reshape(ctx_count, -1, LANES))
    context, grad_q, win_b, up, down, gsum_b, ret_b, ret_c = half(my_place, fetched_b, (context, grad_q, up, down), 1)
    terms = weight_terms(tp_at, context, pieces)
    ret_b = load_terms(terms, shifted(terms, "dp", 1), (gsum_a, gsum_b), ret_b)
    ret_b, back_a = barrier((ret_b, back_a))

    back_b = exchange(ret_b)
    near = ring_near(context, "tp")
    up, down = passed_along(up, "ctx", -1), passed_along(down, "ctx", 1)
    ret_c = load_sums(back_b, ret_c)
    ret_c, up, down, near, w_now = barrier((ret_c, up, down, near, out_weight))

    back_c = exchange(ret_c)
    first = collect_first(send_idx, used, glob_at, win_a, back_a, up, down, capacity)
    win_b = collect_middle(send_idx, used, win_b, back_b, up, down, capacity)
    wcols = [None] * tp_count
    for by in range(tp_count):
        part = lax.dynamic_slice_in_dim(w_now, (tp_me + by) % tp_count * width, width, 1)
        wcols[-by % tp_count] = shifted(part, "tp", -by) if by else part
    projected = project((context, *near, *ring_far(near, "tp")), wcols)
    projected, win_b, first, back_c = barrier((projected, win_b, first, back_c))
    grad_k, grad_v, grad_weight = collect_last(send_idx, used, glob_at, at, win_b, back_c, first, capacity)
    return projected[None], grad_q[None], grad_k[None], grad_v[None], grad_weight


def solution(mesh):
    tokens = P("dp", "ctx", "tp")
    in_specs = (
        tokens, tokens, tokens, tokens, P("tp", None), P("dp", None, None), P("dp", None, None), P("dp", None),
    )
    out_specs = (tokens, tokens, tokens, tokens, P("tp", None))
    return jax.shard_map(per_device, mesh=mesh, in_specs=in_specs, out_specs=out_specs, check_vma=False)
```

```python
import functools

import jax
import jax.numpy as jnp
from jax import lax
from jax.experimental import pallas as pl
from jax.experimental.pallas import tpu as pltpu
from jax.sharding import PartitionSpec as P

HD = 64
BLK = 64
R = 3
G = 2
LANES = 128
NEG_FILL = -1e30
VMEM_LIMIT = 60 * 1024 * 1024
CARRIED = 96

NT = (((1,), (1,)), ((), ()))
NN = (((1,), (0,)), ((), ()))
TN = (((0,), (0,)), ((), ()))


def dot(a, b, dims):
    return lax.dot_general(a, b, dims, preferred_element_type=jnp.float32)


def smem():
    return pl.BlockSpec(memory_space=pltpu.SMEM)


def whole(shape, column=None):
    if column is None:
        return pl.BlockSpec(shape, lambda i: (0,) * len(shape))
    return pl.BlockSpec(shape, lambda i: (0,) * (len(shape) - 1) + (column,))


def params(**more):
    return pltpu.CompilerParams(vmem_limit_bytes=VMEM_LIMIT, **more)


def pick_kernel(slots, idx_ref, k_ref, v_ref, out_ref):
    first = pl.program_id(0) * slots

    def body(s, _):
        src = pl.multiple_of(idx_ref[first + s] * BLK, BLK)
        dst = pl.multiple_of(s * 2 * BLK, 2 * BLK)
        out_ref[pl.ds(dst, BLK), :] = k_ref[pl.ds(src, BLK), :]
        out_ref[pl.ds(dst + BLK, BLK), :] = v_ref[pl.ds(src, BLK), :]
        return 0

    lax.fori_loop(0, slots, body, 0, unroll=4)


def pick_blocks(idx, keys, values, column, slots):
    rows = keys.shape[0]
    return pl.pallas_call(
        functools.partial(pick_kernel, slots // 4),
        grid=(4,),
        in_specs=[smem(), whole((rows, LANES), column), whole((rows, LANES), column)],
        out_specs=pl.BlockSpec((slots // 4 * 2 * BLK, LANES), lambda i: (i, 0)),
        out_shape=jax.ShapeDtypeStruct((slots * 2 * BLK, LANES), jnp.bfloat16),
        compiler_params=params(),
        cost_estimate=pl.CostEstimate(flops=0, bytes_accessed=10 << 20, transcendentals=0),
    )(idx, keys, values)


def pick_global_kernel(blocks, glob_ref, me_ref, k0, v0, k1, v1, k_first, v_first, k_last, v_last, up_ref, down_ref, out_ref):
    for e, pair in enumerate(((k0, v0), (k1, v1))):
        owned = glob_ref[e] // blocks == me_ref[0]
        for t, x in enumerate(pair):
            at = (e * 2 + t) * BLK
            picked = jnp.where(owned, x[...], jnp.zeros_like(x))
            for ref in (up_ref, down_ref, out_ref):
                ref[at : at + BLK, :] = picked
    at = 2 * G * BLK
    up_ref[at : at + BLK, :] = k_last[...]
    up_ref[at + BLK : at + 2 * BLK, :] = v_last[...]
    down_ref[at : at + BLK, :] = k_first[...]
    down_ref[at + BLK : at + 2 * BLK, :] = v_first[...]


def pick_global(glob, me, keys, values):
    rows, width = keys.shape
    blocks = rows // BLK

    def block(place):
        return [pl.BlockSpec((BLK, width), lambda i, glob, me: (place(glob), 0))] * 2

    specs = block(lambda glob: glob[0] % blocks) + block(lambda glob: glob[1] % blocks)
    specs += block(lambda glob: 0) + block(lambda glob: blocks - 1)
    sizes = (2 * G + 2) * BLK, (2 * G + 2) * BLK, 2 * G * BLK
    return pl.pallas_call(
        functools.partial(pick_global_kernel, blocks),
        grid_spec=pltpu.PrefetchScalarGridSpec(
            num_scalar_prefetch=2,
            grid=(1,),
            in_specs=specs,
            out_specs=tuple(pl.BlockSpec((n, width), lambda i, glob, me: (0, 0)) for n in sizes),
        ),
        out_shape=tuple(jax.ShapeDtypeStruct((n, width), jnp.bfloat16) for n in sizes),
        compiler_params=params(),
        cost_estimate=pl.CostEstimate(flops=0, bytes_accessed=1 << 19, transcendentals=0),
    )(glob, me, *[keys, values] * 4)


def sum_four_kernel(a, b, c, d, out_ref):
    out_ref[...] = a[...] + b[...] + c[...] + d[...]


def sum_four(arrays):
    shape = arrays[0].shape
    return pl.pallas_call(
        sum_four_kernel,
        grid=(1,),
        in_specs=[whole(shape)] * 4,
        out_specs=whole(shape),
        out_shape=jax.ShapeDtypeStruct(shape, jnp.bfloat16),
        compiler_params=params(),
        cost_estimate=pl.CostEstimate(flops=0, bytes_accessed=60 << 20, transcendentals=0),
    )(*arrays)


TILE = 512


def ring_specs(rows, width):
    last = rows // TILE // 2
    full = pl.BlockSpec((TILE, width), lambda i, *_: (i, 0))
    upper = pl.BlockSpec((TILE, width), lambda i, *_: (jnp.minimum(i, last - 1), 0))
    lower = pl.BlockSpec((TILE, width), lambda i, *_: (jnp.maximum(i - last, 0), 0))
    return [full, full, full, upper, lower]


def ring_values(refs):
    own, following, previous, upper, lower = refs
    top = pl.program_id(0) < pl.num_programs(0) // 2
    return own[...], following[...], jnp.where(top, upper[...], lower[...]), previous[...]


def grad_context_kernel(at_ref, *refs):
    del at_ref
    total = None
    for g, w in zip(ring_values(refs[:5]), refs[5:9]):
        term = dot(g, w[...], NT)
        total = term if total is None else total + term
    refs[9][...] = total.astype(jnp.bfloat16)


def grad_context_of(at, pieces, weight):
    rows, width = pieces[0].shape
    heads = weight.shape[0]
    turned = [
        pl.BlockSpec((heads, width), functools.partial(lambda j, i, at: (0, (at[0] + j) % 4), j))
        for j in range(4)
    ]
    return pl.pallas_call(
        grad_context_kernel,
        grid_spec=pltpu.PrefetchScalarGridSpec(
            num_scalar_prefetch=1,
            grid=(rows // TILE,),
            in_specs=ring_specs(rows, width) + turned,
            out_specs=pl.BlockSpec((TILE, heads), lambda i, at: (i, 0)),
        ),
        out_shape=jax.ShapeDtypeStruct((rows, heads), jnp.bfloat16),
        compiler_params=params(),
        cost_estimate=pl.CostEstimate(flops=2 * rows * 1024 * heads, bytes_accessed=16 << 20, transcendentals=0),
    )(at, *pieces, weight, weight, weight, weight)


def attend_kernel(
    blocks, last_block, handed_on, me_ref, slot_ref, to_ref, valid_ref, q_ref, k_ref, v_ref, g_ref, before_ref,
    after_ref, glob_ref, fetched_ref, *more,
):
    ctx_ref, dq_ref, win_out_ref, up_ref, down_ref, gsum_out_ref, *more = more[handed_on:]
    parts_out, (kpad, vpad, win_ref, gsum_ref) = more[:-4], more[-4:]
    if len(parts_out) == 1:
        ret_ref = parts_out[0]
    else:
        *parts_out, ret_ref = parts_out
    rows = blocks * BLK
    kpad[0:BLK, :] = before_ref[0:BLK, :]
    vpad[0:BLK, :] = before_ref[BLK : 2 * BLK, :]
    kpad[rows + BLK : rows + 2 * BLK, :] = after_ref[0:BLK, :]
    vpad[rows + BLK : rows + 2 * BLK, :] = after_ref[BLK : 2 * BLK, :]
    kpad[BLK : rows + BLK, :] = k_ref[...]
    vpad[BLK : rows + BLK, :] = v_ref[...]
    win_ref[...] = jnp.zeros_like(win_ref)
    gsum_ref[...] = jnp.zeros_like(gsum_ref)
    low = lax.broadcasted_iota(jnp.int32, (BLK, LANES), 1) < HD

    def body(i, _):
        row = pl.multiple_of(i * BLK, BLK)
        q = q_ref[pl.ds(row, BLK), :] * jnp.bfloat16(0.125)
        g = g_ref[pl.ds(row, BLK), :]
        zero = jnp.zeros_like(q)
        qbd = jnp.concatenate([jnp.where(low, q, zero), jnp.where(low, zero, q)], axis=0)
        gbd = jnp.concatenate([jnp.where(low, g, zero), jnp.where(low, zero, g)], axis=0)
        starts = [pl.multiple_of(slot_ref[i * R + r] * 2 * BLK, 2 * BLK) for r in range(R)]
        kcat = jnp.concatenate(
            [kpad[pl.ds(row, 3 * BLK), :]]
            + [fetched_ref[pl.ds(s, BLK), :] for s in starts]
            + [glob_ref[0, 0], glob_ref[1, 0]],
            axis=0,
        )
        vcat = jnp.concatenate(
            [vpad[pl.ds(row, 3 * BLK), :]]
            + [fetched_ref[pl.ds(s + BLK, BLK), :] for s in starts]
            + [glob_ref[0, 1], glob_ref[1, 1]],
            axis=0,
        )
        scores = dot(kcat, qbd, NT)
        block = me_ref[0] * blocks + i
        present = [block > 0, None, block < last_block]
        present += [valid_ref[i * R + r] == 1 for r in range(R)] + [None] * G
        parts = []
        for e, there in enumerate(present):
            part = scores[e * BLK : (e + 1) * BLK]
            parts.append(part if there is None else part + jnp.where(there, 0.0, NEG_FILL))
        scores = jnp.concatenate(parts, axis=0)
        peak = jnp.max(scores, axis=0, keepdims=True)
        terms = jnp.exp(scores - peak)
        probs = terms * (1.0 / jnp.sum(terms, axis=0, keepdims=True))
        probs_low = probs.astype(jnp.bfloat16)
        grad_probs = dot(vcat, gbd, NT)
        delta = jnp.sum(probs * grad_probs, axis=0, keepdims=True)
        grad_scores = (probs * (grad_probs - delta)).astype(jnp.bfloat16)
        context = dot(probs_low, vcat, TN)
        grad_q = dot(grad_scores, kcat, TN)
        grad_k = dot(grad_scores, qbd, NN)
        grad_v = dot(probs_low, gbd, NN)
        ctx_ref[pl.ds(row, BLK), :] = jnp.where(low, context[:BLK], context[BLK:]).astype(jnp.bfloat16)
        dq_ref[pl.ds(row, BLK), :] = (
            jnp.where(low, grad_q[:BLK], grad_q[BLK:]) * 0.125
        ).astype(jnp.bfloat16)
        win_ref[0, pl.ds(row, 3 * BLK), :] += grad_k[: 3 * BLK]
        win_ref[1, pl.ds(row, 3 * BLK), :] += grad_v[: 3 * BLK]
        for r in range(R):
            part = slice((3 + r) * BLK, (4 + r) * BLK)
            to = pl.multiple_of(to_ref[i * R + r] * 2 * BLK, 2 * BLK)
            ret_ref[pl.ds(to, BLK), :] = grad_k[part].astype(jnp.bfloat16)
            ret_ref[pl.ds(to + BLK, BLK), :] = grad_v[part].astype(jnp.bfloat16)
        for e in range(G):
            part = slice((3 + R + e) * BLK, (4 + R + e) * BLK)
            gsum_ref[e, 0] += grad_k[part]
            gsum_ref[e, 1] += grad_v[part]
        return 0

    lax.fori_loop(0, blocks, body, 0, unroll=2)
    win_out_ref[...] = win_ref[:, BLK : rows + BLK, :]
    up_ref[...] = win_ref[:, 0:BLK, :].astype(jnp.bfloat16)
    down_ref[...] = win_ref[:, rows + BLK : rows + 2 * BLK, :].astype(jnp.bfloat16)
    gsum_out_ref[...] = gsum_ref[...].reshape(G * 2 * BLK, LANES).astype(jnp.bfloat16)
    if len(parts_out) > 1:
        devices, _, lanes = parts_out[0].shape
        count = ret_ref.shape[0] // 2 // devices
        for p, part_ref in enumerate(parts_out):
            for d in range(devices):
                start = (p * devices + d) * count
                part_ref[d, CARRIED : CARRIED + count, :] = ret_ref[start : start + count, :]


def attend(last_block, me, slot, to, valid, q, k, v, g, before, after, glob, fetched, handed, column):
    rows, width = q.shape
    blocks = rows // BLK
    half = whole((rows, LANES), column)
    shapes = [
        ((rows, width), jnp.bfloat16),
        ((rows, width), jnp.bfloat16),
        ((2, rows, LANES), jnp.float32),
        ((2, BLK, width), jnp.bfloat16),
        ((2, BLK, width), jnp.bfloat16),
        ((G * 2 * BLK, LANES), jnp.bfloat16),
    ]
    scratch = [
        pltpu.VMEM((rows + 2 * BLK, LANES), jnp.bfloat16),
        pltpu.VMEM((rows + 2 * BLK, LANES), jnp.bfloat16),
        pltpu.VMEM((2, rows + 2 * BLK, LANES), jnp.float32),
        pltpu.VMEM((G, 2, BLK, LANES), jnp.float32),
    ]
    if not handed:
        shapes.append((fetched.shape, jnp.bfloat16))
    else:
        shapes += [((16, fetched.shape[0] // 32 + CARRIED, LANES), jnp.bfloat16)] * 2
        scratch.insert(0, pltpu.VMEM(fetched.shape, jnp.bfloat16))
    specs = [whole(shape) for shape, _ in shapes]
    specs[0] = specs[1] = half
    specs[3] = specs[4] = whole((2, BLK, LANES), column)
    return pl.pallas_call(
        functools.partial(attend_kernel, blocks, last_block, len(handed)),
        grid=(1,),
        in_specs=[
            smem(), smem(), smem(), smem(), half, half, half, half,
            pl.BlockSpec((2 * BLK, LANES), lambda i: (G, column)),
            pl.BlockSpec((2 * BLK, LANES), lambda i: (G, column)),
            whole((G, 2, BLK, LANES), column),
            whole(fetched.shape),
        ]
        + [pl.BlockSpec(memory_space=pl.ANY)] * len(handed),
        out_specs=tuple(specs),
        out_shape=tuple(jax.ShapeDtypeStruct(*shape) for shape in shapes),
        scratch_shapes=scratch,
        input_output_aliases={12: 0, 13: 1, 14: 3, 15: 4} if handed else {},
        compiler_params=params(),
        cost_estimate=pl.CostEstimate(
            flops=12 * blocks * 512 * 128 * 128 * 2, bytes_accessed=80 << 20, transcendentals=blocks * 512 * 128
        ),
    )(me, slot, to, valid, q, k, v, g, before, after, glob, fetched, *handed)


def land(entries, idx_ref, used_ref, back_ref, acc):
    first, end, capacity, skipped = entries

    def body(a, _):
        @pl.when(used_ref[a] > 0)
        def _():
            for c in range(first, end):
                at = pl.multiple_of(idx_ref[a * capacity + c] * BLK, BLK)
                src = skipped + (c - first) * 2 * BLK
                acc[0, pl.ds(at, BLK), :] += back_ref[a, src : src + BLK, :].astype(jnp.float32)
                acc[1, pl.ds(at, BLK), :] += back_ref[a, src + BLK : src + 2 * BLK, :].astype(jnp.float32)

        return 0

    lax.fori_loop(0, back_ref.shape[0], body, 0)


def edges(up_ref, down_ref, acc):
    rows = acc.shape[1]
    acc[:, rows - BLK : rows, :] += up_ref[...].astype(jnp.float32)
    acc[:, 0:BLK, :] += down_ref[...].astype(jnp.float32)


def first_kernel(
    capacity, idx_ref, used_ref, glob_ref, win_ref, back_ref, up_ref, down_ref, dk_ref, dv_ref, kept_ref, acc
):
    acc[...] = win_ref[...]
    edges(up_ref, down_ref, acc)
    land((0, capacity, capacity, 0), idx_ref, used_ref, back_ref, acc)
    dk_ref[...] = acc[0].astype(jnp.bfloat16)
    dv_ref[...] = acc[1].astype(jnp.bfloat16)
    blocks = acc.shape[1] // BLK
    for e in range(G):
        at = pl.multiple_of(glob_ref[e] % blocks * BLK, BLK)
        kept_ref[e] = acc[:, pl.ds(at, BLK), :]


def middle_kernel(capacity, idx_ref, used_ref, win_ref, back_ref, up_ref, down_ref, acc):
    acc[...] = win_ref[...]
    edges(up_ref, down_ref, acc)
    land((0, capacity // 2, capacity, CARRIED), idx_ref, used_ref, back_ref, acc)


def last_kernel(
    capacity, idx_ref, used_ref, glob_ref, me_ref, win_ref, back_ref, kept_ref, dk_in_ref, dv_in_ref,
    dk_ref, dv_ref, acc,
):
    acc[...] = win_ref[...]
    land((capacity // 2, capacity, capacity, CARRIED), idx_ref, used_ref, back_ref, acc)
    blocks = acc.shape[1] // BLK
    sums = CARRIED - 32

    def total(half, e):
        found = [
            jnp.concatenate(
                [
                    back_ref[(e * 2 + t) * 4 + d, sums + half * 16 : sums + (half + 1) * 16, :].astype(jnp.float32)
                    for d in range(4)
                ]
            )
            for t in range(2)
        ]
        return jnp.stack(found)

    for e in range(G):

        @pl.when(glob_ref[e] // blocks == me_ref[0])
        def _():
            at = pl.multiple_of(glob_ref[e] % blocks * BLK, BLK)
            acc[:, pl.ds(at, BLK), :] += total(1, e)

    dk_ref[:, LANES:] = acc[0].astype(jnp.bfloat16)
    dv_ref[:, LANES:] = acc[1].astype(jnp.bfloat16)
    dk_ref[:, :LANES] = dk_in_ref[...]
    dv_ref[:, :LANES] = dv_in_ref[...]
    for e in range(G):

        @pl.when(glob_ref[e] // blocks == me_ref[0])
        def _():
            at = pl.multiple_of(glob_ref[e] % blocks * BLK, BLK)
            both = (kept_ref[e] + total(0, e)).astype(jnp.bfloat16)
            dk_ref[pl.ds(at, BLK), :LANES] = both[0]
            dv_ref[pl.ds(at, BLK), :LANES] = both[1]


def collect_first(idx, used, glob, win, back, up, down, capacity):
    rows = win.shape[1]
    out = jax.ShapeDtypeStruct((rows, LANES), jnp.bfloat16)
    kept = jax.ShapeDtypeStruct((G, 2, BLK, LANES), jnp.float32)
    return pl.pallas_call(
        functools.partial(first_kernel, capacity),
        grid=(1,),
        in_specs=[smem()] * 3 + [whole(x.shape) for x in (win, back)] + [whole((2, BLK, LANES), 0)] * 2,
        out_specs=(whole(out.shape), whole(out.shape), whole(kept.shape)),
        out_shape=(out, out, kept),
        scratch_shapes=[pltpu.VMEM((2, rows, LANES), jnp.float32)],
        compiler_params=params(),
        cost_estimate=pl.CostEstimate(flops=4 << 20, bytes_accessed=16 << 20, transcendentals=0),
    )(idx, used, glob, win, back, up, down)


def collect_middle(idx, used, win, back, up, down, capacity):
    return pl.pallas_call(
        functools.partial(middle_kernel, capacity),
        grid=(1,),
        in_specs=[smem()] * 2 + [whole(x.shape) for x in (win, back)] + [whole((2, BLK, LANES), 1)] * 2,
        out_specs=whole(win.shape),
        out_shape=jax.ShapeDtypeStruct(win.shape, jnp.float32),
        compiler_params=params(),
        cost_estimate=pl.CostEstimate(flops=4 << 20, bytes_accessed=14 << 20, transcendentals=0),
    )(idx, used, win, back, up, down)


def collect_last(idx, used, glob, me, win, back, before, capacity):
    rows = win.shape[1]
    out = jax.ShapeDtypeStruct((rows, 2 * LANES), jnp.bfloat16)
    dk, dv, kept = before
    arrays = (win, back, kept, dk, dv)
    return pl.pallas_call(
        functools.partial(last_kernel, capacity),
        grid=(1,),
        in_specs=[smem()] * 4 + [whole(x.shape) for x in arrays],
        out_specs=(whole(out.shape), whole(out.shape)),
        out_shape=(out, out),
        scratch_shapes=[pltpu.VMEM((2, rows, LANES), jnp.float32)],
        compiler_params=params(),
        cost_estimate=pl.CostEstimate(flops=4 << 20, bytes_accessed=12 << 20, transcendentals=0),
    )(idx, used, glob, me, *arrays)


def weight_kernel(at_ref, c_ref, *refs):
    pieces, (keep_ref, give_ref, acc) = refs[:5], refs[5:]

    @pl.when(pl.program_id(0) == 0)
    def _():
        acc[...] = jnp.zeros_like(acc)

    width = pieces[0].shape[1]
    values = ring_values(pieces)
    for i, g in enumerate(values):
        acc[:, :, i * width : (i + 1) * width] += dot(c_ref[...], g, TN).reshape(2, LANES, width)

    @pl.when(pl.program_id(0) == pl.num_programs(0) - 1)
    def _():
        for i in range(4):
            to = pl.multiple_of(((at_ref[0] + i) % 4) * width, width)
            part = acc.at[:, :, i * width : (i + 1) * width]
            keep_ref[:, pl.ds(to, width)] = part[at_ref[1]].astype(jnp.bfloat16)
            give_ref[:, pl.ds(to, width)] = part[1 - at_ref[1]].astype(jnp.bfloat16)


def weight_terms(at, context, pieces):
    rows, width = pieces[0].shape
    shape = (LANES, 4 * width)
    return pl.pallas_call(
        weight_kernel,
        grid_spec=pltpu.PrefetchScalarGridSpec(
            num_scalar_prefetch=1,
            grid=(rows // TILE,),
            in_specs=[pl.BlockSpec((TILE, width), lambda i, at: (i, 0))] + ring_specs(rows, width),
            out_specs=(pl.BlockSpec(shape, lambda i, at: (0, 0)),) * 2,
            scratch_shapes=[pltpu.VMEM((2, *shape), jnp.float32)],
        ),
        out_shape=(jax.ShapeDtypeStruct(shape, jnp.bfloat16),) * 2,
        compiler_params=params(),
        cost_estimate=pl.CostEstimate(flops=2 * rows * 1024 * 256, bytes_accessed=16 << 20, transcendentals=0),
    )(at, context, *pieces)


def carried(array):
    return whole((array.shape[0], CARRIED, LANES))


def load_kernel(own_ref, other_ref, s0, s1, part_ref, out_ref):
    del part_ref
    terms = (own_ref[...].astype(jnp.float32) + other_ref[...].astype(jnp.float32)).astype(jnp.bfloat16)
    for d in range(out_ref.shape[0]):
        rows = slice(16 * d, 16 * (d + 1))
        for j in range(4):
            column = (d % 2 * 4 + j) * LANES
            out_ref[d, 16 * j : 16 * (j + 1), :] = terms[d // 2 * 16 : d // 2 * 16 + 16, column : column + LANES]
        out_ref[d, CARRIED - 32 : CARRIED - 16, :] = s0[rows, :]
        out_ref[d, CARRIED - 16 :, :] = s1[rows, :]


def load_terms(own, other, sums, part):
    return pl.pallas_call(
        load_kernel,
        grid=(1,),
        in_specs=[whole(x.shape) for x in (own, other, *sums)] + [pl.BlockSpec(memory_space=pl.ANY)],
        out_specs=carried(part),
        out_shape=jax.ShapeDtypeStruct(part.shape, part.dtype),
        input_output_aliases={4: 0},
        compiler_params=params(),
        cost_estimate=pl.CostEstimate(flops=1 << 18, bytes_accessed=4 << 20, transcendentals=0),
    )(own, other, *sums, part)


def load_sums(back, part):
    total = jnp.sum(back[:, :CARRIED].astype(jnp.float32), axis=0).astype(jnp.bfloat16)
    spread = jnp.broadcast_to(total[None], (part.shape[0], CARRIED, LANES))
    return lax.dynamic_update_slice_in_dim(part, spread, 0, 1)


def weight_kernel_last(at_ref, own_ref, other_ref, out_ref):
    for half_ref, half in ((own_ref, at_ref[1]), (other_ref, 1 - at_ref[1])):
        for d in range(half_ref.shape[0]):
            row = pl.multiple_of(half * LANES + d // 2 * 16, 16)
            for j in range(4):
                column = (d % 2 * 4 + j) * LANES
                tile = half_ref[d, 16 * j : 16 * (j + 1), :].astype(jnp.float32)
                out_ref[pl.ds(row, 16), column : column + LANES] = tile


def weight_last(at, own, other):
    shape = (2 * LANES, 1024)
    return pl.pallas_call(
        weight_kernel_last,
        grid=(1,),
        in_specs=[smem(), whole(own.shape), whole(other.shape)],
        out_specs=whole(shape),
        out_shape=jax.ShapeDtypeStruct(shape, jnp.float32),
        compiler_params=params(),
        cost_estimate=pl.CostEstimate(flops=1 << 18, bytes_accessed=2 << 20, transcendentals=0),
    )(at, own, other)


def project_kernel(*refs):
    total = None
    for c, w in zip(ring_values(refs[:5]), refs[5:9]):
        term = dot(c, w[...], NN)
        total = term if total is None else total + term
    refs[9][...] = total.astype(jnp.bfloat16)


def project(pieces, weights):
    rows, width = pieces[0].shape
    return pl.pallas_call(
        project_kernel,
        grid=(rows // TILE,),
        in_specs=ring_specs(rows, width) + [pl.BlockSpec(w.shape, lambda i: (0, 0)) for w in weights],
        out_specs=pl.BlockSpec((TILE, width), lambda i: (i, 0)),
        out_shape=jax.ShapeDtypeStruct((rows, width), jnp.bfloat16),
        compiler_params=params(),
        cost_estimate=pl.CostEstimate(flops=2 * rows * 1024 * width, bytes_accessed=18 << 20, transcendentals=0),
    )(*pieces, *weights)


def shifted(array, axis, by):
    size = lax.axis_size(axis)
    return lax.ppermute(array, axis, [((i + by) % size, i) for i in range(size)])


def ring_near(array, axis):
    return shifted(array, axis, 1), shifted(array, axis, -1)


def ring_far(near, axis):
    following, previous = near
    half = following.shape[0] // 2
    return shifted(following[:half], axis, 1), shifted(previous[half:], axis, -1)


def passed_along(array, axis, by):
    size = lax.axis_size(axis)
    pairs = [(i, i + by) for i in range(size) if 0 <= i + by < size]
    return lax.ppermute(array, axis, pairs)


def per_device(
    queries, key_vectors, value_vectors, grad_output, out_weight, random_ids, random_valid, global_ids
):
    ctx_count = lax.axis_size("ctx")
    tp_count = lax.axis_size("tp")
    me = lax.axis_index("ctx")
    tp_me = lax.axis_index("tp")
    q, k, v, g_out = queries[0], key_vectors[0], value_vectors[0], grad_output[0]
    rows, width = q.shape
    blocks = rows // BLK
    requests = blocks * R
    capacity = requests // (ctx_count * 3 // 4)
    slots = ctx_count * capacity
    barrier = lax.optimization_barrier
    at = me.reshape(1)
    tp_at = jnp.stack([tp_me, lax.axis_index("dp")])
    glob_at = global_ids[0]

    def exchange(parts):
        return lax.all_to_all(parts, "ctx", split_axis=0, concat_axis=0, tiled=True)

    up, down, picked = pick_global(glob_at, at, k, v)
    before, after = shifted(up, "ctx", -1), shifted(down, "ctx", 1)
    across = shifted(picked, "ctx", 2)

    ids = random_ids[0].reshape(ctx_count, requests)
    owner = ids // blocks
    local = ids % blocks
    order = jnp.arange(requests, dtype=jnp.int32)
    earlier = order[None, :] < order[:, None]
    mine = owner == me
    rank = jnp.sum((mine[:, None, :] & earlier[None]).astype(jnp.int32), axis=2)
    hit = mine[:, None, :] & (rank[:, None, :] == jnp.arange(capacity, dtype=jnp.int32)[None, :, None])
    send_idx = jnp.sum(jnp.where(hit, local[:, None, :], 0), axis=2).reshape(slots)
    send_a = pick_blocks(send_idx, k, v, 0, slots)

    send_a, picked, across, before, after, g_now = barrier((send_a, picked, across, before, after, g_out))
    fetched_a = exchange(send_a.reshape(ctx_count, -1, LANES)).reshape(send_a.shape)
    near = ring_near(g_now, "tp")
    glob = sum_four((picked, before, after, across))
    globs = [glob] + [shifted(glob, "ctx", 4 * by) for by in (1, 3, 2)]
    send_b = pick_blocks(send_idx, k, v, 1, slots)
    used = jnp.sum(mine.astype(jnp.int32), axis=1)
    my_owner = lax.dynamic_index_in_dim(owner, me, 0, keepdims=False)
    my_rank = jnp.sum(((my_owner[:, None] == my_owner[None, :]) & earlier).astype(jnp.int32), axis=1)
    my_slot = my_owner * capacity + my_rank
    part_size = capacity // 2
    my_part = my_rank // part_size
    my_place = (my_part * ctx_count + my_owner) * part_size + my_rank % part_size
    valid = lax.dynamic_slice_in_dim(random_valid[0], me * blocks, blocks, 0).reshape(-1)

    ready = barrier((send_b, fetched_a, near, globs, used, my_slot, my_place, valid))
    send_b, fetched_a, near, globs, used, my_slot, my_place, valid = ready
    glob = sum_four(globs).reshape(G, 2, BLK, width)
    pieces = (g_out, *near, *ring_far(near, "tp"))
    grad_context = grad_context_of(tp_at, pieces, out_weight)

    fetched_b = exchange(send_b.reshape(ctx_count, -1, LANES)).reshape(send_b.shape)
    last_block = blocks * ctx_count - 1

    def half(to, fetched, handed, column):
        return attend(
            last_block, at, my_slot, to, valid, q, k, v, grad_context, before, after, glob, fetched, handed, column
        )

    context, grad_q, win_a, up, down, gsum_a, ret_a = half(my_slot, fetched_a, (), 0)
    ret_a, fetched_b = barrier((ret_a, fetched_b))

    back_a = exchange(ret_a.reshape(ctx_count, -1, LANES))
    context, grad_q, win_b, up, down, gsum_b, ret_b, ret_c = half(my_place, fetched_b, (context, grad_q, up, down), 1)
    keep, give = weight_terms(tp_at, context, pieces)
    ret_b = load_terms(keep, shifted(give, "dp", 1), (gsum_a, gsum_b), ret_b)
    ret_b, back_a = barrier((ret_b, back_a))

    back_b = exchange(ret_b)
    near = ring_near(context, "tp")
    up, down = passed_along(up, "ctx", -1), passed_along(down, "ctx", 1)
    ret_c = load_sums(back_b, ret_c)
    ret_c, up, down, near, w_now = barrier((ret_c, up, down, near, out_weight))

    back_c = exchange(ret_c)
    first = collect_first(send_idx, used, glob_at, win_a, back_a, up, down, capacity)
    win_b = collect_middle(send_idx, used, win_b, back_b, up, down, capacity)
    wcols = [None] * tp_count
    for by in range(tp_count):
        part = lax.dynamic_slice_in_dim(w_now, (tp_me + by) % tp_count * width, width, 1)
        wcols[-by % tp_count] = shifted(part, "tp", -by) if by else part
    projected = project((context, *near, *ring_far(near, "tp")), wcols)
    projected, win_b, first, back_c = barrier((projected, win_b, first, back_c))
    weight_own = back_c[:, : CARRIED - 32]
    grad_weight = weight_last(tp_at, weight_own, shifted(weight_own, "dp", 1))
    grad_k, grad_v = collect_last(send_idx, used, glob_at, at, win_b, back_c, first, capacity)
    return projected[None], grad_q[None], grad_k[None], grad_v[None], grad_weight


def solution(mesh):
    tokens = P("dp", "ctx", "tp")
    in_specs = (
        tokens, tokens, tokens, tokens, P("tp", None), P("dp", None, None), P("dp", None, None), P("dp", None),
    )
    out_specs = (tokens, tokens, tokens, tokens, P("tp", None))
    return jax.shard_map(per_device, mesh=mesh, in_specs=in_specs, out_specs=out_specs, check_vma=False)
```

```python
import functools

import jax
import jax.numpy as jnp
from jax import lax
from jax.experimental import pallas as pl
from jax.experimental.pallas import tpu as pltpu
from jax.sharding import PartitionSpec as P

HD = 64
BLK = 64
R = 3
G = 2
LANES = 128
NEG_FILL = -1e30
CARRIED = 96

NT = (((1,), (1,)), ((), ()))
NN = (((1,), (0,)), ((), ()))
TN = (((0,), (0,)), ((), ()))


def dot(a, b, dims):
    return lax.dot_general(a, b, dims, preferred_element_type=jnp.float32)


def smem():
    return pl.BlockSpec(memory_space=pltpu.SMEM)


def whole(shape, column=None):
    if column is None:
        return pl.BlockSpec(shape, lambda i: (0,) * len(shape))
    return pl.BlockSpec(shape, lambda i: (0,) * (len(shape) - 1) + (column,))


def params(mebibytes):
    return pltpu.CompilerParams(vmem_limit_bytes=mebibytes << 20)


def pick_kernel(slots, idx_ref, k_ref, v_ref, out_ref):
    first = pl.program_id(0) * slots

    def body(s, _):
        src = pl.multiple_of(idx_ref[first + s] * BLK, BLK)
        dst = pl.multiple_of(s * 2 * BLK, 2 * BLK)
        out_ref[pl.ds(dst, BLK), :] = k_ref[pl.ds(src, BLK), :]
        out_ref[pl.ds(dst + BLK, BLK), :] = v_ref[pl.ds(src, BLK), :]
        return 0

    lax.fori_loop(0, slots, body, 0, unroll=4)


def pick_blocks(idx, keys, values, column, slots):
    rows = keys.shape[0]
    return pl.pallas_call(
        functools.partial(pick_kernel, slots // 4),
        grid=(4,),
        in_specs=[smem(), whole((rows, LANES), column), whole((rows, LANES), column)],
        out_specs=pl.BlockSpec((slots // 4 * 2 * BLK, LANES), lambda i: (i, 0)),
        out_shape=jax.ShapeDtypeStruct((slots * 2 * BLK, LANES), jnp.bfloat16),
        compiler_params=params(12),
        cost_estimate=pl.CostEstimate(flops=0, bytes_accessed=10 << 20, transcendentals=0),
    )(idx, keys, values)


def pick_global_kernel(blocks, glob_ref, me_ref, k0, v0, k1, v1, k_first, v_first, k_last, v_last, up_ref, down_ref, out_ref):
    for e, pair in enumerate(((k0, v0), (k1, v1))):
        owned = glob_ref[e] // blocks == me_ref[0]
        for t, x in enumerate(pair):
            at = (e * 2 + t) * BLK
            picked = jnp.where(owned, x[...], jnp.zeros_like(x))
            for ref in (up_ref, down_ref, out_ref):
                ref[at : at + BLK, :] = picked
    at = 2 * G * BLK
    up_ref[at : at + BLK, :] = k_last[...]
    up_ref[at + BLK : at + 2 * BLK, :] = v_last[...]
    down_ref[at : at + BLK, :] = k_first[...]
    down_ref[at + BLK : at + 2 * BLK, :] = v_first[...]


def pick_global(glob, me, keys, values):
    rows, width = keys.shape
    blocks = rows // BLK

    def block(place):
        return [pl.BlockSpec((BLK, width), lambda i, glob, me: (place(glob), 0))] * 2

    specs = block(lambda glob: glob[0] % blocks) + block(lambda glob: glob[1] % blocks)
    specs += block(lambda glob: 0) + block(lambda glob: blocks - 1)
    sizes = (2 * G + 2) * BLK, (2 * G + 2) * BLK, 2 * G * BLK
    return pl.pallas_call(
        functools.partial(pick_global_kernel, blocks),
        grid_spec=pltpu.PrefetchScalarGridSpec(
            num_scalar_prefetch=2,
            grid=(1,),
            in_specs=specs,
            out_specs=tuple(pl.BlockSpec((n, width), lambda i, glob, me: (0, 0)) for n in sizes),
        ),
        out_shape=tuple(jax.ShapeDtypeStruct((n, width), jnp.bfloat16) for n in sizes),
        compiler_params=params(4),
        cost_estimate=pl.CostEstimate(flops=0, bytes_accessed=1 << 19, transcendentals=0),
    )(glob, me, *[keys, values] * 4)


def sum_four_kernel(a, b, c, d, out_ref):
    out_ref[...] = a[...] + b[...] + c[...] + d[...]


def sum_four(arrays):
    shape = arrays[0].shape
    return pl.pallas_call(
        sum_four_kernel,
        grid=(1,),
        in_specs=[whole(shape)] * 4,
        out_specs=whole(shape),
        out_shape=jax.ShapeDtypeStruct(shape, jnp.bfloat16),
        compiler_params=params(4),
        cost_estimate=pl.CostEstimate(flops=0, bytes_accessed=60 << 20, transcendentals=0),
    )(*arrays)


TILE = 512


def ring_specs(rows, width):
    last = rows // TILE // 2
    full = pl.BlockSpec((TILE, width), lambda i, *_: (i, 0))
    upper = pl.BlockSpec((TILE, width), lambda i, *_: (jnp.minimum(i, last - 1), 0))
    lower = pl.BlockSpec((TILE, width), lambda i, *_: (jnp.maximum(i - last, 0), 0))
    return [full, full, full, upper, lower]


def ring_values(refs):
    own, following, previous, upper, lower = refs
    top = pl.program_id(0) < pl.num_programs(0) // 2
    return own[...], following[...], jnp.where(top, upper[...], lower[...]), previous[...]


def grad_context_kernel(at_ref, *refs):
    del at_ref
    total = None
    for g, w in zip(ring_values(refs[:5]), refs[5:9]):
        term = dot(g, w[...], NT)
        total = term if total is None else total + term
    refs[9][...] = total.astype(jnp.bfloat16)


def grad_context_of(at, pieces, weight):
    rows, width = pieces[0].shape
    heads = weight.shape[0]
    turned = [
        pl.BlockSpec((heads, width), functools.partial(lambda j, i, at: (0, (at[0] + j) % 4), j))
        for j in range(4)
    ]
    return pl.pallas_call(
        grad_context_kernel,
        grid_spec=pltpu.PrefetchScalarGridSpec(
            num_scalar_prefetch=1,
            grid=(rows // TILE,),
            in_specs=ring_specs(rows, width) + turned,
            out_specs=pl.BlockSpec((TILE, heads), lambda i, at: (i, 0)),
        ),
        out_shape=jax.ShapeDtypeStruct((rows, heads), jnp.bfloat16),
        compiler_params=params(12),
        cost_estimate=pl.CostEstimate(flops=2 * rows * 1024 * heads, bytes_accessed=16 << 20, transcendentals=0),
    )(at, *pieces, weight, weight, weight, weight)


def attend_kernel(
    blocks, last_block, handed_on, me_ref, slot_ref, to_ref, valid_ref, q_ref, k_ref, v_ref, g_ref, before_ref,
    after_ref, glob_ref, fetched_ref, *more,
):
    ctx_ref, dq_ref, win_out_ref, up_ref, down_ref, gsum_out_ref, *more = more[handed_on:]
    parts_out, (kpad, vpad, win_ref, gsum_ref) = more[:-4], more[-4:]
    if len(parts_out) == 1:
        ret_ref = parts_out[0]
    else:
        *parts_out, ret_ref = parts_out
    rows = blocks * BLK
    kpad[0:BLK, :] = before_ref[0:BLK, :]
    vpad[0:BLK, :] = before_ref[BLK : 2 * BLK, :]
    kpad[rows + BLK : rows + 2 * BLK, :] = after_ref[0:BLK, :]
    vpad[rows + BLK : rows + 2 * BLK, :] = after_ref[BLK : 2 * BLK, :]
    kpad[BLK : rows + BLK, :] = k_ref[...]
    vpad[BLK : rows + BLK, :] = v_ref[...]
    win_ref[...] = jnp.zeros_like(win_ref)
    gsum_ref[...] = jnp.zeros_like(gsum_ref)
    low = lax.broadcasted_iota(jnp.int32, (BLK, LANES), 1) < HD

    def body(i, _):
        row = pl.multiple_of(i * BLK, BLK)
        q = q_ref[pl.ds(row, BLK), :] * jnp.bfloat16(0.125)
        g = g_ref[pl.ds(row, BLK), :]
        zero = jnp.zeros_like(q)
        qbd = jnp.concatenate([jnp.where(low, q, zero), jnp.where(low, zero, q)], axis=0)
        gbd = jnp.concatenate([jnp.where(low, g, zero), jnp.where(low, zero, g)], axis=0)
        starts = [pl.multiple_of(slot_ref[i * R + r] * 2 * BLK, 2 * BLK) for r in range(R)]
        kcat = jnp.concatenate(
            [kpad[pl.ds(row, 3 * BLK), :]]
            + [fetched_ref[pl.ds(s, BLK), :] for s in starts]
            + [glob_ref[0, 0], glob_ref[1, 0]],
            axis=0,
        )
        vcat = jnp.concatenate(
            [vpad[pl.ds(row, 3 * BLK), :]]
            + [fetched_ref[pl.ds(s + BLK, BLK), :] for s in starts]
            + [glob_ref[0, 1], glob_ref[1, 1]],
            axis=0,
        )
        scores = dot(kcat, qbd, NT)
        block = me_ref[0] * blocks + i
        present = [block > 0, None, block < last_block]
        present += [valid_ref[i * R + r] == 1 for r in range(R)] + [None] * G
        parts = []
        for e, there in enumerate(present):
            part = scores[e * BLK : (e + 1) * BLK]
            parts.append(part if there is None else part + jnp.where(there, 0.0, NEG_FILL))
        scores = jnp.concatenate(parts, axis=0)
        peak = jnp.max(scores, axis=0, keepdims=True)
        terms = jnp.exp(scores - peak)
        probs = terms * (1.0 / jnp.sum(terms, axis=0, keepdims=True))
        probs_low = probs.astype(jnp.bfloat16)
        grad_probs = dot(vcat, gbd, NT)
        delta = jnp.sum(probs * grad_probs, axis=0, keepdims=True)
        grad_scores = (probs * (grad_probs - delta)).astype(jnp.bfloat16)
        context = dot(probs_low, vcat, TN)
        grad_q = dot(grad_scores, kcat, TN)
        grad_k = dot(grad_scores, qbd, NN)
        grad_v = dot(probs_low, gbd, NN)
        ctx_ref[pl.ds(row, BLK), :] = jnp.where(low, context[:BLK], context[BLK:]).astype(jnp.bfloat16)
        dq_ref[pl.ds(row, BLK), :] = (
            jnp.where(low, grad_q[:BLK], grad_q[BLK:]) * 0.125
        ).astype(jnp.bfloat16)
        win_ref[0, pl.ds(row, 3 * BLK), :] += grad_k[: 3 * BLK]
        win_ref[1, pl.ds(row, 3 * BLK), :] += grad_v[: 3 * BLK]
        for r in range(R):
            part = slice((3 + r) * BLK, (4 + r) * BLK)
            to = pl.multiple_of(to_ref[i * R + r] * 2 * BLK, 2 * BLK)
            ret_ref[pl.ds(to, BLK), :] = grad_k[part].astype(jnp.bfloat16)
            ret_ref[pl.ds(to + BLK, BLK), :] = grad_v[part].astype(jnp.bfloat16)
        for e in range(G):
            part = slice((3 + R + e) * BLK, (4 + R + e) * BLK)
            gsum_ref[e, 0] += grad_k[part]
            gsum_ref[e, 1] += grad_v[part]
        return 0

    lax.fori_loop(0, blocks, body, 0, unroll=2)
    win_out_ref[...] = win_ref[:, BLK : rows + BLK, :]
    up_ref[...] = win_ref[:, 0:BLK, :].astype(jnp.bfloat16)
    down_ref[...] = win_ref[:, rows + BLK : rows + 2 * BLK, :].astype(jnp.bfloat16)
    gsum_out_ref[...] = gsum_ref[...].reshape(G * 2 * BLK, LANES).astype(jnp.bfloat16)
    if len(parts_out) > 1:
        devices, _, lanes = parts_out[0].shape
        count = ret_ref.shape[0] // 2 // devices
        for p, part_ref in enumerate(parts_out):
            for d in range(devices):
                start = (p * devices + d) * count
                part_ref[d, CARRIED : CARRIED + count, :] = ret_ref[start : start + count, :]


def attend(last_block, me, slot, to, valid, q, k, v, g, before, after, glob, fetched, handed, column):
    rows, width = q.shape
    blocks = rows // BLK
    half = whole((rows, LANES), column)
    shapes = [
        ((rows, width), jnp.bfloat16),
        ((rows, width), jnp.bfloat16),
        ((2, rows, LANES), jnp.float32),
        ((2, BLK, width), jnp.bfloat16),
        ((2, BLK, width), jnp.bfloat16),
        ((G * 2 * BLK, LANES), jnp.bfloat16),
    ]
    scratch = [
        pltpu.VMEM((rows + 2 * BLK, LANES), jnp.bfloat16),
        pltpu.VMEM((rows + 2 * BLK, LANES), jnp.bfloat16),
        pltpu.VMEM((2, rows + 2 * BLK, LANES), jnp.float32),
        pltpu.VMEM((G, 2, BLK, LANES), jnp.float32),
    ]
    if not handed:
        shapes.append((fetched.shape, jnp.bfloat16))
    else:
        shapes += [((16, fetched.shape[0] // 32 + CARRIED, LANES), jnp.bfloat16)] * 2
        scratch.insert(0, pltpu.VMEM(fetched.shape, jnp.bfloat16))
    specs = [whole(shape) for shape, _ in shapes]
    specs[0] = specs[1] = half
    specs[3] = specs[4] = whole((2, BLK, LANES), column)
    return pl.pallas_call(
        functools.partial(attend_kernel, blocks, last_block, len(handed)),
        grid=(1,),
        in_specs=[
            smem(), smem(), smem(), smem(), half, half, half, half,
            pl.BlockSpec((2 * BLK, LANES), lambda i: (G, column)),
            pl.BlockSpec((2 * BLK, LANES), lambda i: (G, column)),
            whole((G, 2, BLK, LANES), column),
            whole(fetched.shape),
        ]
        + [pl.BlockSpec(memory_space=pl.ANY)] * len(handed),
        out_specs=tuple(specs),
        out_shape=tuple(jax.ShapeDtypeStruct(*shape) for shape in shapes),
        scratch_shapes=scratch,
        input_output_aliases={12: 0, 13: 1, 14: 3, 15: 4} if handed else {},
        compiler_params=params(44),
        cost_estimate=pl.CostEstimate(
            flops=12 * blocks * 512 * 128 * 128 * 2, bytes_accessed=80 << 20, transcendentals=blocks * 512 * 128
        ),
    )(me, slot, to, valid, q, k, v, g, before, after, glob, fetched, *handed)


def land(entries, idx_ref, used_ref, back_ref, acc):
    first, end, capacity, skipped = entries

    def body(a, _):
        @pl.when(used_ref[a] > 0)
        def _():
            for c in range(first, end):
                at = pl.multiple_of(idx_ref[a * capacity + c] * BLK, BLK)
                src = skipped + (c - first) * 2 * BLK
                acc[0, pl.ds(at, BLK), :] += back_ref[a, src : src + BLK, :].astype(jnp.float32)
                acc[1, pl.ds(at, BLK), :] += back_ref[a, src + BLK : src + 2 * BLK, :].astype(jnp.float32)

        return 0

    lax.fori_loop(0, back_ref.shape[0], body, 0)


def edges(up_ref, down_ref, acc):
    rows = acc.shape[1]
    acc[:, rows - BLK : rows, :] += up_ref[...].astype(jnp.float32)
    acc[:, 0:BLK, :] += down_ref[...].astype(jnp.float32)


def first_kernel(
    capacity, idx_ref, used_ref, glob_ref, win_ref, back_ref, up_ref, down_ref, dk_ref, dv_ref, kept_ref, acc
):
    acc[...] = win_ref[...]
    edges(up_ref, down_ref, acc)
    land((0, capacity, capacity, 0), idx_ref, used_ref, back_ref, acc)
    dk_ref[...] = acc[0].astype(jnp.bfloat16)
    dv_ref[...] = acc[1].astype(jnp.bfloat16)
    blocks = acc.shape[1] // BLK
    for e in range(G):
        at = pl.multiple_of(glob_ref[e] % blocks * BLK, BLK)
        kept_ref[e] = acc[:, pl.ds(at, BLK), :]


def middle_kernel(capacity, idx_ref, used_ref, win_ref, back_ref, up_ref, down_ref, acc):
    acc[...] = win_ref[...]
    edges(up_ref, down_ref, acc)
    land((0, capacity // 2, capacity, CARRIED), idx_ref, used_ref, back_ref, acc)


def last_kernel(
    capacity, idx_ref, used_ref, glob_ref, me_ref, win_ref, back_ref, kept_ref, dk_in_ref, dv_in_ref,
    dk_ref, dv_ref, acc,
):
    acc[...] = win_ref[...]
    land((capacity // 2, capacity, capacity, CARRIED), idx_ref, used_ref, back_ref, acc)
    blocks = acc.shape[1] // BLK
    sums = CARRIED - 32

    def total(half, e):
        found = [
            jnp.concatenate(
                [
                    back_ref[(e * 2 + t) * 4 + d, sums + half * 16 : sums + (half + 1) * 16, :].astype(jnp.float32)
                    for d in range(4)
                ]
            )
            for t in range(2)
        ]
        return jnp.stack(found)

    for e in range(G):

        @pl.when(glob_ref[e] // blocks == me_ref[0])
        def _():
            at = pl.multiple_of(glob_ref[e] % blocks * BLK, BLK)
            acc[:, pl.ds(at, BLK), :] += total(1, e)

    dk_ref[:, LANES:] = acc[0].astype(jnp.bfloat16)
    dv_ref[:, LANES:] = acc[1].astype(jnp.bfloat16)
    dk_ref[:, :LANES] = dk_in_ref[...]
    dv_ref[:, :LANES] = dv_in_ref[...]
    for e in range(G):

        @pl.when(glob_ref[e] // blocks == me_ref[0])
        def _():
            at = pl.multiple_of(glob_ref[e] % blocks * BLK, BLK)
            both = (kept_ref[e] + total(0, e)).astype(jnp.bfloat16)
            dk_ref[pl.ds(at, BLK), :LANES] = both[0]
            dv_ref[pl.ds(at, BLK), :LANES] = both[1]


def collect_first(idx, used, glob, win, back, up, down, capacity):
    rows = win.shape[1]
    out = jax.ShapeDtypeStruct((rows, LANES), jnp.bfloat16)
    kept = jax.ShapeDtypeStruct((G, 2, BLK, LANES), jnp.float32)
    return pl.pallas_call(
        functools.partial(first_kernel, capacity),
        grid=(1,),
        in_specs=[smem()] * 3 + [whole(x.shape) for x in (win, back)] + [whole((2, BLK, LANES), 0)] * 2,
        out_specs=(whole(out.shape), whole(out.shape), whole(kept.shape)),
        out_shape=(out, out, kept),
        scratch_shapes=[pltpu.VMEM((2, rows, LANES), jnp.float32)],
        compiler_params=params(28),
        cost_estimate=pl.CostEstimate(flops=4 << 20, bytes_accessed=16 << 20, transcendentals=0),
    )(idx, used, glob, win, back, up, down)


def collect_middle(idx, used, win, back, up, down, capacity):
    return pl.pallas_call(
        functools.partial(middle_kernel, capacity),
        grid=(1,),
        in_specs=[smem()] * 2 + [whole(x.shape) for x in (win, back)] + [whole((2, BLK, LANES), 1)] * 2,
        out_specs=whole(win.shape),
        out_shape=jax.ShapeDtypeStruct(win.shape, jnp.float32),
        compiler_params=params(24),
        cost_estimate=pl.CostEstimate(flops=4 << 20, bytes_accessed=14 << 20, transcendentals=0),
    )(idx, used, win, back, up, down)


def collect_last(idx, used, glob, me, win, back, before, capacity):
    rows = win.shape[1]
    out = jax.ShapeDtypeStruct((rows, 2 * LANES), jnp.bfloat16)
    dk, dv, kept = before
    arrays = (win, back, kept, dk, dv)
    return pl.pallas_call(
        functools.partial(last_kernel, capacity),
        grid=(1,),
        in_specs=[smem()] * 4 + [whole(x.shape) for x in arrays],
        out_specs=(whole(out.shape), whole(out.shape)),
        out_shape=(out, out),
        scratch_shapes=[pltpu.VMEM((2, rows, LANES), jnp.float32)],
        compiler_params=params(28),
        cost_estimate=pl.CostEstimate(flops=4 << 20, bytes_accessed=12 << 20, transcendentals=0),
    )(idx, used, glob, me, *arrays)


def weight_kernel(at_ref, c_ref, *refs):
    pieces, (keep_ref, give_ref, acc) = refs[:5], refs[5:]

    @pl.when(pl.program_id(0) == 0)
    def _():
        acc[...] = jnp.zeros_like(acc)

    width = pieces[0].shape[1]
    values = ring_values(pieces)
    for i, g in enumerate(values):
        acc[:, :, i * width : (i + 1) * width] += dot(c_ref[...], g, TN).reshape(2, LANES, width)

    @pl.when(pl.program_id(0) == pl.num_programs(0) - 1)
    def _():
        for i in range(4):
            to = pl.multiple_of(((at_ref[0] + i) % 4) * width, width)
            part = acc.at[:, :, i * width : (i + 1) * width]
            keep_ref[:, pl.ds(to, width)] = part[at_ref[1]].astype(jnp.bfloat16)
            give_ref[:, pl.ds(to, width)] = part[1 - at_ref[1]].astype(jnp.bfloat16)


def weight_terms(at, context, pieces):
    rows, width = pieces[0].shape
    shape = (LANES, 4 * width)
    return pl.pallas_call(
        weight_kernel,
        grid_spec=pltpu.PrefetchScalarGridSpec(
            num_scalar_prefetch=1,
            grid=(rows // TILE,),
            in_specs=[pl.BlockSpec((TILE, width), lambda i, at: (i, 0))] + ring_specs(rows, width),
            out_specs=(pl.BlockSpec(shape, lambda i, at: (0, 0)),) * 2,
            scratch_shapes=[pltpu.VMEM((2, *shape), jnp.float32)],
        ),
        out_shape=(jax.ShapeDtypeStruct(shape, jnp.bfloat16),) * 2,
        compiler_params=params(12),
        cost_estimate=pl.CostEstimate(flops=2 * rows * 1024 * 256, bytes_accessed=16 << 20, transcendentals=0),
    )(at, context, *pieces)


def carried(array):
    return whole((array.shape[0], CARRIED, LANES))


def load_kernel(own_ref, other_ref, s0, s1, part_ref, out_ref):
    del part_ref
    terms = (own_ref[...].astype(jnp.float32) + other_ref[...].astype(jnp.float32)).astype(jnp.bfloat16)
    for d in range(out_ref.shape[0]):
        rows = slice(16 * d, 16 * (d + 1))
        for j in range(4):
            column = (d % 2 * 4 + j) * LANES
            out_ref[d, 16 * j : 16 * (j + 1), :] = terms[d // 2 * 16 : d // 2 * 16 + 16, column : column + LANES]
        out_ref[d, CARRIED - 32 : CARRIED - 16, :] = s0[rows, :]
        out_ref[d, CARRIED - 16 :, :] = s1[rows, :]


def load_terms(own, other, sums, part):
    return pl.pallas_call(
        load_kernel,
        grid=(1,),
        in_specs=[whole(x.shape) for x in (own, other, *sums)] + [pl.BlockSpec(memory_space=pl.ANY)],
        out_specs=carried(part),
        out_shape=jax.ShapeDtypeStruct(part.shape, part.dtype),
        input_output_aliases={4: 0},
        compiler_params=params(8),
        cost_estimate=pl.CostEstimate(flops=1 << 18, bytes_accessed=4 << 20, transcendentals=0),
    )(own, other, *sums, part)


def load_sums(back, part):
    total = jnp.sum(back[:, :CARRIED].astype(jnp.float32), axis=0).astype(jnp.bfloat16)
    spread = jnp.broadcast_to(total[None], (part.shape[0], CARRIED, LANES))
    return lax.dynamic_update_slice_in_dim(part, spread, 0, 1)


def weight_kernel_last(at_ref, own_ref, other_ref, out_ref):
    for half_ref, half in ((own_ref, at_ref[1]), (other_ref, 1 - at_ref[1])):
        for d in range(half_ref.shape[0]):
            row = pl.multiple_of(half * LANES + d // 2 * 16, 16)
            for j in range(4):
                column = (d % 2 * 4 + j) * LANES
                tile = half_ref[d, 16 * j : 16 * (j + 1), :].astype(jnp.float32)
                out_ref[pl.ds(row, 16), column : column + LANES] = tile


def weight_last(at, own, other):
    shape = (2 * LANES, 1024)
    return pl.pallas_call(
        weight_kernel_last,
        grid=(1,),
        in_specs=[smem(), whole(own.shape), whole(other.shape)],
        out_specs=whole(shape),
        out_shape=jax.ShapeDtypeStruct(shape, jnp.float32),
        compiler_params=params(8),
        cost_estimate=pl.CostEstimate(flops=1 << 18, bytes_accessed=2 << 20, transcendentals=0),
    )(at, own, other)


def project_kernel(*refs):
    total = None
    for c, w in zip(ring_values(refs[:5]), refs[5:9]):
        term = dot(c, w[...], NN)
        total = term if total is None else total + term
    refs[9][...] = total.astype(jnp.bfloat16)


def project(pieces, weights):
    rows, width = pieces[0].shape
    return pl.pallas_call(
        project_kernel,
        grid=(rows // TILE,),
        in_specs=ring_specs(rows, width) + [pl.BlockSpec(w.shape, lambda i: (0, 0)) for w in weights],
        out_specs=pl.BlockSpec((TILE, width), lambda i: (i, 0)),
        out_shape=jax.ShapeDtypeStruct((rows, width), jnp.bfloat16),
        compiler_params=params(12),
        cost_estimate=pl.CostEstimate(flops=2 * rows * 1024 * width, bytes_accessed=18 << 20, transcendentals=0),
    )(*pieces, *weights)


def shifted(array, axis, by):
    size = lax.axis_size(axis)
    return lax.ppermute(array, axis, [((i + by) % size, i) for i in range(size)])


def ring_near(array, axis):
    return shifted(array, axis, 1), shifted(array, axis, -1)


def ring_far(near, axis):
    following, previous = near
    half = following.shape[0] // 2
    return shifted(following[:half], axis, 1), shifted(previous[half:], axis, -1)


def passed_along(array, axis, by):
    size = lax.axis_size(axis)
    pairs = [(i, i + by) for i in range(size) if 0 <= i + by < size]
    return lax.ppermute(array, axis, pairs)


def per_device(
    queries, key_vectors, value_vectors, grad_output, out_weight, random_ids, random_valid, global_ids
):
    ctx_count = lax.axis_size("ctx")
    tp_count = lax.axis_size("tp")
    me = lax.axis_index("ctx")
    tp_me = lax.axis_index("tp")
    q, k, v, g_out = queries[0], key_vectors[0], value_vectors[0], grad_output[0]
    rows, width = q.shape
    blocks = rows // BLK
    requests = blocks * R
    capacity = requests // (ctx_count * 3 // 4)
    slots = ctx_count * capacity
    barrier = lax.optimization_barrier
    at = me.reshape(1)
    tp_at = jnp.stack([tp_me, lax.axis_index("dp")])
    glob_at = global_ids[0]

    def exchange(parts):
        return lax.all_to_all(parts, "ctx", split_axis=0, concat_axis=0, tiled=True)

    up, down, picked = pick_global(glob_at, at, k, v)
    before, after = shifted(up, "ctx", -1), shifted(down, "ctx", 1)
    across = shifted(picked, "ctx", 2)

    ids = random_ids[0].reshape(ctx_count, requests)
    owner = ids // blocks
    local = ids % blocks
    order = jnp.arange(requests, dtype=jnp.int32)
    earlier = order[None, :] < order[:, None]
    mine = owner == me
    rank = jnp.sum((mine[:, None, :] & earlier[None]).astype(jnp.int32), axis=2)
    hit = mine[:, None, :] & (rank[:, None, :] == jnp.arange(capacity, dtype=jnp.int32)[None, :, None])
    send_idx = jnp.sum(jnp.where(hit, local[:, None, :], 0), axis=2).reshape(slots)
    send_a = pick_blocks(send_idx, k, v, 0, slots)

    send_a, picked, across, before, after, g_now = barrier((send_a, picked, across, before, after, g_out))
    fetched_a = exchange(send_a.reshape(ctx_count, -1, LANES)).reshape(send_a.shape)
    near = ring_near(g_now, "tp")
    glob = sum_four((picked, before, after, across))
    globs = [glob] + [shifted(glob, "ctx", 4 * by) for by in (1, 3, 2)]
    send_b = pick_blocks(send_idx, k, v, 1, slots)
    used = jnp.sum(mine.astype(jnp.int32), axis=1)
    my_owner = lax.dynamic_index_in_dim(owner, me, 0, keepdims=False)
    my_rank = jnp.sum(((my_owner[:, None] == my_owner[None, :]) & earlier).astype(jnp.int32), axis=1)
    my_slot = my_owner * capacity + my_rank
    part_size = capacity // 2
    my_part = my_rank // part_size
    my_place = (my_part * ctx_count + my_owner) * part_size + my_rank % part_size
    valid = lax.dynamic_slice_in_dim(random_valid[0], me * blocks, blocks, 0).reshape(-1)

    ready = barrier((send_b, fetched_a, near, globs, used, my_slot, my_place, valid))
    send_b, fetched_a, near, globs, used, my_slot, my_place, valid = ready
    glob = sum_four(globs).reshape(G, 2, BLK, width)
    pieces = (g_out, *near, *ring_far(near, "tp"))
    grad_context = grad_context_of(tp_at, pieces, out_weight)

    fetched_b = exchange(send_b.reshape(ctx_count, -1, LANES)).reshape(send_b.shape)
    last_block = blocks * ctx_count - 1

    def half(to, fetched, handed, column):
        return attend(
            last_block, at, my_slot, to, valid, q, k, v, grad_context, before, after, glob, fetched, handed, column
        )

    context, grad_q, win_a, up, down, gsum_a, ret_a = half(my_slot, fetched_a, (), 0)
    ret_a, fetched_b = barrier((ret_a, fetched_b))

    back_a = exchange(ret_a.reshape(ctx_count, -1, LANES))
    context, grad_q, win_b, up, down, gsum_b, ret_b, ret_c = half(my_place, fetched_b, (context, grad_q, up, down), 1)
    keep, give = weight_terms(tp_at, context, pieces)
    ret_b = load_terms(keep, shifted(give, "dp", 1), (gsum_a, gsum_b), ret_b)
    ret_b, back_a = barrier((ret_b, back_a))

    back_b = exchange(ret_b)
    near = ring_near(context, "tp")
    up, down = passed_along(up, "ctx", -1), passed_along(down, "ctx", 1)
    ret_c = load_sums(back_b, ret_c)
    ret_c, up, down, near, w_now = barrier((ret_c, up, down, near, out_weight))

    back_c = exchange(ret_c)
    first = collect_first(send_idx, used, glob_at, win_a, back_a, up, down, capacity)
    win_b = collect_middle(send_idx, used, win_b, back_b, up, down, capacity)
    wcols = [None] * tp_count
    for by in range(tp_count):
        part = lax.dynamic_slice_in_dim(w_now, (tp_me + by) % tp_count * width, width, 1)
        wcols[-by % tp_count] = shifted(part, "tp", -by) if by else part
    projected = project((context, *near, *ring_far(near, "tp")), wcols)
    projected, win_b, first, back_c = barrier((projected, win_b, first, back_c))
    weight_own = back_c[:, : CARRIED - 32]
    grad_weight = weight_last(tp_at, weight_own, shifted(weight_own, "dp", 1))
    grad_k, grad_v = collect_last(send_idx, used, glob_at, at, win_b, back_c, first, capacity)
    return projected[None], grad_q[None], grad_k[None], grad_v[None], grad_weight


def solution(mesh):
    tokens = P("dp", "ctx", "tp")
    in_specs = (
        tokens, tokens, tokens, tokens, P("tp", None), P("dp", None, None), P("dp", None, None), P("dp", None),
    )
    out_specs = (tokens, tokens, tokens, tokens, P("tp", None))
    return jax.shard_map(per_device, mesh=mesh, in_specs=in_specs, out_specs=out_specs, check_vma=False)
```
